32 devices in a mesh: batch: 8 (over y, x, core), seq: 4 (over z).
Axes of the slice: x: 2, y: 2, z: 4, core: 2. Of those that a mesh axis runs over, the one named last changes fastest.
Arguments:
- enc_in: bfloat16 [32, 1024, 768], P('batch', 'seq'), may hold values from -6 to 6
- dec_in: bfloat16 [32, 256, 768], P(('batch', 'seq')), may hold values from -6 to 6
- out_grad: bfloat16 [32, 256, 768], P(('batch', 'seq')), may hold values from -6 to 6
- enc_segs: int32 [32, 1024], P('batch'), may hold values from 0 to 3, as said below
- dec_segs: int32 [32, 256], P(('batch', 'seq')), may hold values from 0 to 3, as said below
- enc_qkv: bfloat16 [768, 2304], replicated, may hold values from -0.109375 to 0.109375
- enc_proj: bfloat16 [768, 768], replicated, may hold values from -1.75 to 1.75
- enc_wi: bfloat16 [768, 3072], replicated, may hold values from -0.21875 to 0.21875
- enc_wo: bfloat16 [3072, 768], replicated, may hold values from -0.15625 to 0.15625
- enc_rel: float32 [32, 12], replicated, may hold values from -4 to 4
- enc_gains: float32 [3, 768], replicated, may hold values from 0.5 to 1.5
- dec_qkv: bfloat16 [768, 2304], replicated, may hold values from -0.109375 to 0.109375
- dec_proj: bfloat16 [768, 768], replicated, may hold values from -1.75 to 1.75
- dec_rel: float32 [32, 12], replicated, may hold values from -4 to 4
- cross_q: bfloat16 [768, 768], replicated, may hold values from -0.109375 to 0.109375
- cross_kv: bfloat16 [768, 1536], replicated, may hold values from -0.109375 to 0.109375
- cross_proj: bfloat16 [768, 768], replicated, may hold values from -1.75 to 1.75
- dec_wi: bfloat16 [768, 3072], replicated, may hold values from -0.21875 to 0.21875
- dec_wo: bfloat16 [3072, 768], replicated, may hold values from -0.15625 to 0.15625
- dec_gains: float32 [3, 768], replicated, may hold values from 0.5 to 1.5
Outputs:
- dec_result: bfloat16 [32, 256, 768], P(('batch', 'seq'))
- enc_in_grad: float32 [32, 1024, 768], P('batch', 'seq')
- dec_in_grad: float32 [32, 256, 768], P(('batch', 'seq'))
- grad_enc_qkv: float32 [768, 2304], P(('batch', 'seq'))
- grad_enc_proj: float32 [768, 768], P(('batch', 'seq'))
- grad_enc_wi: float32 [768, 3072], P(('batch', 'seq'))
- grad_enc_wo: float32 [3072, 768], P(('batch', 'seq'))
- grad_enc_rel: float32 [32, 12], replicated
- grad_enc_gains: float32 [3, 768], replicated
- grad_dec_qkv: float32 [768, 2304], P(('batch', 'seq'))
- grad_dec_proj: float32 [768, 768], P(('batch', 'seq'))
- grad_dec_rel: float32 [32, 12], replicated
- grad_cross_q: float32 [768, 768], P(('batch', 'seq'))
- grad_cross_kv: float32 [768, 1536], P(('batch', 'seq'))
- grad_cross_proj: float32 [768, 768], P(('batch', 'seq'))
- grad_dec_wi: float32 [768, 3072], P(('batch', 'seq'))
- grad_dec_wo: float32 [3072, 768], P(('batch', 'seq'))
- grad_dec_gains: float32 [3, 768], replicated
The draws below stay inside these ranges and needn't reach their ends.
Inputs may be any that keep to these rules, and one draw needn't show every extreme that they name: `enc_segs`: along each row the ids never fall, and each of the 4 ids holds one position or more. `dec_segs`: along each row the ids never fall, and each of the 4 ids holds one position or more; row r of dec_segs and of enc_segs hold the same documents.
All inputs are finite; a program needn't handle non-finite values.
Results may differ from the reference program's by a relative error of at most 0.029.
The reference program's roundings to bfloat16 on the way count: a program that leaves them out, or rounds other values in their place, can miss the bound.
Values may be sent and summed in bfloat16 or wider, within the bound.
No kernel may reach another device: no remote copies, remote signals or barrier semaphores. Data moves between devices by JAX's collectives and lax.ppermute only.
A program may use at most 512 MiB of HBM per device.

```python
import math
import jax
import jax.numpy as jnp
from jax import lax

D = 768
FF = 3072
H = 12
DK = 64
NB = 32
MAXD = 128
ENC_LEN = 1024
DEC_LEN = 256
SEGS = 4
ROWS = 32


def segment_ids(key, row_count, length, seg_count):
    scores = jax.random.randint(key, (row_count, length - 1), 0, 1048576)
    unique = scores * length + jnp.arange(length - 1, dtype=jnp.int32)[None, :]
    ranked = jnp.argsort(unique, axis=1, stable=True)
    cut_points = ranked[:, :seg_count - 1] + 1
    positions = jnp.arange(length, dtype=jnp.int32)
    return jnp.sum((positions[None, :, None] >= cut_points[:, None, :]).astype(jnp.int32), axis=2).astype(jnp.int32)


def draw_enc_segs(key, part):
    return segment_ids(jax.random.fold_in(key, 11), ROWS, ENC_LEN, SEGS)


def draw_dec_segs(key, part):
    return segment_ids(jax.random.fold_in(key, 23), ROWS, DEC_LEN, SEGS)


def level_of(rng, shape, cuts, smallest, high):
    gain = 1.0
    for axis_at, parts in cuts:
        draws = jax.random.uniform(jax.random.fold_in(jax.random.fold_in(rng, 6), axis_at), (parts,), jnp.float32, smallest / len(cuts), high / len(cuts))
        gain = gain * jnp.repeat(jnp.exp(draws), shape[axis_at] // parts).reshape((-1,) + (1,) * (len(shape) - 1 - axis_at))
    return gain


def centred(key, dims, spread, bound, shards=(), kind=jnp.bfloat16):
    values = jax.random.normal(key, dims, jnp.float32) * spread
    if len(shards) > 0:
        values = level_of(key, dims, shards, -0.22, 0.18) * values
    return jnp.clip(values, min=-bound, max=bound).astype(kind)


def setup_inputs(seed: int = 0) -> dict:
    key_of = jax.random.split(jax.random.key(seed), 21)
    enc_in = centred(key_of[0], (ROWS, ENC_LEN, D), 1.0, 6.0, ((0, 8), (1, 4)))
    dec_in = centred(key_of[1], (ROWS, DEC_LEN, D), 1.0, 6.0, ((0, 32),))
    out_grad = centred(key_of[2], (ROWS, DEC_LEN, D), 1.0, 6.0, ((0, 32),))
    enc_segs = draw_enc_segs(jax.random.fold_in(key_of[20], 71), 0)
    dec_segs = draw_dec_segs(jax.random.fold_in(key_of[20], 71), 0)
    enc_qkv = centred(key_of[5], (D, 3 * D), (4 * D) ** -0.5, 0.109375)
    enc_proj = centred(key_of[6], (D, D), (D // 64) ** -0.5, 1.75)
    enc_wi = centred(key_of[7], (D, FF), D ** -0.5, 0.21875)
    enc_wo = centred(key_of[8], (FF, D), (FF // 2) ** -0.5, 0.15625)
    enc_rel = centred(key_of[9], (NB, H), 1.0, 4.0, (), jnp.float32)
    enc_gains = jnp.clip(1.0 + 0.1 * jax.random.normal(key_of[10], (3, D), jnp.float32), 0.5, 1.5)
    dec_qkv = centred(key_of[11], (D, 3 * D), (4 * D) ** -0.5, 0.109375)
    dec_proj = centred(key_of[12], (D, D), (D // 64) ** -0.5, 1.75)
    dec_rel = centred(key_of[13], (NB, H), 1.0, 4.0, (), jnp.float32)
    cross_q = centred(key_of[14], (D, D), (4 * D) ** -0.5, 0.109375)
    cross_kv = centred(key_of[15], (D, 2 * D), (4 * D) ** -0.5, 0.109375)
    cross_proj = centred(key_of[16], (D, D), (D // 64) ** -0.5, 1.75)
    dec_wi = centred(key_of[17], (D, FF), D ** -0.5, 0.21875)
    dec_wo = centred(key_of[18], (FF, D), (FF // 2) ** -0.5, 0.15625)
    dec_gains = jnp.clip(1.0 + 0.1 * jax.random.normal(key_of[19], (3, D), jnp.float32), 0.5, 1.5)
    return dict(enc_in=enc_in, dec_in=dec_in, out_grad=out_grad, enc_segs=enc_segs, dec_segs=dec_segs, enc_qkv=enc_qkv, enc_proj=enc_proj, enc_wi=enc_wi, enc_wo=enc_wo, enc_rel=enc_rel, enc_gains=enc_gains, dec_qkv=dec_qkv, dec_proj=dec_proj, dec_rel=dec_rel, cross_q=cross_q, cross_kv=cross_kv, cross_proj=cross_proj, dec_wi=dec_wi, dec_wo=dec_wo, dec_gains=dec_gains)


@jax.custom_vjp
def low(v):
    return lax.optimization_barrier(v.astype(jnp.bfloat16)).astype(jnp.float32)

@jax.custom_vjp
def low_back(v):
    return v

def low_keep(v):
    return (low(v), None)

def low_pass(kept, grad):
    return (grad,)

def back_keep(v):
    return (v, None)

def back_low(kept, grad):
    return (low(grad),)
low.defvjp(low_keep, low_pass)
low_back.defvjp(back_keep, back_low)
EPS = 1e-06
NEG = -1000000000.0

def bucket_steps(classes, distance, length):
    exact_part = classes // 2
    thresholds = []
    previous = 0
    for offset in range(1, length + 1):
        if offset < exact_part:
            bucket_level = offset
        else:
            bucket_level = min(classes - 1, exact_part + int(math.log(offset / exact_part) / math.log(distance / exact_part) * (classes - exact_part)))
        if bucket_level > previous:
            thresholds.append((offset, bucket_level - previous))
            previous = bucket_level
    return thresholds

def bucket_count(distance_grid, thresholds):
    buckets = jnp.zeros(distance_grid.shape, jnp.int32)
    for edge_pos, step_size in thresholds:
        buckets = buckets + step_size * (distance_grid >= edge_pos).astype(jnp.int32)
    return buckets

def enc_buckets(query_pos, key_pos):
    relative = key_pos[None, :] - query_pos[:, None]
    half_count = NB // 2
    return half_count * (relative > 0).astype(jnp.int32) + bucket_count(jnp.abs(relative), bucket_steps(half_count, MAXD, ENC_LEN))

def dec_buckets(positions):
    relative = positions[:, None] - positions[None, :]
    return bucket_count(jnp.maximum(relative, 0), bucket_steps(NB, MAXD, DEC_LEN))

def rms_norm(values, gain_vec):
    return values * lax.rsqrt(lax.optimization_barrier(jnp.mean(values * values, axis=-1, keepdims=True)) + EPS) * gain_vec

def matmul(left, right):
    return jnp.matmul(left, right, precision=lax.Precision.HIGHEST)

def gelu_part(values):
    return jax.nn.gelu(values, approximate=True)

def attention(query_rows, key_rows, value_rows, pos_bias, allowed):
    query_heads = query_rows.reshape(query_rows.shape[0], H, DK)
    key_heads = key_rows.reshape(key_rows.shape[0], H, DK)
    value_heads = value_rows.reshape(value_rows.shape[0], H, DK)
    scores = jnp.einsum('qhd,khd->hqk', query_heads, key_heads, precision=lax.Precision.HIGHEST)
    if pos_bias is not None:
        scores = scores + pos_bias
    scores = low_back(scores)
    scores = jnp.where(allowed[None], scores, NEG)
    softmaxed = low(jax.nn.softmax(scores, axis=-1))
    mixed_heads = jnp.einsum('hqk,khd->qhd', softmaxed, value_heads, precision=lax.Precision.HIGHEST)
    return low_back(low(mixed_heads.reshape(query_rows.shape[0], H * DK)))

def row_forward(weights, enc_row, dec_row, enc_ids, dec_ids):
    enc_qkv, enc_proj, enc_wi, enc_wo, enc_rel, enc_gains, dec_qkv, dec_proj, dec_rel, cross_q, cross_kv, cross_proj, dec_wi, dec_wo, dec_gains = weights
    positions = jnp.arange(ENC_LEN, dtype=jnp.int32)
    enc_bias = jnp.transpose(enc_rel[enc_buckets(positions, positions)], (2, 0, 1))
    enc_allow = enc_ids[:, None] == enc_ids[None, :]
    normed = low(rms_norm(enc_row, enc_gains[0]))
    packed = low_back(low(matmul(normed, enc_qkv)))
    attended = attention(packed[:, :D], packed[:, D:2 * D], packed[:, 2 * D:], enc_bias, enc_allow)
    after_attn = enc_row + low_back(matmul(attended, enc_proj))
    normed = low(rms_norm(after_attn, enc_gains[1]))
    hidden = low(gelu_part(low_back(matmul(normed, enc_wi))))
    second = after_attn + low_back(matmul(hidden, enc_wo))
    encoded = low(rms_norm(second, enc_gains[2]))
    cross_pack = low_back(low(matmul(encoded, cross_kv)))
    dec_pos = jnp.arange(DEC_LEN, dtype=jnp.int32)
    dec_bias = jnp.transpose(dec_rel[dec_buckets(dec_pos)], (2, 0, 1))
    dec_allow = (dec_ids[:, None] == dec_ids[None, :]) & (dec_pos[None, :] <= dec_pos[:, None])
    normed = low(rms_norm(dec_row, dec_gains[0]))
    packed = low_back(low(matmul(normed, dec_qkv)))
    attended = attention(packed[:, :D], packed[:, D:2 * D], packed[:, 2 * D:], dec_bias, dec_allow)
    after_attn = dec_row + low_back(matmul(attended, dec_proj))
    normed = low(rms_norm(after_attn, dec_gains[1]))
    cross_query = low_back(low(matmul(normed, cross_q)))
    cross_allow = dec_ids[:, None] == enc_ids[None, :]
    attended = attention(cross_query, cross_pack[:, :D], cross_pack[:, D:], None, cross_allow)
    second = after_attn + low_back(matmul(attended, cross_proj))
    normed = low(rms_norm(second, dec_gains[2]))
    hidden = low(gelu_part(low_back(matmul(normed, dec_wi))))
    return second + low_back(matmul(hidden, dec_wo))

def reference(enc_in, dec_in, out_grad, enc_segs, dec_segs, enc_qkv, enc_proj, enc_wi, enc_wo, enc_rel, enc_gains, dec_qkv, dec_proj, dec_rel, cross_q, cross_kv, cross_proj, dec_wi, dec_wo, dec_gains):
    weights = tuple((weight_arr.astype(jnp.float32) for weight_arr in (enc_qkv, enc_proj, enc_wi, enc_wo, enc_rel, enc_gains, dec_qkv, dec_proj, dec_rel, cross_q, cross_kv, cross_proj, dec_wi, dec_wo, dec_gains)))
    checked = jax.checkpoint(row_forward)

    def all_rows(weight_set, enc_all, dec_all):

        def per_row(row_parts):
            return checked(weight_set, row_parts[0], row_parts[1], row_parts[2], row_parts[3])
        return lax.map(per_row, (enc_all, dec_all, enc_segs, dec_segs))
    result, pullback = jax.vjp(all_rows, weights, enc_in.astype(jnp.float32), dec_in.astype(jnp.float32))
    weight_grads, enc_grad, dec_grad = pullback(out_grad.astype(jnp.float32))
    return (result.astype(jnp.bfloat16), enc_grad, dec_grad, weight_grads[0], weight_grads[1], weight_grads[2], weight_grads[3], weight_grads[4], weight_grads[5], weight_grads[6], weight_grads[7], weight_grads[8], weight_grads[9], weight_grads[10], weight_grads[11], weight_grads[12], weight_grads[13], weight_grads[14])
```

```python
import functools
import math

import jax
import jax.numpy as jnp
import numpy as np
from jax import lax
from jax.experimental import pallas as pl
from jax.experimental.pallas import tpu as pltpu
from jax.sharding import PartitionSpec as P

H = 12
DK = 64
NB = 32
MAXD = 128
ENC_LEN = 1024
DEC_LEN = 256
LANES = 128
BQ = 256
BIG = 1e9
VLIM = 56 * 1024 * 1024
EPS = 1e-06

def bucket_steps(classes, distance, length):
    exact_part = classes // 2
    thresholds = []
    previous = 0
    for offset in range(1, length + 1):
        if offset < exact_part:
            bucket_level = offset
        else:
            bucket_level = min(
                classes - 1,
                exact_part
                + int(
                    math.log(offset / exact_part)
                    / math.log(distance / exact_part)
                    * (classes - exact_part)
                ),
            )
        if bucket_level > previous:
            thresholds.append((offset, bucket_level - previous))
            previous = bucket_level
    return thresholds


def step_buckets(distance, steps):
    buckets = np.zeros(distance.shape, np.int32)
    for edge, size in steps:
        buckets = buckets + size * (distance >= edge)
    return buckets


def line_offsets(queries, keys):
    place = np.arange(queries + keys)
    block = min(BQ, queries)
    wrapped = np.where(place >= queries + keys - block, place - queries - keys, place)
    return wrapped - (queries - block)


def enc_selector(length):
    offsets = line_offsets(length, length)
    half = NB // 2
    buckets = half * (offsets > 0) + step_buckets(np.abs(offsets), bucket_steps(half, MAXD, ENC_LEN))
    return jnp.asarray(buckets, jnp.int32)[:, None] == jnp.arange(NB, dtype=jnp.int32)[None, :]


def dec_selector(length):
    offsets = line_offsets(length, length)
    buckets = step_buckets(np.maximum(-offsets, 0), bucket_steps(NB, MAXD, DEC_LEN))
    return jnp.asarray(buckets, jnp.int32)[:, None] == jnp.arange(NB, dtype=jnp.int32)[None, :]


def bias_line(rel_table, selector):
    line = jnp.einsum(
        "nb,bh->hn", selector.astype(jnp.float32), rel_table, precision=lax.Precision.HIGHEST
    )
    return line.reshape(H // 2, 2, -1)


def rel_grad(line_grad, selector):
    return jnp.einsum(
        "hn,nb->bh",
        line_grad.reshape(H, -1),
        selector.astype(jnp.float32),
        precision=lax.Precision.HIGHEST,
    )


def gelu_pair(values):
    scale = math.sqrt(2.0 / math.pi)
    square = values * values
    curve = jnp.tanh(values * (scale + scale * 0.044715 * square))
    half = 0.5 * (1.0 + curve)
    inner = scale + 3.0 * scale * 0.044715 * square
    slope = half + 0.5 * values * (1.0 - curve * curve) * inner
    return (values * half).astype(jnp.bfloat16), slope.astype(jnp.bfloat16)


def row_dot(inputs, weight):
    return jnp.einsum("...i,ij->...j", inputs, weight, preferred_element_type=jnp.float32)


def back_dot(grad_vals, weight):
    return jnp.einsum("...j,ij->...i", grad_vals, weight, preferred_element_type=jnp.float32)


def weight_grad(inputs, grad_vals):
    return jnp.einsum(
        "ti,tj->ij",
        inputs.reshape(-1, inputs.shape[-1]),
        grad_vals.reshape(-1, grad_vals.shape[-1]),
        preferred_element_type=jnp.float32,
    )


def norm_fwd(values, gain_vec):
    inverse = lax.rsqrt(jnp.mean(values * values, axis=-1, keepdims=True) + EPS)
    return (values * inverse * gain_vec, inverse)


def norm_back(values, inverse, gain_vec, grad_vals):
    scaled = grad_vals * gain_vec
    grad_values = inverse * scaled - values * inverse**3 * jnp.mean(
        scaled * values, axis=-1, keepdims=True
    )
    grad_gain = jnp.sum((grad_vals * values * inverse).reshape(-1, values.shape[-1]), axis=0)
    return (grad_values, grad_gain)


NN=(((1,),(0,)),((),()))
NT=(((1,),(1,)),((),()))
TN=(((0,),(0,)),((),()))
def dot(a,b,dims=NN):
    return lax.dot_general(a,b,dims,preferred_element_type=jnp.float32)

def head_mask(rows):
    lane=lax.broadcasted_iota(jnp.int32,(rows,LANES),1)
    return lane<DK

def keep(x,first,head):
    zero=jnp.zeros_like(x)
    return jnp.where(first,x,zero) if head==0 else jnp.where(first,zero,x)

def skew_line(line_row,rows):
    width=line_row.shape[-1]
    wide=jnp.broadcast_to(line_row,(rows,width))
    return pltpu.roll(wide,0,1,stride=1,stride_axis=0)

def line_sums(turned):
    rows,width=turned.shape
    total=turned[:8]
    for g in range(1,rows//8):
        total=total+pltpu.roll(turned[8*g:8*g+8],width-8*g,1)
    row=lax.broadcasted_iota(jnp.int32,(8,width),0)
    for b in range(3):
        total=jnp.where((row>>b)&1==1,pltpu.roll(total,width-(1<<b),1),total)
    return jnp.sum(total,axis=0,keepdims=True)

def fwd_kernel(bq,has_bias,*refs):
    if has_bias:
        q_ref,k_ref,v_ref,qx_ref,kx_ref,line_ref,o_ref,qb_ref,bias_ref=refs
    else:
        q_ref,k_ref,v_ref,qx_ref,kx_ref,o_ref,qb_ref=refs
    lq=q_ref.shape[0]; lk=k_ref.shape[0]
    wide=lk+lq-bq
    if has_bias:
        for h in range(2):
            bias_ref[h]=skew_line(line_ref[0,h:h+1,:],bq)[:,:wide]
    first=head_mask(bq)
    lane=lax.broadcasted_iota(jnp.int32,(bq,LANES),1)
    keys=jnp.concatenate((k_ref[...],kx_ref[...]),axis=1)
    values=v_ref[...]
    for n in range(lq//bq):
        rows=slice(n*bq,(n+1)*bq)
        q=q_ref[rows,:]; qx=qx_ref[rows,:]
        parts=[]
        for h in range(2):
            s=dot(jnp.concatenate((keep(q,first,h),qx),axis=1),keys,NT)
            if has_bias:
                off=lq-bq-n*bq
                s=s+bias_ref[h,:,off:off+lk]
            top=jnp.max(s,axis=1,keepdims=True)
            e=jnp.exp(s-top)
            total=jnp.sum(e,axis=1,keepdims=True)
            p=(e*(1.0/total)).astype(jnp.bfloat16)
            parts.append(dot(p,values))
            low=-(top+jnp.log(total))
            one=low.astype(jnp.bfloat16).astype(jnp.float32)
            two=(low-one).astype(jnp.bfloat16).astype(jnp.float32)
            three=low-one-two
            x=jnp.where(lane==4,one,jnp.where(lane==5,two,jnp.where(lane==6,three,qx.astype(jnp.float32))))
            qb_ref[h,rows,:]=x.astype(jnp.bfloat16)
        o_ref[rows,:]=jnp.where(first,parts[0],parts[1]).astype(jnp.bfloat16)

def bwd_kernel(bq,has_bias,*refs):
    if has_bias:
        q_ref,k_ref,v_ref,g_ref,qb_ref,kx_ref,line_ref,dq_ref,dk_ref,dv_ref,dl_ref,bias_ref,acc_ref,dka_ref,dva_ref=refs
    else:
        q_ref,k_ref,v_ref,g_ref,qb_ref,kx_ref,dq_ref,dk_ref,dv_ref,dka_ref,dva_ref=refs
    lq=q_ref.shape[0]; lk=k_ref.shape[0]
    wide=lk+lq-bq
    if has_bias:
        for h in range(2):
            bias_ref[h]=skew_line(line_ref[0,h:h+1,:],bq)[:,:wide].T
        acc_ref[...]=jnp.zeros_like(acc_ref)
    first=head_mask(bq)
    keyfirst=head_mask(lk)
    k=k_ref[...]
    keys=jnp.concatenate((k,kx_ref[...]),axis=1)
    values=v_ref[...]
    heads_k=[keep(k,keyfirst,h) for h in range(2)]
    for n in range(lq//bq):
        rows=slice(n*bq,(n+1)*bq)
        q=q_ref[rows,:]; g=g_ref[rows,:]
        dq=None
        for h in range(2):
            qh=keep(q,first,h); gh=keep(g,first,h)
            s=dot(keys,jnp.concatenate((qh,qb_ref[h,rows,:]),axis=1),NT)
            off=lq-bq-n*bq
            if has_bias:
                s=s+bias_ref[h,off:off+lk,:]
            p=jnp.exp(s)
            dp=dot(values,gh,NT)
            inner=jnp.sum(p*dp,axis=0,keepdims=True)
            gs=(p*(dp-inner)).astype(jnp.bfloat16)
            if has_bias:
                acc_ref[h,off:off+lk,:]+=gs.astype(jnp.float32)
            dv=dot(p.astype(jnp.bfloat16),gh)
            dk=dot(gs,qh)
            if n==0 and h==0:
                dva_ref[...]=dv; dka_ref[...]=dk
            else:
                dva_ref[...]+=dv; dka_ref[...]+=dk
            part=dot(gs,heads_k[h],TN)
            dq=part if dq is None else dq+part
        dq_ref[rows,:]=dq.astype(jnp.bfloat16)
    dk_ref[...]=dka_ref[...].astype(jnp.bfloat16)
    dv_ref[...]=dva_ref[...].astype(jnp.bfloat16)
    if has_bias:
        width=line_ref.shape[-1]
        for h in range(2):
            turned=jnp.concatenate((acc_ref[h].T,jnp.zeros((bq,width-wide),jnp.float32)),axis=1)
            dl_ref[0,h:h+1,:]=line_sums(turned)

def cost_of(scores,weight):
    return pl.CostEstimate(flops=1000*weight*scores,bytes_accessed=3*weight*scores,transcendentals=scores)

def attend(q,qc,k,kc,v,vc,qx,kx,line,bq):
    lq=q.shape[0]; lk=k.shape[0]
    bq=min(bq,lq)
    has=line is not None
    blk=lambda rows,c: pl.BlockSpec((rows,LANES),lambda i,c=c:(0,c+i))
    fix=lambda rows: pl.BlockSpec((rows,LANES),lambda i:(0,0))
    ins=[blk(lq,qc),blk(lk,kc),blk(lk,vc),fix(lq),fix(lk)]
    args=[q,k,v,qx,kx]
    scratch=[]
    if has:
        ins.append(pl.BlockSpec((1,2,line.shape[-1]),lambda i:(i,0,0))); args.append(line)
        scratch=[pltpu.VMEM((2,bq,lk+lq-bq),jnp.float32)]
    return pl.pallas_call(functools.partial(fwd_kernel,bq,has),grid=(H//2,),in_specs=ins,
        out_specs=[blk(lq,0),pl.BlockSpec((2,lq,LANES),lambda i:(i,0,0))],
        out_shape=[jax.ShapeDtypeStruct((lq,H*DK),jnp.bfloat16),jax.ShapeDtypeStruct((H,lq,LANES),jnp.bfloat16)],
        scratch_shapes=scratch,compiler_params=pltpu.CompilerParams(vmem_limit_bytes=VLIM),cost_estimate=cost_of(H*lq*lk,3),name="attend")(*args)

def attend_back(q,qc,k,kc,v,vc,g,qb,kx,line,bq,pairs=None):
    lq=q.shape[0]; lk=k.shape[0]
    bq=min(bq,lq)
    has=line is not None
    start,count=(0,H//2) if pairs is None else pairs
    blk=lambda rows,c: pl.BlockSpec((rows,LANES),lambda i,c=c:(0,c+start+i))
    fix=lambda rows: pl.BlockSpec((rows,LANES),lambda i:(0,0))
    ins=[blk(lq,qc),blk(lk,kc),blk(lk,vc),blk(lq,0),pl.BlockSpec((2,lq,LANES),lambda i:(start+i,0,0)),fix(lk)]
    args=[q,k,v,g,qb,kx]
    outs=[pl.BlockSpec((n,LANES),lambda i:(0,i)) for n in (lq,lk,lk)]
    shapes=[jax.ShapeDtypeStruct((n,count*LANES),jnp.bfloat16) for n in (lq,lk,lk)]
    scratch=[]
    if has:
        w=line.shape[-1]
        ins.append(pl.BlockSpec((1,2,w),lambda i:(start+i,0,0))); args.append(line)
        outs.append(pl.BlockSpec((1,2,w),lambda i:(i,0,0)))
        shapes.append(jax.ShapeDtypeStruct((count,2,w),jnp.float32))
        scratch=[pltpu.VMEM((2,lk+lq-bq,bq),jnp.float32)]*2
    scratch=scratch+[pltpu.VMEM((lk,LANES),jnp.float32)]*2
    return pl.pallas_call(functools.partial(bwd_kernel,bq,has),grid=(count,),in_specs=ins,out_specs=outs,out_shape=shapes,
        scratch_shapes=scratch,compiler_params=pltpu.CompilerParams(vmem_limit_bytes=VLIM),cost_estimate=cost_of(2*count*lq*lk,5),name="attend_back")(*args)

def seg_features(q_segs,k_segs):
    ids=jnp.arange(LANES,dtype=jnp.int32)[None,:]
    qx=jnp.where((ids<4)&(q_segs[:,None]!=ids),-BIG,0.0).astype(jnp.bfloat16)
    kx=jnp.where(((ids<4)&(k_segs[:,None]==ids))|((ids>=4)&(ids<7)),1.0,0.0).astype(jnp.bfloat16)
    return qx,kx


def marks(query_segs, key_segs):
    pairs = [seg_features(q, k) for q, k in zip(query_segs, key_segs)]
    return [p[0] for p in pairs], [p[1] for p in pairs]


def row_of(array, row, rows):
    length = array.shape[0] // rows
    return array[row * length : (row + 1) * length]


def join(parts):
    return parts[0] if len(parts) == 1 else jnp.concatenate(parts, axis=0)


def attend_rows(rows, queries, q_col, pairs, k_col, v_col, query_marks, key_marks, line):
    outs, kept = [], []
    for r in range(rows):
        q, kv = row_of(queries, r, rows), row_of(pairs, r, rows)
        out, mark = attend(
            q, q_col, kv, k_col, kv, v_col, query_marks[r], key_marks[r], line, BQ
        )
        outs.append(out)
        kept.append(mark)
    return join(outs), kept


def attend_rows_back(
    rows, queries, q_col, pairs, k_col, v_col, grads, kept, key_marks, line, part=None
):
    results = []
    for r in range(rows):
        q, kv = row_of(queries, r, rows), row_of(pairs, r, rows)
        grad = row_of(grads, r, rows)
        results.append(
            attend_back(
                q, q_col, kv, k_col, kv, v_col, grad, kept[r], key_marks[r], line, BQ, part
            )
        )
    gq, gk, gv = (join([res[i] for res in results]) for i in range(3))
    return gq, gk, gv, None if line is None else sum(res[3] for res in results)


def turn_rows(array):
    return lax.all_to_all(array, "seq", split_axis=0, concat_axis=0, tiled=True)


def bits_of(axis_name):
    return lax.axis_size(axis_name).bit_length() - 1


def swap(array, axis_name, bit):
    pairs = [(i, i ^ (1 << bit)) for i in range(lax.axis_size(axis_name))]
    return lax.ppermute(array, axis_name, pairs)


def halve(array, axis_name, bit, dim):
    mine = (lax.axis_index(axis_name) >> bit) & 1
    kept = lax.dynamic_slice_in_dim(array, mine, 1, dim)
    return kept, lax.dynamic_slice_in_dim(array, 1 - mine, 1, dim)


def add(kept, got):
    return kept.astype(jnp.float32) + got.astype(jnp.float32)


def add_low(kept, got):
    return add(kept, got).astype(jnp.bfloat16)


def grads_kernel(plan, stills, ranks, shares, core_ref, *refs):
    o_count = 1 + max(p[3] for p in plan)
    l_count = 1 + max(p[0] for p in plan)
    a_refs, g_refs = refs[:l_count], refs[l_count : l_count + len(plan)]
    o_refs = refs[l_count + len(plan) : l_count + len(plan) + 2 * o_count]
    t_refs = refs[l_count + len(plan) + 2 * o_count :]
    step = pl.program_id(0)
    core = core_ref[0]
    turned = set()
    for index, (at, first, steps, out, block) in enumerate(plan):
        if at in stills and at not in turned:
            turned.add(at)

            @pl.when(step == first)
            def turn(at=at):
                t_refs[stills.index(at)][...] = a_refs[at][...].T

        for mine in range(2):

            @pl.when((step >= first) & (step < first + steps) & (core == mine))
            def work(index=index, at=at, out=out, block=block, mine=mine):
                left, right = a_refs[at], g_refs[index]
                height, columns = left.shape[1], right.shape[1]
                tiles, group = block // 8, shares * block
                if at in stills:
                    turned_left = t_refs[stills.index(at)][...]
                else:
                    turned_left = left[...].T
                for col in range(0, columns, 256):
                    result = dot(turned_left, right[:, col : col + 256])
                    for place in range(height // group):
                        target = o_refs[2 * out + (0 if place % 2 == mine else 1)]
                        home = place // 2 * shares
                        piece = paired(result[place * group : (place + 1) * group], shares, tiles)
                        spot = col // 256 * tiles
                        target[home : home + shares, spot : spot + tiles] = piece


def whole_kernel(plan, stills, ranks, shares, *refs):
    l_count = 1 + max(p[0] for p in plan)
    a_refs, g_refs = refs[:l_count], refs[l_count : l_count + len(plan)]
    target = refs[l_count + len(plan)]
    t_refs = refs[l_count + len(plan) + 1 :]
    step = pl.program_id(0)
    turned = set()
    for index, (at, first, steps, start, block) in enumerate(plan):
        if at in stills and at not in turned:
            turned.add(at)

            @pl.when(step == first)
            def turn(at=at):
                t_refs[stills.index(at)][...] = a_refs[at][...].T

        @pl.when((step >= first) & (step < first + steps))
        def work(index=index, at=at, start=start, first=first, block=block):
            left, right = a_refs[at], g_refs[index]
            height, columns = left.shape[1], right.shape[1]
            tiles, group = block // 8, shares * block
            if at in stills:
                turned_left = t_refs[stills.index(at)][...]
                home, spot = 0, start + (step - first) * (columns // 256 * tiles)
            else:
                turned_left = left[...].T
                home, spot = (step - first) * (height // block), start
            for col in range(0, columns, 256):
                result = dot(turned_left, right[:, col : col + 256])
                for place in range(height // group):
                    piece = paired(result[place * group : (place + 1) * group], shares, tiles)
                    target[
                        pl.ds(home + place * shares, shares), pl.ds(spot + col // 256 * tiles, tiles)
                    ] = piece


def paired(piece, shares, tiles):
    halves = [
        piece[:, side * LANES : (side + 1) * LANES].reshape(shares, tiles, 8, LANES)
        for side in range(2)
    ]
    return jnp.concatenate(halves, axis=2).astype(jnp.bfloat16)


def tile_columns(shapes):
    columns = {}
    for height, width in shapes:
        columns[height] = math.gcd(columns.get(height, 768), width)
    return columns


def packed_grads(items, split=True):
    ranks = lax.axis_size("batch") * lax.axis_size("seq")
    shares = lax.axis_size("seq")
    shapes_in = [(left.shape[1], right.shape[1]) for left, right in items]
    widths = tile_columns(shapes_in)
    least = min(height for height, width in shapes_in)
    outs, plan, totals, firsts, stills = [], [], [], [], []
    lefts, left_specs, right_specs = [], [], []
    step = 0
    for left, right in items:
        height, width = left.shape[1], right.shape[1]
        if height not in outs:
            outs.append(height)
            totals.append(0)
            firsts.append(step)
        out = outs.index(height)
        tall = height > least
        steps = height // least if tall else width // widths[height]
        at = lambda i, c, first=step, last=steps - 1: (0, jnp.clip(i - first, 0, last))
        still = lambda i, c: (0, 0)
        same = [i for i in stills if lefts[i] is left]
        if same and not tall:
            where = same[0]
        else:
            where = len(lefts)
            lefts.append(left)
            left_specs.append(pl.BlockSpec((left.shape[0], least), at if tall else still))
            if not tall:
                stills.append(where)
        right_specs.append(pl.BlockSpec((right.shape[0], widths[height]), still if tall else at))
        plan.append((where, step, steps, out, height // ranks))
        totals[out] += steps
        step += steps
    shapes, specs = [], []
    for out, height in enumerate(outs):
        size = (height // ranks // 8) * (widths[height] // 256)
        tall = height > least
        count = 1 if tall else totals[out]
        parts = totals[out] if tall else 1
        for side in range(2):
            shapes.append(
                jax.ShapeDtypeStruct((ranks // 2, size * count, 16, LANES), jnp.bfloat16)
            )
            at = lambda i, c, first=firsts[out], last=totals[out] - 1, tall=tall: (
                (jnp.clip(i - first, 0, last), 0, 0, 0)
                if tall
                else (0, jnp.clip(i - first, 0, last), 0, 0)
            )
            specs.append(pl.BlockSpec((ranks // 2 // parts, size, 16, LANES), at))
    flops = sum(2 * x.shape[1] * y.shape[0] * y.shape[1] for x, y in items)
    cost = pl.CostEstimate(flops=flops, bytes_accessed=flops // 400, transcendentals=0)
    turned = [pltpu.VMEM((lefts[i].shape[1], lefts[i].shape[0]), jnp.bfloat16) for i in stills]
    if not split:
        whole_plan, tiles = [], 0
        for out in range(len(outs)):
            for where, first, steps, item_out, block in plan:
                if item_out == out:
                    whole_plan.append((where, first, steps, tiles, block))
                    height, width = shapes_in[len(whole_plan) - 1]
                    tiles += block // 8 * (width // 256)
        drop = lambda at: lambda i: at(i, None)
        return pl.pallas_call(
            functools.partial(whole_kernel, whole_plan, stills, ranks, shares),
            grid=(step,),
            in_specs=[
                pl.BlockSpec(x.block_shape, drop(x.index_map)) for x in left_specs + right_specs
            ],
            out_specs=pl.BlockSpec((ranks, tiles, 16, LANES), lambda i: (0, 0, 0, 0)),
            out_shape=jax.ShapeDtypeStruct((ranks, tiles, 16, LANES), jnp.bfloat16),
            scratch_shapes=turned,
            compiler_params=pltpu.CompilerParams(vmem_limit_bytes=VLIM),
            cost_estimate=cost,
            name="whole_grads",
        )(*lefts, *[right for left, right in items])
    core = (lax.axis_index("batch") & 1).astype(jnp.int32).reshape(1)
    results = pl.pallas_call(
        functools.partial(grads_kernel, plan, stills, ranks, shares),
        grid_spec=pltpu.PrefetchScalarGridSpec(
            num_scalar_prefetch=1,
            grid=(step,),
            in_specs=left_specs + right_specs,
            out_specs=specs,
            scratch_shapes=turned,
        ),
        out_shape=shapes,
        compiler_params=pltpu.CompilerParams(vmem_limit_bytes=VLIM),
        cost_estimate=cost,
        name="packed_grads",
    )(core, *lefts, *[right for left, right in items])
    return results[0::2], results[1::2]


def after(value, *others):
    return lax.optimization_barrier((value,) + others)[0]


class Small:
    def __init__(self, values):
        self.sent, self.got, self.kept = [values], [], values
        self.stages = [("seq", -1)] + [("batch", bit) for bit in range(bits_of("batch"))]

    def launch(self, sent):
        name, bit = self.stages.pop(0)
        if bit >= 0:
            self.got = [swap(sent[0], name, bit)]
            return
        size = lax.axis_size(name)
        self.got = [
            lax.ppermute(sent[0], name, [(i, i ^ step) for i in range(size)])
            for step in range(1, size)
        ]

    def advance(self, got):
        terms = [self.kept] + got
        while len(terms) > 1:
            terms = [terms[i] + terms[i + 1] for i in range(0, len(terms), 2)]
        self.kept = terms[0]
        self.got = []
        self.sent = [self.kept] if self.stages else []

    def finish(self):
        return self.kept


class Flow:
    def __init__(self, items, split=True, seq_first=False):
        self.split, self.seq_first = split, seq_first
        self.shapes = [(left.shape[1], right.shape[1]) for left, right in items]
        self.high, self.low = bits_of("batch"), bits_of("seq")
        self.ranks = 1 << (self.high + self.low)
        self.plain = min(shape[0] for shape in self.shapes) % (8 * self.ranks) != 0
        self.got, self.stage = [], 0
        if self.plain:
            self.sent = []
            self.whole = [weight_grad(left, right) for left, right in items]
            return
        heights = []
        for shape in self.shapes:
            if shape[0] not in heights:
                heights.append(shape[0])
        self.order = [
            [i for i, shape in enumerate(self.shapes) if shape[0] == height] for height in heights
        ]
        if split:
            self.kept, self.sent = packed_grads(items)
        else:
            self.sent = [packed_grads(items, False)]
        ups = [("batch", bit) for bit in range(1, self.high)]
        alongs = [("seq", bit) for bit in range(self.low)]
        if seq_first:
            self.steps = [[step] for step in alongs + ups]
        else:
            self.steps = [list(pair) for pair in zip(ups, ups[::-1])] + [[x] for x in alongs]

    def launch(self, sent):
        if self.plain:
            return
        if not self.split:
            axis_name = ("batch", "seq")[self.stage]
            self.got = [lax.psum_scatter(sent[0], axis_name, scatter_dimension=0, tiled=True)]
        elif self.stage == 0:
            self.got = [swap(x, "batch", 0) for x in sent]
        else:
            steps = self.steps[self.stage - 1]
            self.got = [swap(x, name, bit) for x, (name, bit) in zip(sent, steps)]
        self.stage += 1

    def advance(self, got):
        last = self.high - 1
        dim = last + self.low
        if not self.split:
            self.got, self.sent = [], got if self.stage == 1 else []
            self.result = got[0].astype(jnp.float32)
            return
        if self.stage > len(self.steps):
            self.result = add(self.kept[0], got[0])
            self.got, self.sent = [], []
            return
        sums = [add_low(k, g) for k, g in zip(self.kept, got)]
        if self.stage == 1:
            sums = [x.reshape((2,) * dim + x.shape[1:]) for x in sums]
        steps = self.steps[self.stage - 1]
        if len(sums) > len(steps):
            sums = [jnp.concatenate(sums, axis=dim)]
        elif len(sums) < len(steps):
            size = sums[0].shape[dim]
            sums = [
                lax.slice_in_dim(sums[0], 0, size // 2, axis=dim),
                lax.slice_in_dim(sums[0], size // 2, size, axis=dim),
            ]
        halves = [
            halve(x, name, bit, (last if name == "batch" else dim - 1) - bit)
            for x, (name, bit) in zip(sums, steps)
        ]
        self.kept = [h[0] for h in halves]
        self.sent = [h[1] for h in halves]

    def finish(self):
        if not self.plain and not self.split:
            while self.got:
                self.advance(self.got)
                if self.sent:
                    self.launch(self.sent)
        if self.plain:
            results = []
            for grad in self.whole:
                grad = lax.psum_scatter(
                    grad.astype(jnp.bfloat16), ("batch", "seq"), scatter_dimension=0, tiled=True
                )
                results.append(grad.astype(jnp.float32))
            return results
        while self.got:
            self.advance(self.got)
            if self.sent:
                self.launch(self.sent)
        part = self.result.reshape(-1, 16, LANES)
        results, start = [None] * len(self.shapes), 0
        for indices in self.order:
            for i in indices:
                height, width = self.shapes[i]
                tiles = height // self.ranks // 8
                count = tiles * width // 256
                piece = part[start : start + count]
                start += count
                piece = piece.reshape(width // 256, tiles, 2, 8, LANES)
                piece = jnp.transpose(piece, (1, 3, 0, 2, 4))
                results[i] = piece.reshape(tiles * 8, width)
        return results


def tick(value, *flows, fresh=()):
    live = [flow for flow in flows if flow is not None and flow.got]
    gots = [flow.got for flow in live]
    sents = [list(flow.sent) for flow in fresh]
    value, gots, sents = lax.optimization_barrier((value, gots, sents))
    for flow, sent in zip(fresh, sents):
        flow.launch(sent)
    for flow, got in zip(live, gots):
        flow.advance(got)
    value, sents = lax.optimization_barrier((value, [list(flow.sent) for flow in live]))
    for flow, sent in zip(live, sents):
        if sent:
            flow.launch(sent)
    return value


def body(
    enc_in,
    dec_in,
    out_grad,
    enc_segs,
    dec_segs,
    enc_qkv,
    enc_proj,
    enc_wi,
    enc_wo,
    enc_rel,
    enc_gains,
    dec_qkv,
    dec_proj,
    dec_rel,
    cross_q,
    cross_kv,
    cross_proj,
    dec_wi,
    dec_wo,
    dec_gains,
):
    shares = lax.axis_size("seq")
    rows = enc_in.shape[0] // shares
    full_len = enc_segs.shape[1]
    target_len = dec_in.shape[1]
    width = enc_in.shape[2]
    low = jnp.bfloat16
    row_segs = lax.dynamic_slice_in_dim(enc_segs, lax.axis_index("seq") * rows, rows, 0)

    local_len = enc_in.shape[1]
    enc_row = turn_rows(enc_in.reshape(shares, rows, local_len, width))
    enc_values = jnp.swapaxes(enc_row, 0, 1).reshape(-1, width).astype(jnp.float32)
    dec_values = dec_in.reshape(-1, width).astype(jnp.float32)

    enc_select = enc_selector(full_len)
    dec_select = dec_selector(target_len)
    enc_line = bias_line(enc_rel, enc_select)
    dec_offsets = jnp.asarray(line_offsets(target_len, target_len), jnp.int32)
    dec_line = jnp.where(dec_offsets > 0, -BIG, bias_line(dec_rel, dec_select))
    enc_query_marks, enc_key_marks = marks(row_segs, row_segs)
    dec_query_marks, dec_key_marks = marks(dec_segs, dec_segs)

    dec_normed_one, dec_inverse_one = norm_fwd(dec_values, dec_gains[0])
    dec_normed_one = dec_normed_one.astype(low)
    dec_packed = row_dot(dec_normed_one, dec_qkv).astype(low)
    self_mixed, self_marks = attend_rows(
        rows, dec_packed, 0, dec_packed, 6, 12, dec_query_marks, dec_key_marks, dec_line
    )
    dec_first = dec_values + row_dot(self_mixed, dec_proj)
    dec_normed_two, dec_inverse_two = norm_fwd(dec_first, dec_gains[1])
    dec_normed_two = dec_normed_two.astype(low)
    cross_query = row_dot(dec_normed_two, cross_q).astype(low)

    normed_one, inverse_one = norm_fwd(enc_values, enc_gains[0])
    normed_one = normed_one.astype(low)
    packed = row_dot(normed_one, enc_qkv).astype(low)
    enc_mixed, enc_marks = attend_rows(
        rows, packed, 0, packed, 6, 12, enc_query_marks, enc_key_marks, enc_line
    )
    after_attn = enc_values + row_dot(enc_mixed, enc_proj)
    normed_two, inverse_two = norm_fwd(after_attn, enc_gains[1])
    normed_two = normed_two.astype(low)
    enc_hidden, enc_slope = gelu_pair(row_dot(normed_two, enc_wi))
    second = after_attn + row_dot(enc_hidden, enc_wo)
    encoded, inverse_three = norm_fwd(second, enc_gains[2])
    encoded = encoded.astype(low)
    cross_pack = row_dot(encoded, cross_kv).astype(low)

    cross_mixed, cross_marks = attend_rows(
        rows, cross_query, 0, cross_pack, 0, 6, dec_query_marks, enc_key_marks, None
    )
    dec_second = dec_first + row_dot(cross_mixed, cross_proj)
    dec_normed_three, dec_inverse_three = norm_fwd(dec_second, dec_gains[2])
    dec_normed_three = dec_normed_three.astype(low)
    dec_hidden, dec_slope = gelu_pair(row_dot(dec_normed_three, dec_wi))
    dec_result = (dec_second + row_dot(dec_hidden, dec_wo)).astype(low)

    upstream = out_grad.reshape(-1, width)
    grad_pre = (back_dot(upstream, dec_wo) * dec_slope.astype(jnp.float32)).astype(low)
    flow_one = Flow(((dec_hidden, upstream), (dec_normed_three, grad_pre)), False)
    grad_pre, dec_result = tick((grad_pre, dec_result), fresh=(flow_one,))
    grad_input, gain_dec_three = norm_back(
        dec_second, dec_inverse_three, dec_gains[2], back_dot(grad_pre, dec_wi)
    )
    grad_second = upstream.astype(jnp.float32) + grad_input
    grad_cross_branch = grad_second.astype(low)
    grad_mixed = back_dot(grad_cross_branch, cross_proj).astype(low)
    grad_cq, grad_ck, grad_cv, unused = attend_rows_back(
        rows, cross_query, 0, cross_pack, 0, 6, grad_mixed, cross_marks, enc_key_marks, None
    )
    grad_input, gain_dec_two = norm_back(
        dec_first, dec_inverse_two, dec_gains[1], back_dot(grad_cq, cross_q)
    )
    grad_first = grad_second + grad_input
    grad_self_branch = grad_first.astype(low)
    grad_mixed = back_dot(grad_self_branch, dec_proj).astype(low)
    grad_sq, grad_sk, grad_sv, dec_line_grad = attend_rows_back(
        rows, dec_packed, 0, dec_packed, 6, 12, grad_mixed, self_marks, dec_key_marks, dec_line
    )
    flow_two = Flow(
        (
            (dec_normed_one, grad_sq),
            (dec_normed_one, grad_sk),
            (dec_normed_one, grad_sv),
            (self_mixed, grad_self_branch),
            (dec_normed_two, grad_cq),
            (cross_mixed, grad_cross_branch),
        ),
        False,
    )
    (grad_sq, grad_ck, dec_line_grad, gain_dec_three, gain_dec_two) = tick(
        (grad_sq, grad_ck, dec_line_grad, gain_dec_three, gain_dec_two), fresh=(flow_two,)
    )
    grad_input, gain_dec_one = norm_back(
        dec_values,
        dec_inverse_one,
        dec_gains[0],
        back_dot(grad_sq, dec_qkv[:, :width])
        + back_dot(grad_sk, dec_qkv[:, width : 2 * width])
        + back_dot(grad_sv, dec_qkv[:, 2 * width :]),
    )
    dec_in_grad = grad_first + grad_input
    rel_grad_dec = rel_grad(dec_line_grad, dec_select)

    grad_enc_second, gain_enc_three = norm_back(
        second,
        inverse_three,
        enc_gains[2],
        back_dot(grad_ck, cross_kv[:, :width]) + back_dot(grad_cv, cross_kv[:, width:]),
    )
    grad_branch = grad_enc_second.astype(low)
    grad_branch, dec_in_grad, gain_dec_one, rel_grad_dec, gain_enc_three = tick(
        (grad_branch, dec_in_grad, gain_dec_one, rel_grad_dec, gain_enc_three)
    )
    flow_three = Flow(
        ((encoded, grad_ck), (encoded, grad_cv), (enc_hidden, grad_branch)), seq_first=True
    )
    grad_branch = tick(grad_branch, fresh=(flow_three,))
    grad_pre = (back_dot(grad_branch, enc_wo) * enc_slope.astype(jnp.float32)).astype(low)
    grad_pre = tick(grad_pre, flow_one, flow_three)
    grad_input, gain_enc_two = norm_back(
        after_attn, inverse_two, enc_gains[1], back_dot(grad_pre, enc_wi)
    )
    grad_enc_first = grad_enc_second + grad_input
    grad_branch = grad_enc_first.astype(low)
    flow_four = Flow(((normed_two, grad_pre), (enc_mixed, grad_branch)))
    grad_branch, gain_enc_two = tick((grad_branch, gain_enc_two), fresh=(flow_four,))
    grad_mixed = back_dot(grad_branch, enc_proj).astype(low)
    grad_mixed = tick(grad_mixed, flow_four)
    pieces, line_grads, through = [], [], None
    flows = {0: (flow_two, flow_three, flow_four), 2: (flow_three, flow_four)}
    flows[4] = (flow_one, flow_two, flow_three, flow_four)
    for part in ((0, 2), (2, 2), (4, 2)):
        grad_eq, grad_ek, grad_ev, line_grad = attend_rows_back(
            rows,
            packed,
            0,
            packed,
            6,
            12,
            grad_mixed,
            enc_marks,
            enc_key_marks,
            enc_line,
            part,
        )
        grad_eq, grad_ek, grad_ev, line_grad, grad_mixed = tick(
            (grad_eq, grad_ek, grad_ev, line_grad, grad_mixed), *flows[part[0]]
        )
        line_grads.append(line_grad)
        pieces.append((grad_eq, grad_ek, grad_ev))
        for at, piece in enumerate((grad_eq, grad_ek, grad_ev)):
            start = at * width + part[0] * LANES
            term = back_dot(piece, enc_qkv[:, start : start + part[1] * LANES])
            through = term if through is None else through + term
        grad_mixed = after(grad_mixed, through)
    grad_input, gain_enc_one = norm_back(enc_values, inverse_one, enc_gains[0], through)
    enc_grad_row = (grad_enc_first + grad_input).astype(low)
    enc_line_grad = jnp.concatenate(line_grads, axis=0)
    rels = jnp.concatenate((rel_grad(enc_line_grad, enc_select), rel_grad_dec), axis=0)
    gains = jnp.stack(
        (gain_enc_one, gain_enc_two, gain_enc_three, gain_dec_one, gain_dec_two, gain_dec_three)
    )
    small = Small(jnp.concatenate((gains, rels.reshape(1, -1)), axis=0))
    enc_grad_row, pieces = tick((enc_grad_row, pieces), flow_three, flow_four, fresh=(small,))
    flow_five = Flow([(normed_one, piece[at]) for at in range(3) for piece in pieces])
    enc_grad_row = enc_grad_row.reshape(rows, shares, local_len, width)
    enc_grad = turn_rows(jnp.swapaxes(enc_grad_row, 0, 1)).reshape(enc_in.shape)

    dec_result = tick(dec_result, small, fresh=(flow_five,))
    dec_result = tick(dec_result, flow_five, small)
    dec_result = tick(dec_result, flow_five, small)
    dec_result, enc_grad = lax.optimization_barrier((dec_result, enc_grad))
    for unused in range(4):
        dec_result = tick(dec_result, flow_three, flow_four, flow_five, small)
    small = small.finish()
    gains_enc_total, gains_dec_total = small[:3], small[3:6]
    rels = small[6].reshape(2, NB, H)
    rel_enc_total, rel_dec_total = rels[0], rels[1]
    grad_dec_wo, grad_dec_wi = flow_one.finish()
    dec_q, dec_k, dec_v, grad_dec_proj, grad_cross_q, grad_cross_proj = flow_two.finish()
    cross_k, cross_v, grad_enc_wo = flow_three.finish()
    grad_enc_wi, grad_enc_proj = flow_four.finish()
    grad_enc_qkv = jnp.concatenate(flow_five.finish(), axis=1)
    return (
        dec_result.reshape(dec_in.shape),
        enc_grad.astype(jnp.float32),
        dec_in_grad.reshape(dec_in.shape),
        grad_enc_qkv,
        grad_enc_proj,
        grad_enc_wi,
        grad_enc_wo,
        rel_enc_total,
        gains_enc_total,
        jnp.concatenate((dec_q, dec_k, dec_v), axis=1),
        grad_dec_proj,
        rel_dec_total,
        grad_cross_q,
        jnp.concatenate((cross_k, cross_v), axis=1),
        grad_cross_proj,
        grad_dec_wi,
        grad_dec_wo,
        gains_dec_total,
    )


def solution(mesh):
    in_specs = (
        P("batch", "seq", None),
        P(("batch", "seq"), None, None),
        P(("batch", "seq"), None, None),
        P("batch", None),
        P(("batch", "seq"), None),
        P(),
        P(),
        P(),
        P(),
        P(),
        P(),
        P(),
        P(),
        P(),
        P(),
        P(),
        P(),
        P(),
        P(),
        P(),
    )
    out_specs = (
        P(("batch", "seq"), None, None),
        P("batch", "seq", None),
        P(("batch", "seq"), None, None),
        P(("batch", "seq"), None),
        P(("batch", "seq"), None),
        P(("batch", "seq"), None),
        P(("batch", "seq"), None),
        P(),
        P(),
        P(("batch", "seq"), None),
        P(("batch", "seq"), None),
        P(),
        P(("batch", "seq"), None),
        P(("batch", "seq"), None),
        P(("batch", "seq"), None),
        P(("batch", "seq"), None),
        P(("batch", "seq"), None),
        P(),
    )
    return jax.shard_map(body, mesh=mesh, in_specs=in_specs, out_specs=out_specs, check_vma=False)
```

```python
import functools
import math

import jax
import jax.numpy as jnp
import numpy as np
from jax import lax
from jax.experimental import pallas as pl
from jax.experimental.pallas import tpu as pltpu
from jax.sharding import PartitionSpec as P

H = 12
DK = 64
NB = 32
MAXD = 128
ENC_LEN = 1024
DEC_LEN = 256
LANES = 128
BQ = 256
BIG = 1e9
VLIM = 56 * 1024 * 1024
EPS = 1e-06

def bucket_steps(classes, distance, length):
    exact_part = classes // 2
    thresholds = []
    previous = 0
    for offset in range(1, length + 1):
        if offset < exact_part:
            bucket_level = offset
        else:
            bucket_level = min(
                classes - 1,
                exact_part
                + int(
                    math.log(offset / exact_part)
                    / math.log(distance / exact_part)
                    * (classes - exact_part)
                ),
            )
        if bucket_level > previous:
            thresholds.append((offset, bucket_level - previous))
            previous = bucket_level
    return thresholds


def step_buckets(distance, steps):
    buckets = np.zeros(distance.shape, np.int32)
    for edge, size in steps:
        buckets = buckets + size * (distance >= edge)
    return buckets


def line_offsets(queries, keys):
    place = np.arange(queries + keys)
    block = min(BQ, queries)
    wrapped = np.where(place >= queries + keys - block, place - queries - keys, place)
    return wrapped - (queries - block)


def enc_selector(length):
    offsets = line_offsets(length, length)
    half = NB // 2
    buckets = half * (offsets > 0) + step_buckets(np.abs(offsets), bucket_steps(half, MAXD, ENC_LEN))
    return jnp.asarray(buckets, jnp.int32)[:, None] == jnp.arange(NB, dtype=jnp.int32)[None, :]


def dec_selector(length):
    offsets = line_offsets(length, length)
    buckets = step_buckets(np.maximum(-offsets, 0), bucket_steps(NB, MAXD, DEC_LEN))
    return jnp.asarray(buckets, jnp.int32)[:, None] == jnp.arange(NB, dtype=jnp.int32)[None, :]


def bias_line(rel_table, selector):
    line = jnp.einsum(
        "nb,bh->hn", selector.astype(jnp.float32), rel_table, precision=lax.Precision.HIGHEST
    )
    return line.reshape(H // 2, 2, -1)


def rel_grad(line_grad, selector):
    return jnp.einsum(
        "hn,nb->bh",
        line_grad.reshape(H, -1),
        selector.astype(jnp.float32),
        precision=lax.Precision.HIGHEST,
    )


def gelu_pair(values):
    scale = math.sqrt(2.0 / math.pi)
    square = values * values
    curve = jnp.tanh(values * (scale + scale * 0.044715 * square))
    half = 0.5 * (1.0 + curve)
    inner = scale + 3.0 * scale * 0.044715 * square
    slope = half + 0.5 * values * (1.0 - curve * curve) * inner
    return (values * half).astype(jnp.bfloat16), slope.astype(jnp.bfloat16)


def row_dot(inputs, weight):
    return jnp.einsum("...i,ij->...j", inputs, weight, preferred_element_type=jnp.float32)


def back_dot(grad_vals, weight):
    return jnp.einsum("...j,ij->...i", grad_vals, weight, preferred_element_type=jnp.float32)


def weight_grad(inputs, grad_vals):
    return jnp.einsum(
        "ti,tj->ij",
        inputs.reshape(-1, inputs.shape[-1]),
        grad_vals.reshape(-1, grad_vals.shape[-1]),
        preferred_element_type=jnp.float32,
    )


def norm_fwd(values, gain_vec):
    inverse = lax.rsqrt(jnp.mean(values * values, axis=-1, keepdims=True) + EPS)
    return (values * inverse * gain_vec, inverse)


def norm_back(values, inverse, gain_vec, grad_vals):
    scaled = grad_vals * gain_vec
    grad_values = inverse * scaled - values * inverse**3 * jnp.mean(
        scaled * values, axis=-1, keepdims=True
    )
    grad_gain = jnp.sum((grad_vals * values * inverse).reshape(-1, values.shape[-1]), axis=0)
    return (grad_values, grad_gain)


NN=(((1,),(0,)),((),()))
NT=(((1,),(1,)),((),()))
TN=(((0,),(0,)),((),()))
def dot(a,b,dims=NN):
    return lax.dot_general(a,b,dims,preferred_element_type=jnp.float32)

def head_mask(rows):
    lane=lax.broadcasted_iota(jnp.int32,(rows,LANES),1)
    return lane<DK

def keep(x,first,head):
    zero=jnp.zeros_like(x)
    return jnp.where(first,x,zero) if head==0 else jnp.where(first,zero,x)

def skew_line(line_row,rows):
    width=line_row.shape[-1]
    wide=jnp.broadcast_to(line_row,(rows,width))
    return pltpu.roll(wide,0,1,stride=1,stride_axis=0)

def line_sums(band):
    rows,width=band.shape
    total=band[:8]
    for g in range(1,rows//8):
        total=total+pltpu.roll(band[8*g:8*g+8],width-8*g,1)
    row=lax.broadcasted_iota(jnp.int32,(8,width),0)
    for b in range(3):
        total=jnp.where((row>>b)&1==1,pltpu.roll(total,width-(1<<b),1),total)
    return jnp.sum(total,axis=0,keepdims=True)

def on_line(values,start,width):
    size=values.shape[1]
    blank=lambda n: [jnp.zeros((1,n),jnp.float32)] if n>0 else []
    if start>=0:
        return jnp.concatenate(blank(start)+[values]+blank(width-start-size),axis=1)
    late,early=values[:,-start:],values[:,:-start]
    late=jnp.concatenate([late]+blank(width-size-start),axis=1)
    return late+jnp.concatenate(blank(width+start)+[early],axis=1)

def fwd_kernel(bq,has_bias,*refs):
    if has_bias:
        q_ref,k_ref,v_ref,qx_ref,kx_ref,line_ref,o_ref,qb_ref,bias_ref=refs
    else:
        q_ref,k_ref,v_ref,qx_ref,kx_ref,o_ref,qb_ref=refs
    lq=q_ref.shape[0]; lk=k_ref.shape[0]
    wide=lk+lq-bq
    if has_bias:
        for h in range(2):
            bias_ref[h]=skew_line(line_ref[0,h:h+1,:],bq)[:,:wide]
    first=head_mask(bq)
    lane=lax.broadcasted_iota(jnp.int32,(bq,LANES),1)
    keys=jnp.concatenate((k_ref[...],kx_ref[...]),axis=1)
    values=v_ref[...]
    def score(n,h):
        rows=slice(n*bq,(n+1)*bq)
        return dot(jnp.concatenate((keep(q_ref[rows,:],first,h),qx_ref[rows,:]),axis=1),keys,NT)
    tiles=[(n,h) for n in range(lq//bq) for h in range(2)]
    ahead=score(*tiles[0])
    for at,(n,h) in enumerate(tiles):
        rows=slice(n*bq,(n+1)*bq)
        s=ahead
        if at+1<len(tiles):
            ahead=score(*tiles[at+1])
        if has_bias:
            bias=bias_ref[h,:,lq-bq-n*bq:lq-bq-n*bq+lk]
            top=jnp.max(s+bias,axis=1,keepdims=True)
            e=jnp.exp((s-top)+bias)
        else:
            top=jnp.max(s,axis=1,keepdims=True)
            e=jnp.exp(s-top)
        total=jnp.sum(e,axis=1,keepdims=True)
        p=(e*(1.0/total)).astype(jnp.bfloat16)
        out=dot(p,values)
        low=jnp.broadcast_to(-(top+jnp.log(total)),(bq,LANES))
        one=low.astype(jnp.bfloat16).astype(jnp.float32)
        two=(low-one).astype(jnp.bfloat16).astype(jnp.float32)
        three=low-one-two
        x=jnp.where(lane==4,one,jnp.where(lane==5,two,jnp.where(lane==6,three,qx_ref[rows,:].astype(jnp.float32))))
        qb_ref[h,rows,:]=x.astype(jnp.bfloat16)
        if h==0:
            kept=out
        else:
            o_ref[rows,:]=jnp.where(first,kept,out).astype(jnp.bfloat16)

def bwd_kernel(bq,has_bias,*refs):
    if has_bias:
        q_ref,k_ref,v_ref,g_ref,qb_ref,kx_ref,line_ref,dq_ref,dk_ref,dv_ref,dl_ref,bias_ref,acc_ref,far_ref,dka_ref,dva_ref=refs
    else:
        q_ref,k_ref,v_ref,g_ref,qb_ref,kx_ref,dq_ref,dk_ref,dv_ref,dka_ref,dva_ref=refs
    lq=q_ref.shape[0]; lk=k_ref.shape[0]
    wide=lk+lq-bq
    if has_bias:
        for h in range(2):
            bias_ref[h]=skew_line(line_ref[0,h:h+1,:],bq)[:,:wide]
        acc_ref[...]=jnp.zeros_like(acc_ref)
        far_ref[...]=jnp.zeros_like(far_ref)
    first=head_mask(bq)
    keyfirst=head_mask(lk)
    k=k_ref[...]
    keys=jnp.concatenate((k,kx_ref[...]),axis=1)
    values=v_ref[...]
    heads_k=[keep(k,keyfirst,h) for h in range(2)]
    def start(n,h):
        rows=slice(n*bq,(n+1)*bq)
        qh=keep(q_ref[rows,:],first,h); gh=keep(g_ref[rows,:],first,h)
        s=dot(jnp.concatenate((qh,qb_ref[h,rows,:]),axis=1),keys,NT)
        return qh,gh,s,dot(gh,values,NT)
    tiles=[(n,h) for n in range(lq//bq) for h in range(2)]
    ahead=start(*tiles[0])
    for at,(n,h) in enumerate(tiles):
        rows=slice(n*bq,(n+1)*bq)
        qh,gh,s,dp=ahead
        if at+1<len(tiles):
            ahead=start(*tiles[at+1])
        if has_bias:
            off=lq-bq-n*bq
            s=s+bias_ref[h,:,off:off+lk]
        p=jnp.exp(s)
        inner=jnp.sum(p*dp,axis=1,keepdims=True)
        gs=(p*(dp-inner)).astype(jnp.bfloat16)
        if has_bias:
            lo,hi=max(0,n*bq-LANES),min(lk,n*bq+bq+LANES)
            spot=lo-n*bq+LANES
            acc_ref[h,:,spot:spot+hi-lo]+=gs[:,lo:hi].astype(jnp.float32)
            for side,(a,b) in enumerate(((0,lo),(hi,lk))):
                if b>a:
                    total=gs[:,a:a+LANES].astype(jnp.float32)
                    for c in range(a+LANES,b,LANES):
                        total=total+gs[:,c:c+LANES].astype(jnp.float32)
                    far_ref[h,side]+=total
        dv=dot(gh,p.astype(jnp.bfloat16),TN)
        dk=dot(qh,gs,TN)
        if at==0:
            dva_ref[...]=dv; dka_ref[...]=dk
        else:
            dva_ref[...]+=dv; dka_ref[...]+=dk
        part=dot(gs,heads_k[h])
        if h==0:
            kept=part
        else:
            dq_ref[rows,:]=(kept+part).astype(jnp.bfloat16)
    dk_ref[...]=dka_ref[...].T.astype(jnp.bfloat16)
    dv_ref[...]=dva_ref[...].T.astype(jnp.bfloat16)
    if has_bias:
        width=line_ref.shape[-1]
        lane=lax.broadcasted_iota(jnp.int32,(1,width),1)
        for h in range(2):
            band=jnp.concatenate((acc_ref[h],jnp.zeros((bq,bq),jnp.float32)),axis=1)
            sums=pltpu.roll(line_sums(band),bq,1)
            line=on_line(sums,lq-2*bq-LANES,width)
            for side,place in enumerate((0,wide-1)):
                far=jnp.sum(far_ref[h,side],axis=0,keepdims=True)
                far=jnp.sum(far,axis=1,keepdims=True)
                line=line+jnp.where(lane==place,far,0.0)
            dl_ref[0,h:h+1,:]=line

def cost_of():
    return pl.CostEstimate(flops=1,bytes_accessed=1,transcendentals=0)

def attend(q,qc,k,kc,v,vc,qx,kx,line,bq):
    lq=q.shape[0]; lk=k.shape[0]
    bq=min(bq,lq)
    has=line is not None
    blk=lambda rows,c: pl.BlockSpec((rows,LANES),lambda i,c=c:(0,c+i))
    fix=lambda rows: pl.BlockSpec((rows,LANES),lambda i:(0,0))
    ins=[blk(lq,qc),blk(lk,kc),blk(lk,vc),fix(lq),fix(lk)]
    args=[q,k,v,qx,kx]
    scratch=[]
    if has:
        ins.append(pl.BlockSpec((1,2,line.shape[-1]),lambda i:(i,0,0))); args.append(line)
        scratch=[pltpu.VMEM((2,bq,lk+lq-bq),jnp.float32)]
    return pl.pallas_call(functools.partial(fwd_kernel,bq,has),grid=(H//2,),in_specs=ins,
        out_specs=[blk(lq,0),pl.BlockSpec((2,lq,LANES),lambda i:(i,0,0))],
        out_shape=[jax.ShapeDtypeStruct((lq,H*DK),jnp.bfloat16),jax.ShapeDtypeStruct((H,lq,LANES),jnp.bfloat16)],
        scratch_shapes=scratch,compiler_params=pltpu.CompilerParams(vmem_limit_bytes=VLIM),cost_estimate=cost_of(),name="attend")(*args)

def attend_back(q,qc,k,kc,v,vc,g,qb,kx,line,bq,pairs=None):
    lq=q.shape[0]; lk=k.shape[0]
    bq=min(bq,lq)
    has=line is not None
    start,count=(0,H//2) if pairs is None else pairs
    blk=lambda rows,c: pl.BlockSpec((rows,LANES),lambda i,c=c:(0,c+start+i))
    fix=lambda rows: pl.BlockSpec((rows,LANES),lambda i:(0,0))
    ins=[blk(lq,qc),blk(lk,kc),blk(lk,vc),blk(lq,0),pl.BlockSpec((2,lq,LANES),lambda i:(start+i,0,0)),fix(lk)]
    args=[q,k,v,g,qb,kx]
    outs=[pl.BlockSpec((n,LANES),lambda i:(0,i)) for n in (lq,lk,lk)]
    shapes=[jax.ShapeDtypeStruct((n,count*LANES),jnp.bfloat16) for n in (lq,lk,lk)]
    scratch=[]
    if has:
        w=line.shape[-1]
        ins.append(pl.BlockSpec((1,2,w),lambda i:(start+i,0,0))); args.append(line)
        outs.append(pl.BlockSpec((1,2,w),lambda i:(i,0,0)))
        shapes.append(jax.ShapeDtypeStruct((count,2,w),jnp.float32))
        scratch=[pltpu.VMEM((2,bq,lk+lq-bq),jnp.float32),pltpu.VMEM((2,bq,bq+2*LANES),jnp.float32),pltpu.VMEM((2,2,bq,LANES),jnp.float32)]
    scratch=scratch+[pltpu.VMEM((LANES,lk),jnp.float32)]*2
    return pl.pallas_call(functools.partial(bwd_kernel,bq,has),grid=(count,),in_specs=ins,out_specs=outs,out_shape=shapes,
        scratch_shapes=scratch,compiler_params=pltpu.CompilerParams(vmem_limit_bytes=VLIM),cost_estimate=cost_of(),name="attend_back")(*args)

def seg_features(q_segs,k_segs):
    ids=jnp.arange(LANES,dtype=jnp.int32)[None,:]
    qx=jnp.where((ids<4)&(q_segs[:,None]!=ids),-BIG,0.0).astype(jnp.bfloat16)
    kx=jnp.where(((ids<4)&(k_segs[:,None]==ids))|((ids>=4)&(ids<7)),1.0,0.0).astype(jnp.bfloat16)
    return qx,kx


def marks(query_segs, key_segs):
    pairs = [seg_features(q, k) for q, k in zip(query_segs, key_segs)]
    return [p[0] for p in pairs], [p[1] for p in pairs]


def row_of(array, row, rows):
    length = array.shape[0] // rows
    return array[row * length : (row + 1) * length]


def join(parts):
    return parts[0] if len(parts) == 1 else jnp.concatenate(parts, axis=0)


def attend_rows(rows, queries, q_col, pairs, k_col, v_col, query_marks, key_marks, line):
    outs, kept = [], []
    for r in range(rows):
        q, kv = row_of(queries, r, rows), row_of(pairs, r, rows)
        out, mark = attend(
            q, q_col, kv, k_col, kv, v_col, query_marks[r], key_marks[r], line, BQ
        )
        outs.append(out)
        kept.append(mark)
    return join(outs), kept


def attend_rows_back(
    rows, queries, q_col, pairs, k_col, v_col, grads, kept, key_marks, line, part=None
):
    results = []
    for r in range(rows):
        q, kv = row_of(queries, r, rows), row_of(pairs, r, rows)
        grad = row_of(grads, r, rows)
        results.append(
            attend_back(
                q, q_col, kv, k_col, kv, v_col, grad, kept[r], key_marks[r], line, BQ, part
            )
        )
    gq, gk, gv = (join([res[i] for res in results]) for i in range(3))
    return gq, gk, gv, None if line is None else sum(res[3] for res in results)


def turn_rows(array):
    return lax.all_to_all(array, "seq", split_axis=0, concat_axis=0, tiled=True)


def bits_of(axis_name):
    return lax.axis_size(axis_name).bit_length() - 1


def swap(array, axis_name, bit):
    pairs = [(i, i ^ (1 << bit)) for i in range(lax.axis_size(axis_name))]
    return lax.ppermute(array, axis_name, pairs)


def halve(array, axis_name, bit, dim):
    mine = (lax.axis_index(axis_name) >> bit) & 1
    kept = lax.dynamic_slice_in_dim(array, mine, 1, dim)
    return kept, lax.dynamic_slice_in_dim(array, 1 - mine, 1, dim)


def add(kept, got):
    return kept.astype(jnp.float32) + got.astype(jnp.float32)


def add_low(kept, got):
    return add(kept, got).astype(jnp.bfloat16)


def grads_kernel(plan, stills, ranks, shares, core_ref, *refs):
    o_count = 1 + max(p[3] for p in plan)
    l_count = 1 + max(p[0] for p in plan)
    a_refs, g_refs = refs[:l_count], refs[l_count : l_count + len(plan)]
    o_refs = refs[l_count + len(plan) : l_count + len(plan) + 2 * o_count]
    t_refs = refs[l_count + len(plan) + 2 * o_count :]
    step = pl.program_id(0)
    core = core_ref[0]
    turned = set()
    for index, (at, first, steps, out, block) in enumerate(plan):
        if at in stills and at not in turned:
            turned.add(at)

            @pl.when(step == first)
            def turn(at=at):
                t_refs[stills.index(at)][...] = a_refs[at][...].T

        for mine in range(2):

            @pl.when((step >= first) & (step < first + steps) & (core == mine))
            def work(index=index, at=at, out=out, block=block, mine=mine):
                left, right = a_refs[at], g_refs[index]
                height, columns = left.shape[1], right.shape[1]
                tiles, group = block // 8, shares * block
                if at in stills:
                    turned_left = t_refs[stills.index(at)][...]
                else:
                    turned_left = left[...].T
                for col in range(0, columns, 256):
                    result = dot(turned_left, right[:, col : col + 256])
                    for place in range(height // group):
                        target = o_refs[2 * out + (0 if place % 2 == mine else 1)]
                        home = place // 2 * shares
                        piece = paired(result[place * group : (place + 1) * group], shares, tiles)
                        spot = col // 256 * tiles
                        target[home : home + shares, spot : spot + tiles] = piece


def whole_kernel(plan, stills, ranks, shares, *refs):
    l_count = 1 + max(p[0] for p in plan)
    a_refs, g_refs = refs[:l_count], refs[l_count : l_count + len(plan)]
    target = refs[l_count + len(plan)]
    t_refs = refs[l_count + len(plan) + 1 :]
    step = pl.program_id(0)
    turned = set()
    for index, (at, first, steps, start, block) in enumerate(plan):
        if at in stills and at not in turned:
            turned.add(at)

            @pl.when(step == first)
            def turn(at=at):
                t_refs[stills.index(at)][...] = a_refs[at][...].T

        @pl.when((step >= first) & (step < first + steps))
        def work(index=index, at=at, start=start, first=first, block=block):
            left, right = a_refs[at], g_refs[index]
            height, columns = left.shape[1], right.shape[1]
            tiles, group = block // 8, shares * block
            if at in stills:
                turned_left = t_refs[stills.index(at)][...]
                home, spot = 0, start + (step - first) * (columns // 256 * tiles)
            else:
                turned_left = left[...].T
                home, spot = (step - first) * (height // block), start
            for col in range(0, columns, 256):
                result = dot(turned_left, right[:, col : col + 256])
                for place in range(height // group):
                    piece = paired(result[place * group : (place + 1) * group], shares, tiles)
                    target[
                        pl.ds(home + place * shares, shares), pl.ds(spot + col // 256 * tiles, tiles)
                    ] = piece


def paired(piece, shares, tiles):
    halves = [
        piece[:, side * LANES : (side + 1) * LANES].reshape(shares, tiles, 8, LANES)
        for side in range(2)
    ]
    return jnp.concatenate(halves, axis=2).astype(jnp.bfloat16)


def tile_columns(shapes):
    columns = {}
    for height, width in shapes:
        columns[height] = math.gcd(columns.get(height, 768), width)
    return columns


def packed_grads(items, split=True):
    ranks = lax.axis_size("batch") * lax.axis_size("seq")
    shares = lax.axis_size("seq")
    shapes_in = [(left.shape[1], right.shape[1]) for left, right in items]
    widths = tile_columns(shapes_in)
    least = min(height for height, width in shapes_in)
    outs, plan, totals, firsts, stills = [], [], [], [], []
    lefts, left_specs, right_specs = [], [], []
    step = 0
    for left, right in items:
        height, width = left.shape[1], right.shape[1]
        if height not in outs:
            outs.append(height)
            totals.append(0)
            firsts.append(step)
        out = outs.index(height)
        tall = height > least
        steps = height // least if tall else width // widths[height]
        at = lambda i, c, first=step, last=steps - 1: (0, jnp.clip(i - first, 0, last))
        still = lambda i, c: (0, 0)
        same = [i for i in stills if lefts[i] is left]
        if same and not tall:
            where = same[0]
        else:
            where = len(lefts)
            lefts.append(left)
            left_specs.append(pl.BlockSpec((left.shape[0], least), at if tall else still))
            if not tall:
                stills.append(where)
        right_specs.append(pl.BlockSpec((right.shape[0], widths[height]), still if tall else at))
        plan.append((where, step, steps, out, height // ranks))
        totals[out] += steps
        step += steps
    shapes, specs = [], []
    for out, height in enumerate(outs):
        size = (height // ranks // 8) * (widths[height] // 256)
        tall = height > least
        count = 1 if tall else totals[out]
        parts = totals[out] if tall else 1
        for side in range(2):
            shapes.append(
                jax.ShapeDtypeStruct((ranks // 2, size * count, 16, LANES), jnp.bfloat16)
            )
            at = lambda i, c, first=firsts[out], last=totals[out] - 1, tall=tall: (
                (jnp.clip(i - first, 0, last), 0, 0, 0)
                if tall
                else (0, jnp.clip(i - first, 0, last), 0, 0)
            )
            specs.append(pl.BlockSpec((ranks // 2 // parts, size, 16, LANES), at))
    cost = cost_of()
    turned = [pltpu.VMEM((lefts[i].shape[1], lefts[i].shape[0]), jnp.bfloat16) for i in stills]
    if not split:
        whole_plan, tiles = [], 0
        for out in range(len(outs)):
            for where, first, steps, item_out, block in plan:
                if item_out == out:
                    whole_plan.append((where, first, steps, tiles, block))
                    height, width = shapes_in[len(whole_plan) - 1]
                    tiles += block // 8 * (width // 256)
        drop = lambda at: lambda i: at(i, None)
        return pl.pallas_call(
            functools.partial(whole_kernel, whole_plan, stills, ranks, shares),
            grid=(step,),
            in_specs=[
                pl.BlockSpec(x.block_shape, drop(x.index_map)) for x in left_specs + right_specs
            ],
            out_specs=pl.BlockSpec((ranks, tiles, 16, LANES), lambda i: (0, 0, 0, 0)),
            out_shape=jax.ShapeDtypeStruct((ranks, tiles, 16, LANES), jnp.bfloat16),
            scratch_shapes=turned,
            compiler_params=pltpu.CompilerParams(vmem_limit_bytes=VLIM),
            cost_estimate=cost,
            name="whole_grads",
        )(*lefts, *[right for left, right in items])
    core = (lax.axis_index("batch") & 1).astype(jnp.int32).reshape(1)
    results = pl.pallas_call(
        functools.partial(grads_kernel, plan, stills, ranks, shares),
        grid_spec=pltpu.PrefetchScalarGridSpec(
            num_scalar_prefetch=1,
            grid=(step,),
            in_specs=left_specs + right_specs,
            out_specs=specs,
            scratch_shapes=turned,
        ),
        out_shape=shapes,
        compiler_params=pltpu.CompilerParams(vmem_limit_bytes=VLIM),
        cost_estimate=cost,
        name="packed_grads",
    )(core, *lefts, *[right for left, right in items])
    return results[0::2], results[1::2]


def after(value, *others):
    return lax.optimization_barrier((value,) + others)[0]


class Small:
    def __init__(self, values):
        self.sent, self.got, self.kept = [values], [], values
        self.stages = [("seq", -1)] + [("batch", bit) for bit in range(bits_of("batch"))]

    def launch(self, sent):
        name, bit = self.stages.pop(0)
        if bit >= 0:
            self.got = [swap(sent[0], name, bit)]
            return
        size = lax.axis_size(name)
        self.got = [
            lax.ppermute(sent[0], name, [(i, i ^ step) for i in range(size)])
            for step in range(1, size)
        ]

    def advance(self, got):
        terms = [self.kept] + got
        while len(terms) > 1:
            terms = [terms[i] + terms[i + 1] for i in range(0, len(terms), 2)]
        self.kept = terms[0]
        self.got = []
        self.sent = [self.kept] if self.stages else []

    def finish(self):
        return self.kept


class Flow:
    def __init__(self, items, split=True, seq_first=False):
        self.split, self.seq_first = split, seq_first
        self.shapes = [(left.shape[1], right.shape[1]) for left, right in items]
        self.high, self.low = bits_of("batch"), bits_of("seq")
        self.ranks = 1 << (self.high + self.low)
        self.plain = min(shape[0] for shape in self.shapes) % (8 * self.ranks) != 0
        self.got, self.stage = [], 0
        if self.plain:
            self.sent = []
            self.whole = [weight_grad(left, right) for left, right in items]
            return
        heights = []
        for shape in self.shapes:
            if shape[0] not in heights:
                heights.append(shape[0])
        self.order = [
            [i for i, shape in enumerate(self.shapes) if shape[0] == height] for height in heights
        ]
        if split:
            self.kept, self.sent = packed_grads(items)
        else:
            self.sent = [packed_grads(items, False)]
        ups = [("batch", bit) for bit in range(1, self.high)]
        alongs = [("seq", bit) for bit in range(self.low)]
        if seq_first:
            self.steps = [[step] for step in alongs + ups]
        else:
            self.steps = [list(pair) for pair in zip(ups, ups[::-1])] + [[x] for x in alongs]

    def launch(self, sent):
        if self.plain:
            return
        if not self.split:
            axis_name = ("batch", "seq")[self.stage]
            self.got = [lax.psum_scatter(sent[0], axis_name, scatter_dimension=0, tiled=True)]
        elif self.stage == 0:
            self.got = [swap(x, "batch", 0) for x in sent]
        else:
            steps = self.steps[self.stage - 1]
            self.got = [swap(x, name, bit) for x, (name, bit) in zip(sent, steps)]
        self.stage += 1

    def advance(self, got):
        last = self.high - 1
        dim = last + self.low
        if not self.split:
            self.got, self.sent = [], got if self.stage == 1 else []
            self.result = got[0].astype(jnp.float32)
            return
        if self.stage > len(self.steps):
            self.result = add(self.kept[0], got[0])
            self.got, self.sent = [], []
            return
        sums = [add_low(k, g) for k, g in zip(self.kept, got)]
        if self.stage == 1:
            sums = [x.reshape((2,) * dim + x.shape[1:]) for x in sums]
        steps = self.steps[self.stage - 1]
        if len(sums) > len(steps):
            sums = [jnp.concatenate(sums, axis=dim)]
        elif len(sums) < len(steps):
            size = sums[0].shape[dim]
            sums = [
                lax.slice_in_dim(sums[0], 0, size // 2, axis=dim),
                lax.slice_in_dim(sums[0], size // 2, size, axis=dim),
            ]
        halves = [
            halve(x, name, bit, (last if name == "batch" else dim - 1) - bit)
            for x, (name, bit) in zip(sums, steps)
        ]
        self.kept = [h[0] for h in halves]
        self.sent = [h[1] for h in halves]

    def finish(self):
        if not self.plain and not self.split:
            while self.got:
                self.advance(self.got)
                if self.sent:
                    self.launch(self.sent)
        if self.plain:
            results = []
            for grad in self.whole:
                grad = lax.psum_scatter(
                    grad.astype(jnp.bfloat16), ("batch", "seq"), scatter_dimension=0, tiled=True
                )
                results.append(grad.astype(jnp.float32))
            return results
        while self.got:
            self.advance(self.got)
            if self.sent:
                self.launch(self.sent)
        part = self.result.reshape(-1, 16, LANES)
        results, start = [None] * len(self.shapes), 0
        for indices in self.order:
            for i in indices:
                height, width = self.shapes[i]
                tiles = height // self.ranks // 8
                count = tiles * width // 256
                piece = part[start : start + count]
                start += count
                piece = piece.reshape(width // 256, tiles, 2, 8, LANES)
                piece = jnp.transpose(piece, (1, 3, 0, 2, 4))
                results[i] = piece.reshape(tiles * 8, width)
        return results


def tick(value, *flows, fresh=()):
    live = [flow for flow in flows if flow is not None and flow.got]
    gots = [flow.got for flow in live]
    sents = [list(flow.sent) for flow in fresh]
    value, gots, sents = lax.optimization_barrier((value, gots, sents))
    for flow, sent in zip(fresh, sents):
        flow.launch(sent)
    for flow, got in zip(live, gots):
        flow.advance(got)
    value, sents = lax.optimization_barrier((value, [list(flow.sent) for flow in live]))
    for flow, sent in zip(live, sents):
        if sent:
            flow.launch(sent)
    return value


def body(
    enc_in,
    dec_in,
    out_grad,
    enc_segs,
    dec_segs,
    enc_qkv,
    enc_proj,
    enc_wi,
    enc_wo,
    enc_rel,
    enc_gains,
    dec_qkv,
    dec_proj,
    dec_rel,
    cross_q,
    cross_kv,
    cross_proj,
    dec_wi,
    dec_wo,
    dec_gains,
):
    shares = lax.axis_size("seq")
    rows = enc_in.shape[0] // shares
    full_len = enc_segs.shape[1]
    target_len = dec_in.shape[1]
    width = enc_in.shape[2]
    low = jnp.bfloat16
    row_segs = lax.dynamic_slice_in_dim(enc_segs, lax.axis_index("seq") * rows, rows, 0)

    local_len = enc_in.shape[1]
    enc_row = turn_rows(enc_in.reshape(shares, rows, local_len, width))
    enc_values = jnp.swapaxes(enc_row, 0, 1).reshape(-1, width).astype(jnp.float32)
    dec_values = dec_in.reshape(-1, width).astype(jnp.float32)

    enc_select = enc_selector(full_len)
    dec_select = dec_selector(target_len)
    enc_line = bias_line(enc_rel, enc_select)
    dec_offsets = jnp.asarray(line_offsets(target_len, target_len), jnp.int32)
    dec_line = jnp.where(dec_offsets > 0, -BIG, bias_line(dec_rel, dec_select))
    enc_query_marks, enc_key_marks = marks(row_segs, row_segs)
    dec_query_marks, dec_key_marks = marks(dec_segs, dec_segs)

    dec_normed_one, dec_inverse_one = norm_fwd(dec_values, dec_gains[0])
    dec_normed_one = dec_normed_one.astype(low)
    dec_packed = row_dot(dec_normed_one, dec_qkv).astype(low)
    self_mixed, self_marks = attend_rows(
        rows, dec_packed, 0, dec_packed, 6, 12, dec_query_marks, dec_key_marks, dec_line
    )
    dec_first = dec_values + row_dot(self_mixed, dec_proj)
    dec_normed_two, dec_inverse_two = norm_fwd(dec_first, dec_gains[1])
    dec_normed_two = dec_normed_two.astype(low)
    cross_query = row_dot(dec_normed_two, cross_q).astype(low)

    normed_one, inverse_one = norm_fwd(enc_values, enc_gains[0])
    normed_one = normed_one.astype(low)
    packed = row_dot(normed_one, enc_qkv).astype(low)
    enc_mixed, enc_marks = attend_rows(
        rows, packed, 0, packed, 6, 12, enc_query_marks, enc_key_marks, enc_line
    )
    after_attn = enc_values + row_dot(enc_mixed, enc_proj)
    normed_two, inverse_two = norm_fwd(after_attn, enc_gains[1])
    normed_two = normed_two.astype(low)
    enc_hidden, enc_slope = gelu_pair(row_dot(normed_two, enc_wi))
    second = after_attn + row_dot(enc_hidden, enc_wo)
    encoded, inverse_three = norm_fwd(second, enc_gains[2])
    encoded = encoded.astype(low)
    cross_pack = row_dot(encoded, cross_kv).astype(low)

    cross_mixed, cross_marks = attend_rows(
        rows, cross_query, 0, cross_pack, 0, 6, dec_query_marks, enc_key_marks, None
    )
    dec_second = dec_first + row_dot(cross_mixed, cross_proj)
    dec_normed_three, dec_inverse_three = norm_fwd(dec_second, dec_gains[2])
    dec_normed_three = dec_normed_three.astype(low)
    dec_hidden, dec_slope = gelu_pair(row_dot(dec_normed_three, dec_wi))
    dec_result = (dec_second + row_dot(dec_hidden, dec_wo)).astype(low)

    upstream = out_grad.reshape(-1, width)
    grad_pre = (back_dot(upstream, dec_wo) * dec_slope.astype(jnp.float32)).astype(low)
    flow_one = Flow(((dec_hidden, upstream), (dec_normed_three, grad_pre)), False)
    grad_pre, dec_result = tick((grad_pre, dec_result), fresh=(flow_one,))
    grad_input, gain_dec_three = norm_back(
        dec_second, dec_inverse_three, dec_gains[2], back_dot(grad_pre, dec_wi)
    )
    grad_second = upstream.astype(jnp.float32) + grad_input
    grad_cross_branch = grad_second.astype(low)
    grad_mixed = back_dot(grad_cross_branch, cross_proj).astype(low)
    grad_cq, grad_ck, grad_cv, unused = attend_rows_back(
        rows, cross_query, 0, cross_pack, 0, 6, grad_mixed, cross_marks, enc_key_marks, None
    )
    grad_input, gain_dec_two = norm_back(
        dec_first, dec_inverse_two, dec_gains[1], back_dot(grad_cq, cross_q)
    )
    grad_first = grad_second + grad_input
    grad_self_branch = grad_first.astype(low)
    grad_mixed = back_dot(grad_self_branch, dec_proj).astype(low)
    grad_sq, grad_sk, grad_sv, dec_line_grad = attend_rows_back(
        rows, dec_packed, 0, dec_packed, 6, 12, grad_mixed, self_marks, dec_key_marks, dec_line
    )
    flow_two = Flow(
        (
            (dec_normed_one, grad_sq),
            (dec_normed_one, grad_sk),
            (dec_normed_one, grad_sv),
            (self_mixed, grad_self_branch),
            (dec_normed_two, grad_cq),
            (cross_mixed, grad_cross_branch),
        ),
        False,
    )
    (grad_sq, grad_ck, dec_line_grad, gain_dec_three, gain_dec_two) = tick(
        (grad_sq, grad_ck, dec_line_grad, gain_dec_three, gain_dec_two), fresh=(flow_two,)
    )
    grad_input, gain_dec_one = norm_back(
        dec_values,
        dec_inverse_one,
        dec_gains[0],
        back_dot(grad_sq, dec_qkv[:, :width])
        + back_dot(grad_sk, dec_qkv[:, width : 2 * width])
        + back_dot(grad_sv, dec_qkv[:, 2 * width :]),
    )
    dec_in_grad = grad_first + grad_input
    rel_grad_dec = rel_grad(dec_line_grad, dec_select)

    grad_enc_second, gain_enc_three = norm_back(
        second,
        inverse_three,
        enc_gains[2],
        back_dot(grad_ck, cross_kv[:, :width]) + back_dot(grad_cv, cross_kv[:, width:]),
    )
    grad_branch = grad_enc_second.astype(low)
    grad_branch, dec_in_grad, gain_dec_one, rel_grad_dec, gain_enc_three = tick(
        (grad_branch, dec_in_grad, gain_dec_one, rel_grad_dec, gain_enc_three)
    )
    flow_three = Flow(
        ((encoded, grad_ck), (encoded, grad_cv), (enc_hidden, grad_branch)), seq_first=True
    )
    grad_branch = tick(grad_branch, fresh=(flow_three,))
    grad_pre = (back_dot(grad_branch, enc_wo) * enc_slope.astype(jnp.float32)).astype(low)
    grad_pre = tick(grad_pre, flow_one, flow_three)
    grad_input, gain_enc_two = norm_back(
        after_attn, inverse_two, enc_gains[1], back_dot(grad_pre, enc_wi)
    )
    grad_enc_first = grad_enc_second + grad_input
    grad_branch = grad_enc_first.astype(low)
    flow_four = Flow(((normed_two, grad_pre), (enc_mixed, grad_branch)))
    grad_branch, gain_enc_two = tick((grad_branch, gain_enc_two), fresh=(flow_four,))
    grad_mixed = back_dot(grad_branch, enc_proj).astype(low)
    grad_mixed = tick(grad_mixed, flow_four)
    pieces, line_grads, through = [], [], None
    flows = {0: (flow_two, flow_three, flow_four), 2: (flow_four,)}
    flows[4] = (flow_one, flow_two, flow_three, flow_four)
    for part in ((0, 2), (2, 2), (4, 2)):
        grad_eq, grad_ek, grad_ev, line_grad = attend_rows_back(
            rows,
            packed,
            0,
            packed,
            6,
            12,
            grad_mixed,
            enc_marks,
            enc_key_marks,
            enc_line,
            part,
        )
        grad_eq, grad_ek, grad_ev, line_grad, grad_mixed = tick(
            (grad_eq, grad_ek, grad_ev, line_grad, grad_mixed), *flows[part[0]]
        )
        line_grads.append(line_grad)
        pieces.append((grad_eq, grad_ek, grad_ev))
        for at, piece in enumerate((grad_eq, grad_ek, grad_ev)):
            start = at * width + part[0] * LANES
            term = back_dot(piece, enc_qkv[:, start : start + part[1] * LANES])
            through = term if through is None else through + term
        grad_mixed = after(grad_mixed, through)
    grad_input, gain_enc_one = norm_back(enc_values, inverse_one, enc_gains[0], through)
    enc_grad_row = (grad_enc_first + grad_input).astype(low)
    enc_line_grad = jnp.concatenate(line_grads, axis=0)
    rels = jnp.concatenate((rel_grad(enc_line_grad, enc_select), rel_grad_dec), axis=0)
    gains = jnp.stack(
        (gain_enc_one, gain_enc_two, gain_enc_three, gain_dec_one, gain_dec_two, gain_dec_three)
    )
    small = Small(jnp.concatenate((gains, rels.reshape(1, -1)), axis=0))
    enc_grad_row = tick(enc_grad_row, flow_three, flow_four, fresh=(small,))
    enc_grad_row = enc_grad_row.reshape(rows, shares, local_len, width)
    enc_grad = turn_rows(jnp.swapaxes(enc_grad_row, 0, 1)).reshape(enc_in.shape)
    pieces = tick(pieces, small)
    flow_five = Flow([(normed_one, piece[at]) for at in range(3) for piece in pieces])

    dec_result = tick(dec_result, fresh=(flow_five,))
    dec_result = tick(dec_result, flow_five, small)
    dec_result = tick(dec_result, flow_five, small)
    dec_result = tick(dec_result, flow_three, flow_five, small)
    dec_result, enc_grad = lax.optimization_barrier((dec_result, enc_grad))
    for unused in range(3):
        dec_result = tick(dec_result, flow_three, flow_four, flow_five, small)
    small = small.finish()
    gains_enc_total, gains_dec_total = small[:3], small[3:6]
    rels = small[6].reshape(2, NB, H)
    rel_enc_total, rel_dec_total = rels[0], rels[1]
    grad_dec_wo, grad_dec_wi = flow_one.finish()
    dec_q, dec_k, dec_v, grad_dec_proj, grad_cross_q, grad_cross_proj = flow_two.finish()
    cross_k, cross_v, grad_enc_wo = flow_three.finish()
    grad_enc_wi, grad_enc_proj = flow_four.finish()
    grad_enc_qkv = jnp.concatenate(flow_five.finish(), axis=1)
    return (
        dec_result.reshape(dec_in.shape),
        enc_grad.astype(jnp.float32),
        dec_in_grad.reshape(dec_in.shape),
        grad_enc_qkv,
        grad_enc_proj,
        grad_enc_wi,
        grad_enc_wo,
        rel_enc_total,
        gains_enc_total,
        jnp.concatenate((dec_q, dec_k, dec_v), axis=1),
        grad_dec_proj,
        rel_dec_total,
        grad_cross_q,
        jnp.concatenate((cross_k, cross_v), axis=1),
        grad_cross_proj,
        grad_dec_wi,
        grad_dec_wo,
        gains_dec_total,
    )


def solution(mesh):
    in_specs = (
        P("batch", "seq", None),
        P(("batch", "seq"), None, None),
        P(("batch", "seq"), None, None),
        P("batch", None),
        P(("batch", "seq"), None),
        P(),
        P(),
        P(),
        P(),
        P(),
        P(),
        P(),
        P(),
        P(),
        P(),
        P(),
        P(),
        P(),
        P(),
        P(),
    )
    out_specs = (
        P(("batch", "seq"), None, None),
        P("batch", "seq", None),
        P(("batch", "seq"), None, None),
        P(("batch", "seq"), None),
        P(("batch", "seq"), None),
        P(("batch", "seq"), None),
        P(("batch", "seq"), None),
        P(),
        P(),
        P(("batch", "seq"), None),
        P(("batch", "seq"), None),
        P(),
        P(("batch", "seq"), None),
        P(("batch", "seq"), None),
        P(("batch", "seq"), None),
        P(("batch", "seq"), None),
        P(("batch", "seq"), None),
        P(),
    )
    return jax.shard_map(body, mesh=mesh, in_specs=in_specs, out_specs=out_specs, check_vma=False)
```

```python
import functools
import math

import jax
import jax.numpy as jnp
import numpy as np
from jax import lax
from jax.experimental import pallas as pl
from jax.experimental.pallas import tpu as pltpu
from jax.sharding import PartitionSpec as P

H = 12
DK = 64
NB = 32
MAXD = 128
ENC_LEN = 1024
DEC_LEN = 256
LANES = 128
BQ = 256
BIG = 1e9
VLIM = 56 * 1024 * 1024
EPS = 1e-06

def bucket_steps(classes, distance, length):
    exact_part = classes // 2
    thresholds = []
    previous = 0
    for offset in range(1, length + 1):
        if offset < exact_part:
            bucket_level = offset
        else:
            bucket_level = min(
                classes - 1,
                exact_part
                + int(
                    math.log(offset / exact_part)
                    / math.log(distance / exact_part)
                    * (classes - exact_part)
                ),
            )
        if bucket_level > previous:
            thresholds.append((offset, bucket_level - previous))
            previous = bucket_level
    return thresholds


def step_buckets(distance, steps):
    buckets = np.zeros(distance.shape, np.int32)
    for edge, size in steps:
        buckets = buckets + size * (distance >= edge)
    return buckets


def line_offsets(queries, keys):
    place = np.arange(queries + keys)
    block = min(BQ, queries)
    wrapped = np.where(place >= queries + keys - block, place - queries - keys, place)
    return wrapped - (queries - block)


def turned_offsets(queries, keys):
    block = min(BQ, queries)
    place = np.arange(2 * block)
    wrapped = np.where(place >= block, place - 2 * block, place)
    starts = np.arange(0, keys + queries - block, block) - (queries - block)
    return (starts[:, None] - wrapped[None, :]).reshape(-1)


def enc_selector(offsets):
    half = NB // 2
    buckets = half * (offsets > 0) + step_buckets(np.abs(offsets), bucket_steps(half, MAXD, ENC_LEN))
    return jnp.asarray(buckets, jnp.int32)[:, None] == jnp.arange(NB, dtype=jnp.int32)[None, :]


def dec_selector(offsets):
    buckets = step_buckets(np.maximum(-offsets, 0), bucket_steps(NB, MAXD, DEC_LEN))
    return jnp.asarray(buckets, jnp.int32)[:, None] == jnp.arange(NB, dtype=jnp.int32)[None, :]


def bias_line(rel_table, selector):
    line = jnp.einsum(
        "nb,bh->hn", selector.astype(jnp.float32), rel_table, precision=lax.Precision.HIGHEST
    )
    return line.reshape(H // 2, 2, -1)


def rel_grad(line_grad, selector):
    return jnp.einsum(
        "hn,nb->bh",
        line_grad.reshape(H, -1),
        selector.astype(jnp.float32),
        precision=lax.Precision.HIGHEST,
    )


def gelu_pair(values):
    scale = math.sqrt(2.0 / math.pi)
    square = values * values
    curve = jnp.tanh(values * (scale + scale * 0.044715 * square))
    half = 0.5 * (1.0 + curve)
    inner = scale + 3.0 * scale * 0.044715 * square
    slope = half + 0.5 * values * (1.0 - curve * curve) * inner
    return (values * half).astype(jnp.bfloat16), slope.astype(jnp.bfloat16)


def row_dot(inputs, weight):
    return jnp.einsum("...i,ij->...j", inputs, weight, preferred_element_type=jnp.float32)


def back_dot(grad_vals, weight):
    return jnp.einsum("...j,ij->...i", grad_vals, weight, preferred_element_type=jnp.float32)


def weight_grad(inputs, grad_vals):
    return jnp.einsum(
        "ti,tj->ij",
        inputs.reshape(-1, inputs.shape[-1]),
        grad_vals.reshape(-1, grad_vals.shape[-1]),
        preferred_element_type=jnp.float32,
    )


def slope_kernel(grad_ref, weight_ref, slope_ref, out_ref):
    weight = weight_ref[...]
    for at in range(0, grad_ref.shape[0], 256):
        rows = slice(at, at + 256)
        grad = dot(grad_ref[rows, :], weight, NT)
        out_ref[rows, :] = (grad * slope_ref[rows, :].astype(jnp.float32)).astype(jnp.bfloat16)


def slope_back(grad, weight, slope):
    tokens, hidden = slope.shape
    step = 768
    return pl.pallas_call(
        slope_kernel,
        grid=(hidden // step,),
        in_specs=[
            pl.BlockSpec(grad.shape, lambda i: (0, 0)),
            pl.BlockSpec((step, weight.shape[1]), lambda i: (i, 0)),
            pl.BlockSpec((tokens, step), lambda i: (0, i)),
        ],
        out_specs=pl.BlockSpec((tokens, step), lambda i: (0, i)),
        out_shape=jax.ShapeDtypeStruct(slope.shape, jnp.bfloat16),
        compiler_params=pltpu.CompilerParams(vmem_limit_bytes=VLIM),
        cost_estimate=cost_of(),
        name="slope_back",
    )(grad, weight, slope)


def norm_fwd(values, gain_vec):
    inverse = lax.rsqrt(jnp.mean(values * values, axis=-1, keepdims=True) + EPS)
    return (values * inverse * gain_vec, inverse)


def norm_back(values, inverse, gain_vec, grad_vals):
    scaled = grad_vals * gain_vec
    grad_values = inverse * scaled - values * inverse**3 * jnp.mean(
        scaled * values, axis=-1, keepdims=True
    )
    grad_gain = jnp.sum((grad_vals * values * inverse).reshape(-1, values.shape[-1]), axis=0)
    return (grad_values, grad_gain)


NN=(((1,),(0,)),((),()))
NT=(((1,),(1,)),((),()))
TN=(((0,),(0,)),((),()))
def dot(a,b,dims=NN):
    return lax.dot_general(a,b,dims,preferred_element_type=jnp.float32)

def head_mask(rows):
    lane=lax.broadcasted_iota(jnp.int32,(rows,LANES),1)
    return lane<DK

def keep(x,first,head):
    zero=jnp.zeros_like(x)
    return jnp.where(first,x,zero) if head==0 else jnp.where(first,zero,x)

def skew_line(line_row,rows):
    width=line_row.shape[-1]
    wide=jnp.broadcast_to(line_row,(rows,width))
    return pltpu.roll(wide,0,1,stride=1,stride_axis=0)

def line_sums(band):
    rows,width=band.shape
    total=band[:8]
    for g in range(1,rows//8):
        total=total+pltpu.roll(band[8*g:8*g+8],width-8*g,1)
    row=lax.broadcasted_iota(jnp.int32,(8,width),0)
    for b in range(3):
        total=jnp.where((row>>b)&1==1,pltpu.roll(total,width-(1<<b),1),total)
    return jnp.sum(total,axis=0,keepdims=True)

def on_line(values,start,width):
    size=values.shape[1]
    blank=lambda n: [jnp.zeros((1,n),jnp.float32)] if n>0 else []
    if start>=0:
        return jnp.concatenate(blank(start)+[values]+blank(width-start-size),axis=1)
    late,early=values[:,-start:],values[:,:-start]
    late=jnp.concatenate([late]+blank(width-size-start),axis=1)
    return late+jnp.concatenate(blank(width+start)+[early],axis=1)

def fwd_kernel(bq,has_bias,*refs):
    if has_bias:
        q_ref,k_ref,v_ref,qx_ref,kx_ref,line_ref,o_ref,qb_ref,bias_ref=refs
    else:
        q_ref,k_ref,v_ref,qx_ref,kx_ref,o_ref,qb_ref=refs
    lq=q_ref.shape[0]; lk=k_ref.shape[0]
    if has_bias:
        for h in range(2):
            for b in range(bias_ref.shape[1]//bq):
                source=line_ref[0,h:h+1,2*b*bq:2*(b+1)*bq]
                least=b*bq-(lq-bq)-(bq-1)
                if least>=MAXD or least+2*bq-2<=-MAXD:
                    block=jnp.broadcast_to(source[:,:bq],(bq,bq))
                else:
                    block=skew_line(source,bq)[:,:bq]
                bias_ref[h,b*bq:(b+1)*bq,:]=block
    first=head_mask(bq)
    row=lax.broadcasted_iota(jnp.int32,(LANES,bq),0)
    keys=jnp.concatenate((k_ref[...],kx_ref[...]),axis=1)
    values=v_ref[...].T
    def score(n,h):
        rows=slice(n*bq,(n+1)*bq)
        return dot(keys,jnp.concatenate((keep(q_ref[rows,:],first,h),qx_ref[rows,:]),axis=1),NT)
    tiles=[(n,h) for n in range(lq//bq) for h in range(2)]
    ahead=score(*tiles[0])
    for at,(n,h) in enumerate(tiles):
        rows=slice(n*bq,(n+1)*bq)
        s=ahead
        if at+1<len(tiles):
            ahead=score(*tiles[at+1])
        if has_bias:
            off=lq-bq-n*bq
            bias=bias_ref[h,off:off+lk,:]
            top=jnp.max(s+bias,axis=0,keepdims=True)
            e=jnp.exp((s-top)+bias)
        else:
            top=jnp.max(s,axis=0,keepdims=True)
            e=jnp.exp(s-top)
        total=jnp.sum(e,axis=0,keepdims=True)
        p=(e*(1.0/total)).astype(jnp.bfloat16)
        out=dot(values,p)
        low=-(top+jnp.log(total))
        one=low.astype(jnp.bfloat16).astype(jnp.float32)
        two=(low-one).astype(jnp.bfloat16).astype(jnp.float32)
        three=low-one-two
        x=jnp.where(row==4,one,jnp.where(row==5,two,jnp.where(row==6,three,0.0)))
        qb_ref[h,rows,:]=(x.T+qx_ref[rows,:].astype(jnp.float32)).astype(jnp.bfloat16)
        if h==0:
            kept=out
        else:
            o_ref[rows,:]=jnp.where(row<DK,kept,out).T.astype(jnp.bfloat16)

def bwd_kernel(bq,has_bias,*refs):
    if has_bias:
        q_ref,k_ref,v_ref,g_ref,qb_ref,kx_ref,line_ref,dq_ref,dk_ref,dv_ref,dl_ref,bias_ref,acc_ref,far_ref,dka_ref,dva_ref=refs
    else:
        q_ref,k_ref,v_ref,g_ref,qb_ref,kx_ref,dq_ref,dk_ref,dv_ref,dka_ref,dva_ref=refs
    lq=q_ref.shape[0]; lk=k_ref.shape[0]
    wide=lk+lq-bq
    if has_bias:
        for h in range(2):
            bias_ref[h]=skew_line(line_ref[0,h:h+1,:],bq)[:,:wide]
        acc_ref[...]=jnp.zeros_like(acc_ref)
        far_ref[...]=jnp.zeros_like(far_ref)
    first=head_mask(bq)
    keyfirst=head_mask(lk)
    k=k_ref[...]
    keys=jnp.concatenate((k,kx_ref[...]),axis=1)
    values=v_ref[...]
    heads_k=[keep(k,keyfirst,h) for h in range(2)]
    def start(n,h):
        rows=slice(n*bq,(n+1)*bq)
        qh=keep(q_ref[rows,:],first,h); gh=keep(g_ref[rows,:],first,h)
        s=dot(jnp.concatenate((qh,qb_ref[h,rows,:]),axis=1),keys,NT)
        return qh,gh,s,dot(gh,values,NT)
    tiles=[(n,h) for n in range(lq//bq) for h in range(2)]
    ahead=start(*tiles[0])
    for at,(n,h) in enumerate(tiles):
        rows=slice(n*bq,(n+1)*bq)
        qh,gh,s,dp=ahead
        if at+1<len(tiles):
            ahead=start(*tiles[at+1])
        if has_bias:
            off=lq-bq-n*bq
            s=s+bias_ref[h,:,off:off+lk]
        p=jnp.exp(s)
        inner=jnp.sum(p*dp,axis=1,keepdims=True)
        gs=(p*(dp-inner)).astype(jnp.bfloat16)
        if has_bias:
            lo,hi=max(0,n*bq-LANES),min(lk,n*bq+bq+LANES)
            spot=lo-n*bq+LANES
            acc_ref[h,:,spot:spot+hi-lo]+=gs[:,lo:hi].astype(jnp.float32)
            for side,(a,b) in enumerate(((0,lo),(hi,lk))):
                if b>a:
                    total=gs[:,a:a+LANES].astype(jnp.float32)
                    for c in range(a+LANES,b,LANES):
                        total=total+gs[:,c:c+LANES].astype(jnp.float32)
                    far_ref[h,side]+=total
        dv=dot(gh,p.astype(jnp.bfloat16),TN)
        dk=dot(qh,gs,TN)
        if at==0:
            dva_ref[...]=dv; dka_ref[...]=dk
        else:
            dva_ref[...]+=dv; dka_ref[...]+=dk
        part=dot(gs,heads_k[h])
        if h==0:
            kept=part
        else:
            dq_ref[rows,:]=(kept+part).astype(jnp.bfloat16)
    dk_ref[...]=dka_ref[...].T.astype(jnp.bfloat16)
    dv_ref[...]=dva_ref[...].T.astype(jnp.bfloat16)
    if has_bias:
        width=line_ref.shape[-1]
        lane=lax.broadcasted_iota(jnp.int32,(1,width),1)
        for h in range(2):
            band=jnp.concatenate((acc_ref[h],jnp.zeros((bq,bq),jnp.float32)),axis=1)
            sums=pltpu.roll(line_sums(band),bq,1)
            line=on_line(sums,lq-2*bq-LANES,width)
            for side,place in enumerate((0,wide-1)):
                far=jnp.sum(far_ref[h,side],axis=0,keepdims=True)
                far=jnp.sum(far,axis=1,keepdims=True)
                line=line+jnp.where(lane==place,far,0.0)
            dl_ref[0,h:h+1,:]=line

def cost_of():
    return pl.CostEstimate(flops=1,bytes_accessed=1,transcendentals=0)

def attend(q,qc,k,kc,v,vc,qx,kx,line,bq):
    lq=q.shape[0]; lk=k.shape[0]
    bq=min(bq,lq)
    has=line is not None
    blk=lambda rows,c: pl.BlockSpec((rows,LANES),lambda i,c=c:(0,c+i))
    fix=lambda rows: pl.BlockSpec((rows,LANES),lambda i:(0,0))
    ins=[blk(lq,qc),blk(lk,kc),blk(lk,vc),fix(lq),fix(lk)]
    args=[q,k,v,qx,kx]
    scratch=[]
    if has:
        ins.append(pl.BlockSpec((1,2,line.shape[-1]),lambda i:(i,0,0))); args.append(line)
        scratch=[pltpu.VMEM((2,lk+lq-bq,bq),jnp.float32)]
    return pl.pallas_call(functools.partial(fwd_kernel,bq,has),grid=(H//2,),in_specs=ins,
        out_specs=[blk(lq,0),pl.BlockSpec((2,lq,LANES),lambda i:(i,0,0))],
        out_shape=[jax.ShapeDtypeStruct((lq,H*DK),jnp.bfloat16),jax.ShapeDtypeStruct((H,lq,LANES),jnp.bfloat16)],
        scratch_shapes=scratch,compiler_params=pltpu.CompilerParams(vmem_limit_bytes=VLIM),cost_estimate=cost_of(),name="attend")(*args)

def attend_back(q,qc,k,kc,v,vc,g,qb,kx,line,bq,pairs=None):
    lq=q.shape[0]; lk=k.shape[0]
    bq=min(bq,lq)
    has=line is not None
    start,count=(0,H//2) if pairs is None else pairs
    blk=lambda rows,c: pl.BlockSpec((rows,LANES),lambda i,c=c:(0,c+start+i))
    fix=lambda rows: pl.BlockSpec((rows,LANES),lambda i:(0,0))
    ins=[blk(lq,qc),blk(lk,kc),blk(lk,vc),blk(lq,0),pl.BlockSpec((2,lq,LANES),lambda i:(start+i,0,0)),fix(lk)]
    args=[q,k,v,g,qb,kx]
    outs=[pl.BlockSpec((n,LANES),lambda i:(0,i)) for n in (lq,lk,lk)]
    shapes=[jax.ShapeDtypeStruct((n,count*LANES),jnp.bfloat16) for n in (lq,lk,lk)]
    scratch=[]
    if has:
        w=line.shape[-1]
        ins.append(pl.BlockSpec((1,2,w),lambda i:(start+i,0,0))); args.append(line)
        outs.append(pl.BlockSpec((1,2,w),lambda i:(i,0,0)))
        shapes.append(jax.ShapeDtypeStruct((count,2,w),jnp.float32))
        scratch=[pltpu.VMEM((2,bq,lk+lq-bq),jnp.float32),pltpu.VMEM((2,bq,bq+2*LANES),jnp.float32),pltpu.VMEM((2,2,bq,LANES),jnp.float32)]
    scratch=scratch+[pltpu.VMEM((LANES,lk),jnp.float32)]*2
    return pl.pallas_call(functools.partial(bwd_kernel,bq,has),grid=(count,),in_specs=ins,out_specs=outs,out_shape=shapes,
        scratch_shapes=scratch,compiler_params=pltpu.CompilerParams(vmem_limit_bytes=VLIM),cost_estimate=cost_of(),name="attend_back")(*args)

def seg_features(q_segs,k_segs):
    ids=jnp.arange(LANES,dtype=jnp.int32)[None,:]
    qx=jnp.where((ids<4)&(q_segs[:,None]!=ids),-BIG,0.0).astype(jnp.bfloat16)
    kx=jnp.where(((ids<4)&(k_segs[:,None]==ids))|((ids>=4)&(ids<7)),1.0,0.0).astype(jnp.bfloat16)
    return qx,kx


def marks(query_segs, key_segs):
    pairs = [seg_features(q, k) for q, k in zip(query_segs, key_segs)]
    return [p[0] for p in pairs], [p[1] for p in pairs]


def row_of(array, row, rows):
    length = array.shape[0] // rows
    return array[row * length : (row + 1) * length]


def join(parts):
    return parts[0] if len(parts) == 1 else jnp.concatenate(parts, axis=0)


def attend_rows(rows, queries, q_col, pairs, k_col, v_col, query_marks, key_marks, line):
    outs, kept = [], []
    for r in range(rows):
        q, kv = row_of(queries, r, rows), row_of(pairs, r, rows)
        out, mark = attend(
            q, q_col, kv, k_col, kv, v_col, query_marks[r], key_marks[r], line, BQ
        )
        outs.append(out)
        kept.append(mark)
    return join(outs), kept


def attend_rows_back(
    rows, queries, q_col, pairs, k_col, v_col, grads, kept, key_marks, line, part=None
):
    results = []
    for r in range(rows):
        q, kv = row_of(queries, r, rows), row_of(pairs, r, rows)
        grad = row_of(grads, r, rows)
        results.append(
            attend_back(
                q, q_col, kv, k_col, kv, v_col, grad, kept[r], key_marks[r], line, BQ, part
            )
        )
    gq, gk, gv = (join([res[i] for res in results]) for i in range(3))
    return gq, gk, gv, None if line is None else sum(res[3] for res in results)


def turn_rows(array):
    return lax.all_to_all(array, "seq", split_axis=0, concat_axis=0, tiled=True)


def bits_of(axis_name):
    return lax.axis_size(axis_name).bit_length() - 1


def swap(array, axis_name, bit):
    pairs = [(i, i ^ (1 << bit)) for i in range(lax.axis_size(axis_name))]
    return lax.ppermute(array, axis_name, pairs)


def halve(array, axis_name, bit, dim):
    mine = (lax.axis_index(axis_name) >> bit) & 1
    kept = lax.dynamic_slice_in_dim(array, mine, 1, dim)
    return kept, lax.dynamic_slice_in_dim(array, 1 - mine, 1, dim)


def add(kept, got):
    return kept.astype(jnp.float32) + got.astype(jnp.float32)


def add_low(kept, got):
    return add(kept, got).astype(jnp.bfloat16)


def grads_kernel(plan, stills, ranks, shares, core_ref, *refs):
    o_count = 1 + max(p[3] for p in plan)
    l_count = 1 + max(p[0] for p in plan)
    a_refs, g_refs = refs[:l_count], refs[l_count : l_count + len(plan)]
    o_refs = refs[l_count + len(plan) : l_count + len(plan) + 2 * o_count]
    t_refs = refs[l_count + len(plan) + 2 * o_count :]
    step = pl.program_id(0)
    core = core_ref[0]
    turned = set()
    for index, (at, first, steps, out, block) in enumerate(plan):
        if at in stills and at not in turned:
            turned.add(at)

            @pl.when(step == first)
            def turn(at=at):
                t_refs[stills.index(at)][...] = a_refs[at][...].T

        for mine in range(2):

            @pl.when((step >= first) & (step < first + steps) & (core == mine))
            def work(index=index, at=at, out=out, block=block, mine=mine):
                left, right = a_refs[at], g_refs[index]
                height, columns = left.shape[1], right.shape[1]
                tiles, group = block // 8, shares * block
                if at in stills:
                    turned_left = t_refs[stills.index(at)][...]
                else:
                    turned_left = left[...].T
                for col in range(0, columns, 256):
                    result = dot(turned_left, right[:, col : col + 256])
                    for place in range(height // group):
                        target = o_refs[2 * out + (0 if place % 2 == mine else 1)]
                        home = place // 2 * shares
                        piece = paired(result[place * group : (place + 1) * group], shares, tiles)
                        spot = col // 256 * tiles
                        target[home : home + shares, spot : spot + tiles] = piece


def whole_kernel(plan, stills, ranks, shares, *refs):
    l_count = 1 + max(p[0] for p in plan)
    a_refs, g_refs = refs[:l_count], refs[l_count : l_count + len(plan)]
    target = refs[l_count + len(plan)]
    t_refs = refs[l_count + len(plan) + 1 :]
    step = pl.program_id(0)
    turned = set()
    for index, (at, first, steps, start, block) in enumerate(plan):
        if at in stills and at not in turned:
            turned.add(at)

            @pl.when(step == first)
            def turn(at=at):
                t_refs[stills.index(at)][...] = a_refs[at][...].T

        @pl.when((step >= first) & (step < first + steps))
        def work(index=index, at=at, start=start, first=first, block=block):
            left, right = a_refs[at], g_refs[index]
            height, columns = left.shape[1], right.shape[1]
            tiles, group = block // 8, shares * block
            if at in stills:
                turned_left = t_refs[stills.index(at)][...]
                home, spot = 0, start + (step - first) * (columns // 256 * tiles)
            else:
                turned_left = left[...].T
                home, spot = (step - first) * (height // block), start
            for col in range(0, columns, 256):
                result = dot(turned_left, right[:, col : col + 256])
                for place in range(height // group):
                    piece = paired(result[place * group : (place + 1) * group], shares, tiles)
                    target[
                        pl.ds(home + place * shares, shares), pl.ds(spot + col // 256 * tiles, tiles)
                    ] = piece


def paired(piece, shares, tiles):
    halves = [
        piece[:, side * LANES : (side + 1) * LANES].reshape(shares, tiles, 8, LANES)
        for side in range(2)
    ]
    return jnp.concatenate(halves, axis=2).astype(jnp.bfloat16)


def tile_columns(shapes):
    columns = {}
    for height, width in shapes:
        columns[height] = math.gcd(columns.get(height, 768), width)
    return columns


def packed_grads(items, split=True):
    ranks = lax.axis_size("batch") * lax.axis_size("seq")
    shares = lax.axis_size("seq")
    shapes_in = [(left.shape[1], right.shape[1]) for left, right in items]
    widths = tile_columns(shapes_in)
    least = min([768] + [height for height, width in shapes_in])
    outs, plan, totals, firsts, stills = [], [], [], [], []
    lefts, left_specs, right_specs = [], [], []
    step = 0
    for left, right in items:
        height, width = left.shape[1], right.shape[1]
        if height not in outs:
            outs.append(height)
            totals.append(0)
            firsts.append(step)
        out = outs.index(height)
        tall = height > least
        steps = height // least if tall else width // widths[height]
        at = lambda i, c, first=step, last=steps - 1: (0, jnp.clip(i - first, 0, last))
        still = lambda i, c: (0, 0)
        same = [i for i in stills if lefts[i] is left]
        if same and not tall:
            where = same[0]
        else:
            where = len(lefts)
            lefts.append(left)
            left_specs.append(pl.BlockSpec((left.shape[0], least), at if tall else still))
            if not tall:
                stills.append(where)
        right_specs.append(pl.BlockSpec((right.shape[0], widths[height]), still if tall else at))
        plan.append((where, step, steps, out, height // ranks))
        totals[out] += steps
        step += steps
    shapes, specs = [], []
    for out, height in enumerate(outs):
        size = (height // ranks // 8) * (widths[height] // 256)
        tall = height > least
        count = 1 if tall else totals[out]
        parts = totals[out] if tall else 1
        for side in range(2):
            shapes.append(
                jax.ShapeDtypeStruct((ranks // 2, size * count, 16, LANES), jnp.bfloat16)
            )
            at = lambda i, c, first=firsts[out], last=totals[out] - 1, tall=tall: (
                (jnp.clip(i - first, 0, last), 0, 0, 0)
                if tall
                else (0, jnp.clip(i - first, 0, last), 0, 0)
            )
            specs.append(pl.BlockSpec((ranks // 2 // parts, size, 16, LANES), at))
    cost = cost_of()
    turned = [pltpu.VMEM((lefts[i].shape[1], lefts[i].shape[0]), jnp.bfloat16) for i in stills]
    if not split:
        whole_plan, tiles = [], 0
        for out in range(len(outs)):
            for where, first, steps, item_out, block in plan:
                if item_out == out:
                    whole_plan.append((where, first, steps, tiles, block))
                    height, width = shapes_in[len(whole_plan) - 1]
                    tiles += block // 8 * (width // 256)
        drop = lambda at: lambda i: at(i, None)
        return pl.pallas_call(
            functools.partial(whole_kernel, whole_plan, stills, ranks, shares),
            grid=(step,),
            in_specs=[
                pl.BlockSpec(x.block_shape, drop(x.index_map)) for x in left_specs + right_specs
            ],
            out_specs=pl.BlockSpec((ranks, tiles, 16, LANES), lambda i: (0, 0, 0, 0)),
            out_shape=jax.ShapeDtypeStruct((ranks, tiles, 16, LANES), jnp.bfloat16),
            scratch_shapes=turned,
            compiler_params=pltpu.CompilerParams(vmem_limit_bytes=VLIM),
            cost_estimate=cost,
            name="whole_grads",
        )(*lefts, *[right for left, right in items])
    core = (lax.axis_index("batch") & 1).astype(jnp.int32).reshape(1)
    results = pl.pallas_call(
        functools.partial(grads_kernel, plan, stills, ranks, shares),
        grid_spec=pltpu.PrefetchScalarGridSpec(
            num_scalar_prefetch=1,
            grid=(step,),
            in_specs=left_specs + right_specs,
            out_specs=specs,
            scratch_shapes=turned,
        ),
        out_shape=shapes,
        compiler_params=pltpu.CompilerParams(vmem_limit_bytes=VLIM),
        cost_estimate=cost,
        name="packed_grads",
    )(core, *lefts, *[right for left, right in items])
    return results[0::2], results[1::2]


def after(value, *others):
    return lax.optimization_barrier((value,) + others)[0]


class Small:
    def __init__(self, values):
        self.sent, self.got, self.kept = [values], [], values
        self.stages = [("batch", bit) for bit in range(bits_of("batch"))] + [("seq", -1)]

    def launch(self, sent):
        name, bit = self.stages.pop(0)
        if bit >= 0:
            self.got = [swap(sent[0], name, bit)]
            return
        size = lax.axis_size(name)
        self.got = [
            lax.ppermute(sent[0], name, [(i, i ^ step) for i in range(size)])
            for step in range(1, size)
        ]

    def advance(self, got):
        terms = [self.kept] + got
        while len(terms) > 1:
            terms = [terms[i] + terms[i + 1] for i in range(0, len(terms), 2)]
        self.kept = terms[0]
        self.got = []
        self.sent = [self.kept] if self.stages else []

    def finish(self):
        while self.got:
            self.advance(self.got)
            if self.sent:
                self.launch(self.sent)
        return self.kept


class Flow:
    def __init__(self, items, split=True, seq_first=False):
        self.split, self.seq_first = split, seq_first
        self.shapes = [(left.shape[1], right.shape[1]) for left, right in items]
        self.high, self.low = bits_of("batch"), bits_of("seq")
        self.ranks = 1 << (self.high + self.low)
        self.plain = min(shape[0] for shape in self.shapes) % (8 * self.ranks) != 0
        self.got, self.stage = [], 0
        if self.plain:
            self.sent = []
            self.whole = [weight_grad(left, right) for left, right in items]
            return
        heights = []
        for shape in self.shapes:
            if shape[0] not in heights:
                heights.append(shape[0])
        self.order = [
            [i for i, shape in enumerate(self.shapes) if shape[0] == height] for height in heights
        ]
        if split:
            self.kept, self.sent = packed_grads(items)
        else:
            self.sent = [packed_grads(items, False)]
        ups = [("batch", bit) for bit in range(1, self.high)]
        alongs = [("seq", bit) for bit in range(self.low)]
        if seq_first:
            self.steps = [[step] for step in alongs + ups]
        else:
            self.steps = [list(pair) for pair in zip(ups, ups[::-1])] + [[x] for x in alongs]

    def launch(self, sent):
        if self.plain:
            return
        if not self.split:
            axis_name = ("batch", "seq")[self.stage]
            self.got = [lax.psum_scatter(sent[0], axis_name, scatter_dimension=0, tiled=True)]
        elif self.stage == 0:
            self.got = [swap(x, "batch", 0) for x in sent]
        else:
            steps = self.steps[self.stage - 1]
            self.got = [swap(x, name, bit) for x, (name, bit) in zip(sent, steps)]
        self.stage += 1

    def advance(self, got):
        last = self.high - 1
        dim = last + self.low
        if not self.split:
            self.got, self.sent = [], got if self.stage == 1 else []
            self.result = got[0].astype(jnp.float32)
            return
        if self.stage > len(self.steps):
            self.result = add(self.kept[0], got[0])
            self.got, self.sent = [], []
            return
        sums = [add_low(k, g) for k, g in zip(self.kept, got)]
        if self.stage == 1:
            sums = [x.reshape((2,) * dim + x.shape[1:]) for x in sums]
        steps = self.steps[self.stage - 1]
        if len(sums) > len(steps):
            sums = [jnp.concatenate(sums, axis=dim)]
        elif len(sums) < len(steps):
            size = sums[0].shape[dim]
            sums = [
                lax.slice_in_dim(sums[0], 0, size // 2, axis=dim),
                lax.slice_in_dim(sums[0], size // 2, size, axis=dim),
            ]
        halves = [
            halve(x, name, bit, (last if name == "batch" else dim - 1) - bit)
            for x, (name, bit) in zip(sums, steps)
        ]
        self.kept = [h[0] for h in halves]
        self.sent = [h[1] for h in halves]

    def finish(self):
        if not self.plain and not self.split:
            while self.got:
                self.advance(self.got)
                if self.sent:
                    self.launch(self.sent)
        if self.plain:
            results = []
            for grad in self.whole:
                grad = lax.psum_scatter(
                    grad.astype(jnp.bfloat16), ("batch", "seq"), scatter_dimension=0, tiled=True
                )
                results.append(grad.astype(jnp.float32))
            return results
        while self.got:
            self.advance(self.got)
            if self.sent:
                self.launch(self.sent)
        part = self.result.reshape(-1, 16, LANES)
        results, start = [None] * len(self.shapes), 0
        for indices in self.order:
            for i in indices:
                height, width = self.shapes[i]
                tiles = height // self.ranks // 8
                count = tiles * width // 256
                piece = part[start : start + count]
                start += count
                piece = piece.reshape(width // 256, tiles, 2, 8, LANES)
                piece = jnp.transpose(piece, (1, 3, 0, 2, 4))
                results[i] = piece.reshape(tiles * 8, width)
        return results


def tick(value, *flows, fresh=()):
    live = [flow for flow in flows if flow is not None and flow.got]
    gots = [flow.got for flow in live]
    sents = [list(flow.sent) for flow in fresh]
    value, gots, sents = lax.optimization_barrier((value, gots, sents))
    for flow, sent in zip(fresh, sents):
        flow.launch(sent)
    for flow, got in zip(live, gots):
        flow.advance(got)
    value, sents = lax.optimization_barrier((value, [list(flow.sent) for flow in live]))
    for flow, sent in zip(live, sents):
        if sent:
            flow.launch(sent)
    return value


def body(
    enc_in,
    dec_in,
    out_grad,
    enc_segs,
    dec_segs,
    enc_qkv,
    enc_proj,
    enc_wi,
    enc_wo,
    enc_rel,
    enc_gains,
    dec_qkv,
    dec_proj,
    dec_rel,
    cross_q,
    cross_kv,
    cross_proj,
    dec_wi,
    dec_wo,
    dec_gains,
):
    shares = lax.axis_size("seq")
    rows = enc_in.shape[0] // shares
    full_len = enc_segs.shape[1]
    target_len = dec_in.shape[1]
    width = enc_in.shape[2]
    low = jnp.bfloat16
    row_segs = lax.dynamic_slice_in_dim(enc_segs, lax.axis_index("seq") * rows, rows, 0)

    local_len = enc_in.shape[1]
    enc_row = turn_rows(enc_in.reshape(shares, rows, local_len, width))
    enc_values = jnp.swapaxes(enc_row, 0, 1).reshape(-1, width).astype(jnp.float32)
    dec_values = dec_in.reshape(-1, width).astype(jnp.float32)

    offsets = line_offsets(full_len, full_len)
    turned = turned_offsets(full_len, full_len)
    enc_select = enc_selector(offsets)
    enc_line = bias_line(enc_rel, enc_select)
    enc_turned = bias_line(enc_rel, enc_selector(turned))
    offsets = line_offsets(target_len, target_len)
    turned = turned_offsets(target_len, target_len)
    dec_select = dec_selector(offsets)
    dec_line = bias_line(dec_rel, dec_select)
    dec_line = jnp.where(jnp.asarray(offsets > 0), -BIG, dec_line)
    dec_turned = bias_line(dec_rel, dec_selector(turned))
    dec_turned = jnp.where(jnp.asarray(turned > 0), -BIG, dec_turned)
    enc_query_marks, enc_key_marks = marks(row_segs, row_segs)
    dec_query_marks, dec_key_marks = marks(dec_segs, dec_segs)

    dec_normed_one, dec_inverse_one = norm_fwd(dec_values, dec_gains[0])
    dec_normed_one = dec_normed_one.astype(low)
    dec_packed = row_dot(dec_normed_one, dec_qkv).astype(low)
    self_mixed, self_marks = attend_rows(
        rows, dec_packed, 0, dec_packed, 6, 12, dec_query_marks, dec_key_marks, dec_turned
    )
    dec_first = dec_values + row_dot(self_mixed, dec_proj)
    dec_normed_two, dec_inverse_two = norm_fwd(dec_first, dec_gains[1])
    dec_normed_two = dec_normed_two.astype(low)
    cross_query = row_dot(dec_normed_two, cross_q).astype(low)

    normed_one, inverse_one = norm_fwd(enc_values, enc_gains[0])
    normed_one = normed_one.astype(low)
    packed = row_dot(normed_one, enc_qkv).astype(low)
    enc_mixed, enc_marks = attend_rows(
        rows, packed, 0, packed, 6, 12, enc_query_marks, enc_key_marks, enc_turned
    )
    after_attn = enc_values + row_dot(enc_mixed, enc_proj)
    normed_two, inverse_two = norm_fwd(after_attn, enc_gains[1])
    normed_two = normed_two.astype(low)
    enc_hidden, enc_slope = gelu_pair(row_dot(normed_two, enc_wi))
    second = after_attn + row_dot(enc_hidden, enc_wo)
    encoded, inverse_three = norm_fwd(second, enc_gains[2])
    encoded = encoded.astype(low)
    cross_pack = row_dot(encoded, cross_kv).astype(low)

    cross_mixed, cross_marks = attend_rows(
        rows, cross_query, 0, cross_pack, 0, 6, dec_query_marks, enc_key_marks, None
    )
    dec_second = dec_first + row_dot(cross_mixed, cross_proj)
    dec_normed_three, dec_inverse_three = norm_fwd(dec_second, dec_gains[2])
    dec_normed_three = dec_normed_three.astype(low)
    dec_hidden, dec_slope = gelu_pair(row_dot(dec_normed_three, dec_wi))
    dec_result = (dec_second + row_dot(dec_hidden, dec_wo)).astype(low)

    upstream = out_grad.reshape(-1, width)
    grad_pre = (back_dot(upstream, dec_wo) * dec_slope.astype(jnp.float32)).astype(low)
    flow_one = Flow(((dec_hidden, upstream), (dec_normed_three, grad_pre)), False)
    grad_pre, dec_result = tick((grad_pre, dec_result), fresh=(flow_one,))
    grad_input, gain_dec_three = norm_back(
        dec_second, dec_inverse_three, dec_gains[2], back_dot(grad_pre, dec_wi)
    )
    grad_second = upstream.astype(jnp.float32) + grad_input
    grad_cross_branch = grad_second.astype(low)
    grad_mixed = back_dot(grad_cross_branch, cross_proj).astype(low)
    grad_cq, grad_ck, grad_cv, unused = attend_rows_back(
        rows, cross_query, 0, cross_pack, 0, 6, grad_mixed, cross_marks, enc_key_marks, None
    )
    grad_input, gain_dec_two = norm_back(
        dec_first, dec_inverse_two, dec_gains[1], back_dot(grad_cq, cross_q)
    )
    grad_first = grad_second + grad_input
    grad_self_branch = grad_first.astype(low)
    grad_mixed = back_dot(grad_self_branch, dec_proj).astype(low)
    grad_sq, grad_sk, grad_sv, dec_line_grad = attend_rows_back(
        rows, dec_packed, 0, dec_packed, 6, 12, grad_mixed, self_marks, dec_key_marks, dec_line
    )
    flow_two = Flow(
        (
            (dec_normed_one, grad_sq),
            (dec_normed_one, grad_sk),
            (dec_normed_one, grad_sv),
            (self_mixed, grad_self_branch),
            (dec_normed_two, grad_cq),
            (cross_mixed, grad_cross_branch),
            (encoded, grad_ck),
            (encoded, grad_cv),
        ),
        False,
    )
    (grad_sq, grad_ck, dec_line_grad, gain_dec_three, gain_dec_two) = tick(
        (grad_sq, grad_ck, dec_line_grad, gain_dec_three, gain_dec_two), fresh=(flow_two,)
    )
    rel_grad_dec = rel_grad(dec_line_grad, dec_select)

    grad_enc_second, gain_enc_three = norm_back(
        second,
        inverse_three,
        enc_gains[2],
        back_dot(grad_ck, cross_kv[:, :width]) + back_dot(grad_cv, cross_kv[:, width:]),
    )
    grad_branch = grad_enc_second.astype(low)
    grad_branch, rel_grad_dec, gain_enc_three = tick((grad_branch, rel_grad_dec, gain_enc_three))
    flow_three = Flow(((enc_hidden, grad_branch),), seq_first=True)
    grad_branch = tick(grad_branch, fresh=(flow_three,))
    grad_pre = slope_back(grad_branch, enc_wo, enc_slope)
    grad_pre = tick(grad_pre, flow_one, flow_three)
    grad_input, gain_enc_two = norm_back(
        after_attn, inverse_two, enc_gains[1], back_dot(grad_pre, enc_wi)
    )
    grad_enc_first = grad_enc_second + grad_input
    grad_branch = grad_enc_first.astype(low)
    flow_four = Flow(((normed_two, grad_pre), (enc_mixed, grad_branch)))
    grad_branch, gain_enc_two = tick((grad_branch, gain_enc_two), fresh=(flow_four,))
    grad_mixed = back_dot(grad_branch, enc_proj).astype(low)
    grad_mixed = tick(grad_mixed, flow_four)
    pieces, line_grads, through = [], [], None
    flows = {0: (flow_three, flow_four), 2: (flow_two, flow_four), 4: ()}
    for part in ((0, 2), (2, 2), (4, 2)):
        grad_eq, grad_ek, grad_ev, line_grad = attend_rows_back(
            rows,
            packed,
            0,
            packed,
            6,
            12,
            grad_mixed,
            enc_marks,
            enc_key_marks,
            enc_line,
            part,
        )
        grad_eq, grad_ek, grad_ev, line_grad, grad_mixed = tick(
            (grad_eq, grad_ek, grad_ev, line_grad, grad_mixed), *flows[part[0]]
        )
        line_grads.append(line_grad)
        pieces.append((grad_eq, grad_ek, grad_ev))
        if part[0] == 4:
            flow_five = Flow([(normed_one, piece[at]) for at in range(3) for piece in pieces])
            pieces = tick(pieces, fresh=(flow_five,))
            grad_eq, grad_ek, grad_ev = pieces[-1]
        for at, piece in enumerate((grad_eq, grad_ek, grad_ev)):
            start = at * width + part[0] * LANES
            term = back_dot(piece, enc_qkv[:, start : start + part[1] * LANES])
            through = term if through is None else through + term
        grad_mixed = after(grad_mixed, through)
    grad_input, gain_enc_one = norm_back(enc_values, inverse_one, enc_gains[0], through)
    enc_grad_row = (grad_enc_first + grad_input).astype(low)
    enc_grad_turned = enc_grad_row.reshape(rows, shares, local_len, width)
    enc_grad = turn_rows(jnp.swapaxes(enc_grad_turned, 0, 1)).reshape(enc_in.shape)

    grad_sq = after(grad_sq, enc_grad_row)
    grad_sq = tick(grad_sq, flow_one, flow_two, flow_three, flow_four, flow_five)
    grad_input, gain_dec_one = norm_back(
        dec_values,
        dec_inverse_one,
        dec_gains[0],
        back_dot(grad_sq, dec_qkv[:, :width])
        + back_dot(grad_sk, dec_qkv[:, width : 2 * width])
        + back_dot(grad_sv, dec_qkv[:, 2 * width :]),
    )
    dec_in_grad = grad_first + grad_input
    enc_line_grad = jnp.concatenate(line_grads, axis=0)
    rels = jnp.concatenate((rel_grad(enc_line_grad, enc_select), rel_grad_dec), axis=0)
    gains = (
        (gain_enc_one, gain_enc_two, gain_enc_three) + (gain_dec_one, gain_dec_two, gain_dec_three)
    )
    small = Small(jnp.concatenate((jnp.stack(gains), rels.reshape(1, -1)), axis=0))
    dec_in_grad, dec_result = tick((dec_in_grad, dec_result), flow_five, fresh=(small,))
    dec_result = tick(dec_result, flow_three, flow_five, small)
    dec_result = tick(dec_result, flow_three, flow_five, small)
    dec_result = tick(dec_result, small)
    dec_result, enc_grad = lax.optimization_barrier((dec_result, enc_grad))
    for unused in range(3):
        dec_result = tick(dec_result, flow_three, flow_four, flow_five, small)
    small = small.finish()
    gains_enc_total, gains_dec_total = small[:3], small[3:6]
    rels = small[6].reshape(2, NB, H)
    rel_enc_total, rel_dec_total = rels[0], rels[1]
    grad_dec_wo, grad_dec_wi = flow_one.finish()
    two = flow_two.finish()
    dec_q, dec_k, dec_v, grad_dec_proj, grad_cross_q, grad_cross_proj, cross_k, cross_v = two
    (grad_enc_wo,) = flow_three.finish()
    grad_enc_wi, grad_enc_proj = flow_four.finish()
    grad_enc_qkv = jnp.concatenate(flow_five.finish(), axis=1)
    return (
        dec_result.reshape(dec_in.shape),
        enc_grad.astype(jnp.float32),
        dec_in_grad.reshape(dec_in.shape),
        grad_enc_qkv,
        grad_enc_proj,
        grad_enc_wi,
        grad_enc_wo,
        rel_enc_total,
        gains_enc_total,
        jnp.concatenate((dec_q, dec_k, dec_v), axis=1),
        grad_dec_proj,
        rel_dec_total,
        grad_cross_q,
        jnp.concatenate((cross_k, cross_v), axis=1),
        grad_cross_proj,
        grad_dec_wi,
        grad_dec_wo,
        gains_dec_total,
    )


def solution(mesh):
    in_specs = (
        P("batch", "seq", None),
        P(("batch", "seq"), None, None),
        P(("batch", "seq"), None, None),
        P("batch", None),
        P(("batch", "seq"), None),
        P(),
        P(),
        P(),
        P(),
        P(),
        P(),
        P(),
        P(),
        P(),
        P(),
        P(),
        P(),
        P(),
        P(),
        P(),
    )
    out_specs = (
        P(("batch", "seq"), None, None),
        P("batch", "seq", None),
        P(("batch", "seq"), None, None),
        P(("batch", "seq"), None),
        P(("batch", "seq"), None),
        P(("batch", "seq"), None),
        P(("batch", "seq"), None),
        P(),
        P(),
        P(("batch", "seq"), None),
        P(("batch", "seq"), None),
        P(),
        P(("batch", "seq"), None),
        P(("batch", "seq"), None),
        P(("batch", "seq"), None),
        P(("batch", "seq"), None),
        P(("batch", "seq"), None),
        P(),
    )
    return jax.shard_map(body, mesh=mesh, in_specs=in_specs, out_specs=out_specs, check_vma=False)
```

```python
import functools
import math

import jax
import jax.numpy as jnp
import numpy as np
from jax import lax
from jax.experimental import pallas as pl
from jax.experimental.pallas import tpu as pltpu
from jax.sharding import PartitionSpec as P

H = 12
DK = 64
NB = 32
MAXD = 128
ENC_LEN = 1024
DEC_LEN = 256
LANES = 128
BQ = 256
BIG = 1e9
VLIM = 56 * 1024 * 1024
EPS = 1e-06

def bucket_steps(classes, distance, length):
    exact_part = classes // 2
    thresholds = []
    previous = 0
    for offset in range(1, length + 1):
        if offset < exact_part:
            bucket_level = offset
        else:
            bucket_level = min(
                classes - 1,
                exact_part
                + int(
                    math.log(offset / exact_part)
                    / math.log(distance / exact_part)
                    * (classes - exact_part)
                ),
            )
        if bucket_level > previous:
            thresholds.append((offset, bucket_level - previous))
            previous = bucket_level
    return thresholds


def step_buckets(distance, steps):
    buckets = np.zeros(distance.shape, np.int32)
    for edge, size in steps:
        buckets = buckets + size * (distance >= edge)
    return buckets


def line_offsets(queries, keys):
    place = np.arange(queries + keys)
    block = min(BQ, queries)
    wrapped = np.where(place >= queries + keys - block, place - queries - keys, place)
    return wrapped - (queries - block)


def turned_offsets(queries, keys):
    block = min(BQ, queries)
    place = np.arange(2 * block)
    wrapped = np.where(place >= block, place - 2 * block, place)
    starts = np.arange(0, keys + queries - block, block) - (queries - block)
    return (starts[:, None] - wrapped[None, :]).reshape(-1)


def enc_selector(offsets):
    half = NB // 2
    buckets = half * (offsets > 0) + step_buckets(np.abs(offsets), bucket_steps(half, MAXD, ENC_LEN))
    return jnp.asarray(buckets, jnp.int32)[:, None] == jnp.arange(NB, dtype=jnp.int32)[None, :]


def dec_selector(offsets):
    buckets = step_buckets(np.maximum(-offsets, 0), bucket_steps(NB, MAXD, DEC_LEN))
    return jnp.asarray(buckets, jnp.int32)[:, None] == jnp.arange(NB, dtype=jnp.int32)[None, :]


def bias_line(rel_table, selector):
    line = jnp.einsum(
        "nb,bh->hn", selector.astype(jnp.float32), rel_table, precision=lax.Precision.HIGHEST
    )
    return line.reshape(H // 2, 2, -1)


def rel_grad(line_grad, selector):
    return jnp.einsum(
        "hn,nb->bh",
        line_grad.reshape(H, -1),
        selector.astype(jnp.float32),
        precision=lax.Precision.HIGHEST,
    )


def gelu_pair(values):
    scale = math.sqrt(2.0 / math.pi)
    square = values * values
    curve = jnp.tanh(values * (scale + scale * 0.044715 * square))
    half = 0.5 * (1.0 + curve)
    inner = scale + 3.0 * scale * 0.044715 * square
    slope = half + 0.5 * values * (1.0 - curve * curve) * inner
    return (values * half).astype(jnp.bfloat16), slope.astype(jnp.bfloat16)


def row_dot(inputs, weight):
    return jnp.einsum("...i,ij->...j", inputs, weight, preferred_element_type=jnp.float32)


def back_dot(grad_vals, weight):
    return jnp.einsum("...j,ij->...i", grad_vals, weight, preferred_element_type=jnp.float32)


def weight_grad(inputs, grad_vals):
    return jnp.einsum(
        "ti,tj->ij",
        inputs.reshape(-1, inputs.shape[-1]),
        grad_vals.reshape(-1, grad_vals.shape[-1]),
        preferred_element_type=jnp.float32,
    )


def slope_kernel(grad_ref, weight_ref, slope_ref, out_ref):
    weight = weight_ref[...]
    for at in range(0, grad_ref.shape[0], 256):
        rows = slice(at, at + 256)
        grad = dot(grad_ref[rows, :], weight, NT)
        out_ref[rows, :] = (grad * slope_ref[rows, :].astype(jnp.float32)).astype(jnp.bfloat16)


def slope_back(grad, weight, slope):
    tokens, hidden = slope.shape
    step = 768
    return pl.pallas_call(
        slope_kernel,
        grid=(hidden // step,),
        in_specs=[
            pl.BlockSpec(grad.shape, lambda i: (0, 0)),
            pl.BlockSpec((step, weight.shape[1]), lambda i: (i, 0)),
            pl.BlockSpec((tokens, step), lambda i: (0, i)),
        ],
        out_specs=pl.BlockSpec((tokens, step), lambda i: (0, i)),
        out_shape=jax.ShapeDtypeStruct(slope.shape, jnp.bfloat16),
        compiler_params=pltpu.CompilerParams(vmem_limit_bytes=VLIM),
        cost_estimate=cost_of(),
        name="slope_back",
    )(grad, weight, slope)


def norm_fwd(values, gain_vec):
    inverse = lax.rsqrt(jnp.mean(values * values, axis=-1, keepdims=True) + EPS)
    return (values * inverse * gain_vec, inverse)


def norm_back(values, inverse, gain_vec, grad_vals):
    scaled = grad_vals * gain_vec
    grad_values = inverse * scaled - values * inverse**3 * jnp.mean(
        scaled * values, axis=-1, keepdims=True
    )
    grad_gain = jnp.sum((grad_vals * values * inverse).reshape(-1, values.shape[-1]), axis=0)
    return (grad_values, grad_gain)


NN=(((1,),(0,)),((),()))
NT=(((1,),(1,)),((),()))
TN=(((0,),(0,)),((),()))
def dot(a,b,dims=NN):
    return lax.dot_general(a,b,dims,preferred_element_type=jnp.float32)

def head_mask(rows):
    lane=lax.broadcasted_iota(jnp.int32,(rows,LANES),1)
    return lane<DK

def keep(x,first,head):
    zero=jnp.zeros_like(x)
    return jnp.where(first,x,zero) if head==0 else jnp.where(first,zero,x)

def skew_line(line_row,rows):
    width=line_row.shape[-1]
    wide=jnp.broadcast_to(line_row,(rows,width))
    return pltpu.roll(wide,0,1,stride=1,stride_axis=0)

def line_sums(band):
    rows,width=band.shape
    total=band[:8]
    for g in range(1,rows//8):
        total=total+pltpu.roll(band[8*g:8*g+8],width-8*g,1)
    row=lax.broadcasted_iota(jnp.int32,(8,width),0)
    for b in range(3):
        total=jnp.where((row>>b)&1==1,pltpu.roll(total,width-(1<<b),1),total)
    return jnp.sum(total,axis=0,keepdims=True)

def on_line(values,start,width):
    size=values.shape[1]
    blank=lambda n: [jnp.zeros((1,n),jnp.float32)] if n>0 else []
    if start>=0:
        return jnp.concatenate(blank(start)+[values]+blank(width-start-size),axis=1)
    late,early=values[:,-start:],values[:,:-start]
    late=jnp.concatenate([late]+blank(width-size-start),axis=1)
    return late+jnp.concatenate(blank(width+start)+[early],axis=1)

def fwd_kernel(bq,has_bias,*refs):
    if has_bias:
        q_ref,k_ref,v_ref,qx_ref,kx_ref,line_ref,o_ref,qb_ref,bias_ref=refs
    else:
        q_ref,k_ref,v_ref,qx_ref,kx_ref,o_ref,qb_ref=refs
    lq=q_ref.shape[0]; lk=k_ref.shape[0]
    if has_bias:
        for h in range(2):
            for b in range(bias_ref.shape[1]//bq):
                source=line_ref[0,h:h+1,2*b*bq:2*(b+1)*bq]
                least=b*bq-(lq-bq)-(bq-1)
                if least>=MAXD or least+2*bq-2<=-MAXD:
                    block=jnp.broadcast_to(source[:,:bq],(bq,bq))
                else:
                    block=skew_line(source,bq)[:,:bq]
                bias_ref[h,b*bq:(b+1)*bq,:]=block
    first=head_mask(bq)
    row=lax.broadcasted_iota(jnp.int32,(LANES,bq),0)
    keys=jnp.concatenate((k_ref[...],kx_ref[...]),axis=1)
    values=v_ref[...].T
    def score(n,h):
        rows=slice(n*bq,(n+1)*bq)
        return dot(keys,jnp.concatenate((keep(q_ref[rows,:],first,h),qx_ref[rows,:]),axis=1),NT)
    tiles=[(n,h) for n in range(lq//bq) for h in range(2)]
    ahead=score(*tiles[0])
    for at,(n,h) in enumerate(tiles):
        rows=slice(n*bq,(n+1)*bq)
        s=ahead
        if at+1<len(tiles):
            ahead=score(*tiles[at+1])
        if has_bias:
            off=lq-bq-n*bq
            bias=bias_ref[h,off:off+lk,:]
            top=jnp.max(s+bias,axis=0,keepdims=True)
            e=jnp.exp((s-top)+bias)
        else:
            top=jnp.max(s,axis=0,keepdims=True)
            e=jnp.exp(s-top)
        total=jnp.sum(e,axis=0,keepdims=True)
        p=(e*(1.0/total)).astype(jnp.bfloat16)
        out=dot(values,p)
        low=-(top+jnp.log(total))
        one=low.astype(jnp.bfloat16).astype(jnp.float32)
        two=(low-one).astype(jnp.bfloat16).astype(jnp.float32)
        three=low-one-two
        x=jnp.where(row==4,one,jnp.where(row==5,two,jnp.where(row==6,three,0.0)))
        qb_ref[h,rows,:]=(x.T+qx_ref[rows,:].astype(jnp.float32)).astype(jnp.bfloat16)
        if h==0:
            kept=out
        else:
            o_ref[rows,:]=jnp.where(row<DK,kept,out).T.astype(jnp.bfloat16)

def bwd_kernel(bq,has_bias,*refs):
    if has_bias:
        q_ref,k_ref,v_ref,g_ref,qb_ref,kx_ref,line_ref,dq_ref,dk_ref,dv_ref,dl_ref,bias_ref,acc_ref,far_ref,dka_ref,dva_ref=refs
    else:
        q_ref,k_ref,v_ref,g_ref,qb_ref,kx_ref,dq_ref,dk_ref,dv_ref,dka_ref,dva_ref=refs
    lq=q_ref.shape[0]; lk=k_ref.shape[0]
    wide=lk+lq-bq
    if has_bias:
        for h in range(2):
            bias_ref[h]=skew_line(line_ref[0,h:h+1,:],bq)[:,:wide]
        acc_ref[...]=jnp.zeros_like(acc_ref)
        far_ref[...]=jnp.zeros_like(far_ref)
    first=head_mask(bq)
    keyfirst=head_mask(lk)
    k=k_ref[...]
    keys=jnp.concatenate((k,kx_ref[...]),axis=1)
    values=v_ref[...]
    heads_k=[keep(k,keyfirst,h) for h in range(2)]
    def start(n,h):
        rows=slice(n*bq,(n+1)*bq)
        qh=keep(q_ref[rows,:],first,h); gh=keep(g_ref[rows,:],first,h)
        s=dot(jnp.concatenate((qh,qb_ref[h,rows,:]),axis=1),keys,NT)
        return qh,gh,s,dot(gh,values,NT)
    both_k=jnp.concatenate(heads_k,axis=0)
    count=lq//bq
    ahead=[start(0,h) for h in range(2)]
    for n in range(count):
        rows=slice(n*bq,(n+1)*bq)
        now,ahead=ahead,[]
        probs,grads=[],[]
        for h in range(2):
            qh,gh,s,dp=now[h]
            if n+1<count:
                ahead.append(start(n+1,h))
            if has_bias:
                off=lq-bq-n*bq
                s=s+bias_ref[h,:,off:off+lk]
            p=jnp.exp(s)
            inner=jnp.sum(p*dp,axis=1,keepdims=True)
            gs=(p*(dp-inner)).astype(jnp.bfloat16)
            if has_bias:
                lo,hi=max(0,n*bq-LANES),min(lk,n*bq+bq+LANES)
                spot=lo-n*bq+LANES
                acc_ref[h,:,spot:spot+hi-lo]+=gs[:,lo:hi].astype(jnp.float32)
                for side,(a,b) in enumerate(((0,lo),(hi,lk))):
                    if b>a:
                        total=gs[:,a:a+LANES].astype(jnp.float32)
                        for c in range(a+LANES,b,LANES):
                            total=total+gs[:,c:c+LANES].astype(jnp.float32)
                        far_ref[h,side]+=total
            probs.append(p.astype(jnp.bfloat16)); grads.append(gs)
        dv=dot(jnp.concatenate((now[0][1],now[1][1]),axis=0),jnp.concatenate(probs,axis=0),TN)
        dk=dot(jnp.concatenate((now[0][0],now[1][0]),axis=0),jnp.concatenate(grads,axis=0),TN)
        if n==0:
            dva_ref[...]=dv; dka_ref[...]=dk
        else:
            dva_ref[...]+=dv; dka_ref[...]+=dk
        dq_ref[rows,:]=dot(jnp.concatenate(grads,axis=1),both_k).astype(jnp.bfloat16)
    dk_ref[...]=dka_ref[...].T.astype(jnp.bfloat16)
    dv_ref[...]=dva_ref[...].T.astype(jnp.bfloat16)
    if has_bias:
        width=line_ref.shape[-1]
        lane=lax.broadcasted_iota(jnp.int32,(1,width),1)
        for h in range(2):
            band=jnp.concatenate((acc_ref[h],jnp.zeros((bq,bq),jnp.float32)),axis=1)
            sums=pltpu.roll(line_sums(band),bq,1)
            line=on_line(sums,lq-2*bq-LANES,width)
            for side,place in enumerate((0,wide-1)):
                far=jnp.sum(far_ref[h,side],axis=0,keepdims=True)
                far=jnp.sum(far,axis=1,keepdims=True)
                line=line+jnp.where(lane==place,far,0.0)
            dl_ref[0,h:h+1,:]=line

def cost_of():
    return pl.CostEstimate(flops=1,bytes_accessed=1,transcendentals=0)

def attend(q,qc,k,kc,v,vc,qx,kx,line,bq):
    lq=q.shape[0]; lk=k.shape[0]
    bq=min(bq,lq)
    has=line is not None
    blk=lambda rows,c: pl.BlockSpec((rows,LANES),lambda i,c=c:(0,c+i))
    fix=lambda rows: pl.BlockSpec((rows,LANES),lambda i:(0,0))
    ins=[blk(lq,qc),blk(lk,kc),blk(lk,vc),fix(lq),fix(lk)]
    args=[q,k,v,qx,kx]
    scratch=[]
    if has:
        ins.append(pl.BlockSpec((1,2,line.shape[-1]),lambda i:(i,0,0))); args.append(line)
        scratch=[pltpu.VMEM((2,lk+lq-bq,bq),jnp.float32)]
    return pl.pallas_call(functools.partial(fwd_kernel,bq,has),grid=(H//2,),in_specs=ins,
        out_specs=[blk(lq,0),pl.BlockSpec((2,lq,LANES),lambda i:(i,0,0))],
        out_shape=[jax.ShapeDtypeStruct((lq,H*DK),jnp.bfloat16),jax.ShapeDtypeStruct((H,lq,LANES),jnp.bfloat16)],
        scratch_shapes=scratch,compiler_params=pltpu.CompilerParams(vmem_limit_bytes=VLIM),cost_estimate=cost_of(),name="attend")(*args)

def attend_back(q,qc,k,kc,v,vc,g,qb,kx,line,bq,pairs=None):
    lq=q.shape[0]; lk=k.shape[0]
    bq=min(bq,lq)
    has=line is not None
    start,count=(0,H//2) if pairs is None else pairs
    blk=lambda rows,c: pl.BlockSpec((rows,LANES),lambda i,c=c:(0,c+start+i))
    fix=lambda rows: pl.BlockSpec((rows,LANES),lambda i:(0,0))
    ins=[blk(lq,qc),blk(lk,kc),blk(lk,vc),blk(lq,0),pl.BlockSpec((2,lq,LANES),lambda i:(start+i,0,0)),fix(lk)]
    args=[q,k,v,g,qb,kx]
    outs=[pl.BlockSpec((n,LANES),lambda i:(0,i)) for n in (lq,lk,lk)]
    shapes=[jax.ShapeDtypeStruct((n,count*LANES),jnp.bfloat16) for n in (lq,lk,lk)]
    scratch=[]
    if has:
        w=line.shape[-1]
        ins.append(pl.BlockSpec((1,2,w),lambda i:(start+i,0,0))); args.append(line)
        outs.append(pl.BlockSpec((1,2,w),lambda i:(i,0,0)))
        shapes.append(jax.ShapeDtypeStruct((count,2,w),jnp.float32))
        scratch=[pltpu.VMEM((2,bq,lk+lq-bq),jnp.float32),pltpu.VMEM((2,bq,bq+2*LANES),jnp.float32),pltpu.VMEM((2,2,bq,LANES),jnp.float32)]
    scratch=scratch+[pltpu.VMEM((LANES,lk),jnp.float32)]*2
    return pl.pallas_call(functools.partial(bwd_kernel,bq,has),grid=(count,),in_specs=ins,out_specs=outs,out_shape=shapes,
        scratch_shapes=scratch,compiler_params=pltpu.CompilerParams(vmem_limit_bytes=VLIM),cost_estimate=cost_of(),name="attend_back")(*args)

def seg_features(q_segs,k_segs):
    ids=jnp.arange(LANES,dtype=jnp.int32)[None,:]
    qx=jnp.where((ids<4)&(q_segs[:,None]!=ids),-BIG,0.0).astype(jnp.bfloat16)
    kx=jnp.where(((ids<4)&(k_segs[:,None]==ids))|((ids>=4)&(ids<7)),1.0,0.0).astype(jnp.bfloat16)
    return qx,kx


def marks(query_segs, key_segs):
    pairs = [seg_features(q, k) for q, k in zip(query_segs, key_segs)]
    return [p[0] for p in pairs], [p[1] for p in pairs]


def row_of(array, row, rows):
    length = array.shape[0] // rows
    return array[row * length : (row + 1) * length]


def join(parts):
    return parts[0] if len(parts) == 1 else jnp.concatenate(parts, axis=0)


def attend_rows(rows, queries, q_col, pairs, k_col, v_col, query_marks, key_marks, line):
    outs, kept = [], []
    for r in range(rows):
        q, kv = row_of(queries, r, rows), row_of(pairs, r, rows)
        out, mark = attend(
            q, q_col, kv, k_col, kv, v_col, query_marks[r], key_marks[r], line, BQ
        )
        outs.append(out)
        kept.append(mark)
    return join(outs), kept


def attend_rows_back(
    rows, queries, q_col, pairs, k_col, v_col, grads, kept, key_marks, line, part=None
):
    results = []
    for r in range(rows):
        q, kv = row_of(queries, r, rows), row_of(pairs, r, rows)
        grad = row_of(grads, r, rows)
        results.append(
            attend_back(
                q, q_col, kv, k_col, kv, v_col, grad, kept[r], key_marks[r], line, BQ, part
            )
        )
    gq, gk, gv = (join([res[i] for res in results]) for i in range(3))
    return gq, gk, gv, None if line is None else sum(res[3] for res in results)


def turn_rows(array):
    return lax.all_to_all(array, "seq", split_axis=0, concat_axis=0, tiled=True)


def bits_of(axis_name):
    return lax.axis_size(axis_name).bit_length() - 1


def swap(array, axis_name, bit):
    pairs = [(i, i ^ (1 << bit)) for i in range(lax.axis_size(axis_name))]
    return lax.ppermute(array, axis_name, pairs)


def halve(array, axis_name, bit, dim):
    mine = (lax.axis_index(axis_name) >> bit) & 1
    kept = lax.dynamic_slice_in_dim(array, mine, 1, dim)
    return kept, lax.dynamic_slice_in_dim(array, 1 - mine, 1, dim)


def add(kept, got):
    return kept.astype(jnp.float32) + got.astype(jnp.float32)


def add_low(kept, got):
    return add(kept, got).astype(jnp.bfloat16)


def grads_kernel(plan, stills, ranks, shares, core_ref, *refs):
    o_count = 1 + max(p[3] for p in plan)
    l_count = 1 + max(p[0] for p in plan)
    a_refs, g_refs = refs[:l_count], refs[l_count : l_count + len(plan)]
    o_refs = refs[l_count + len(plan) : l_count + len(plan) + 2 * o_count]
    t_refs = refs[l_count + len(plan) + 2 * o_count :]
    step = pl.program_id(0)
    core = core_ref[0]
    turned = set()
    for index, (at, first, steps, out, block) in enumerate(plan):
        if at in stills and at not in turned:
            turned.add(at)

            @pl.when(step == first)
            def turn(at=at):
                t_refs[stills.index(at)][...] = a_refs[at][...].T

        for mine in range(2):

            @pl.when((step >= first) & (step < first + steps) & (core == mine))
            def work(index=index, at=at, out=out, block=block, mine=mine):
                left, right = a_refs[at], g_refs[index]
                height, columns = left.shape[1], right.shape[1]
                tiles, group = block // 8, shares * block
                if at in stills:
                    turned_left = t_refs[stills.index(at)][...]
                else:
                    turned_left = left[...].T
                for col in range(0, columns, 256):
                    result = dot(turned_left, right[:, col : col + 256])
                    for place in range(height // group):
                        target = o_refs[2 * out + (0 if place % 2 == mine else 1)]
                        home = place // 2 * shares
                        piece = paired(result[place * group : (place + 1) * group], shares, tiles)
                        spot = col // 256 * tiles
                        target[home : home + shares, spot : spot + tiles] = piece


def whole_kernel(plan, stills, ranks, shares, *refs):
    l_count = 1 + max(p[0] for p in plan)
    a_refs, g_refs = refs[:l_count], refs[l_count : l_count + len(plan)]
    target = refs[l_count + len(plan)]
    t_refs = refs[l_count + len(plan) + 1 :]
    step = pl.program_id(0)
    turned = set()
    for index, (at, first, steps, start, block) in enumerate(plan):
        if at in stills and at not in turned:
            turned.add(at)

            @pl.when(step == first)
            def turn(at=at):
                t_refs[stills.index(at)][...] = a_refs[at][...].T

        @pl.when((step >= first) & (step < first + steps))
        def work(index=index, at=at, start=start, first=first, block=block):
            left, right = a_refs[at], g_refs[index]
            height, columns = left.shape[1], right.shape[1]
            tiles, group = block // 8, shares * block
            if at in stills:
                turned_left = t_refs[stills.index(at)][...]
                home, spot = 0, start + (step - first) * (columns // 256 * tiles)
            else:
                turned_left = left[...].T
                home, spot = (step - first) * (height // block), start
            for col in range(0, columns, 256):
                result = dot(turned_left, right[:, col : col + 256])
                for place in range(height // group):
                    piece = paired(result[place * group : (place + 1) * group], shares, tiles)
                    target[
                        pl.ds(home + place * shares, shares), pl.ds(spot + col // 256 * tiles, tiles)
                    ] = piece


def paired(piece, shares, tiles):
    halves = [
        piece[:, side * LANES : (side + 1) * LANES].reshape(shares, tiles, 8, LANES)
        for side in range(2)
    ]
    return jnp.concatenate(halves, axis=2).astype(jnp.bfloat16)


def tile_columns(shapes):
    columns = {}
    for height, width in shapes:
        columns[height] = math.gcd(columns.get(height, 768), width)
    return columns


def packed_grads(items, split=True):
    ranks = lax.axis_size("batch") * lax.axis_size("seq")
    shares = lax.axis_size("seq")
    shapes_in = [(left.shape[1], right.shape[1]) for left, right in items]
    widths = tile_columns(shapes_in)
    least = min([768] + [height for height, width in shapes_in])
    outs, plan, totals, firsts, stills = [], [], [], [], []
    lefts, left_specs, right_specs = [], [], []
    step = 0
    for left, right in items:
        height, width = left.shape[1], right.shape[1]
        if height not in outs:
            outs.append(height)
            totals.append(0)
            firsts.append(step)
        out = outs.index(height)
        tall = height > least
        steps = height // least if tall else width // widths[height]
        at = lambda i, c, first=step, last=steps - 1: (0, jnp.clip(i - first, 0, last))
        still = lambda i, c: (0, 0)
        same = [i for i in stills if lefts[i] is left]
        if same and not tall:
            where = same[0]
        else:
            where = len(lefts)
            lefts.append(left)
            left_specs.append(pl.BlockSpec((left.shape[0], least), at if tall else still))
            if not tall:
                stills.append(where)
        right_specs.append(pl.BlockSpec((right.shape[0], widths[height]), still if tall else at))
        plan.append((where, step, steps, out, height // ranks))
        totals[out] += steps
        step += steps
    shapes, specs = [], []
    for out, height in enumerate(outs):
        size = (height // ranks // 8) * (widths[height] // 256)
        tall = height > least
        count = 1 if tall else totals[out]
        parts = totals[out] if tall else 1
        for side in range(2):
            shapes.append(
                jax.ShapeDtypeStruct((ranks // 2, size * count, 16, LANES), jnp.bfloat16)
            )
            at = lambda i, c, first=firsts[out], last=totals[out] - 1, tall=tall: (
                (jnp.clip(i - first, 0, last), 0, 0, 0)
                if tall
                else (0, jnp.clip(i - first, 0, last), 0, 0)
            )
            specs.append(pl.BlockSpec((ranks // 2 // parts, size, 16, LANES), at))
    cost = cost_of()
    turned = [pltpu.VMEM((lefts[i].shape[1], lefts[i].shape[0]), jnp.bfloat16) for i in stills]
    if not split:
        whole_plan, tiles = [], 0
        for out in range(len(outs)):
            for where, first, steps, item_out, block in plan:
                if item_out == out:
                    whole_plan.append((where, first, steps, tiles, block))
                    height, width = shapes_in[len(whole_plan) - 1]
                    tiles += block // 8 * (width // 256)
        drop = lambda at: lambda i: at(i, None)
        return pl.pallas_call(
            functools.partial(whole_kernel, whole_plan, stills, ranks, shares),
            grid=(step,),
            in_specs=[
                pl.BlockSpec(x.block_shape, drop(x.index_map)) for x in left_specs + right_specs
            ],
            out_specs=pl.BlockSpec((ranks, tiles, 16, LANES), lambda i: (0, 0, 0, 0)),
            out_shape=jax.ShapeDtypeStruct((ranks, tiles, 16, LANES), jnp.bfloat16),
            scratch_shapes=turned,
            compiler_params=pltpu.CompilerParams(vmem_limit_bytes=VLIM),
            cost_estimate=cost,
            name="whole_grads",
        )(*lefts, *[right for left, right in items])
    core = (lax.axis_index("batch") & 1).astype(jnp.int32).reshape(1)
    results = pl.pallas_call(
        functools.partial(grads_kernel, plan, stills, ranks, shares),
        grid_spec=pltpu.PrefetchScalarGridSpec(
            num_scalar_prefetch=1,
            grid=(step,),
            in_specs=left_specs + right_specs,
            out_specs=specs,
            scratch_shapes=turned,
        ),
        out_shape=shapes,
        compiler_params=pltpu.CompilerParams(vmem_limit_bytes=VLIM),
        cost_estimate=cost,
        name="packed_grads",
    )(core, *lefts, *[right for left, right in items])
    return results[0::2], results[1::2]


def after(value, *others):
    return lax.optimization_barrier((value,) + others)[0]


class Small:
    def __init__(self, values):
        self.sent, self.got, self.kept = [values], [], values
        self.stages = [("batch", bit) for bit in range(bits_of("batch"))] + [("seq", -1)]

    def launch(self, sent):
        name, bit = self.stages.pop(0)
        if bit >= 0:
            self.got = [swap(sent[0], name, bit)]
            return
        size = lax.axis_size(name)
        self.got = [
            lax.ppermute(sent[0], name, [(i, i ^ step) for i in range(size)])
            for step in range(1, size)
        ]

    def advance(self, got):
        terms = [self.kept] + got
        while len(terms) > 1:
            terms = [terms[i] + terms[i + 1] for i in range(0, len(terms), 2)]
        self.kept = terms[0]
        self.got = []
        self.sent = [self.kept] if self.stages else []

    def finish(self):
        while self.got:
            self.advance(self.got)
            if self.sent:
                self.launch(self.sent)
        return self.kept


class Flow:
    def __init__(self, items, split=True, seq_first=False):
        self.split, self.seq_first = split, seq_first
        self.shapes = [(left.shape[1], right.shape[1]) for left, right in items]
        self.high, self.low = bits_of("batch"), bits_of("seq")
        self.ranks = 1 << (self.high + self.low)
        self.plain = min(shape[0] for shape in self.shapes) % (8 * self.ranks) != 0
        self.got, self.stage = [], 0
        if self.plain:
            self.sent = []
            self.whole = [weight_grad(left, right) for left, right in items]
            return
        heights = []
        for shape in self.shapes:
            if shape[0] not in heights:
                heights.append(shape[0])
        self.order = [
            [i for i, shape in enumerate(self.shapes) if shape[0] == height] for height in heights
        ]
        if split:
            self.kept, self.sent = packed_grads(items)
        else:
            self.sent = [packed_grads(items, False)]
        ups = [("batch", bit) for bit in range(1, self.high)]
        alongs = [("seq", bit) for bit in range(self.low)]
        if seq_first:
            self.steps = [[step] for step in alongs + ups]
        else:
            self.steps = [list(pair) for pair in zip(ups, ups[::-1])] + [[x] for x in alongs]

    def launch(self, sent):
        if self.plain:
            return
        if not self.split:
            axis_name = ("batch", "seq")[self.stage]
            self.got = [lax.psum_scatter(sent[0], axis_name, scatter_dimension=0, tiled=True)]
        elif self.stage == 0:
            self.got = [swap(x, "batch", 0) for x in sent]
        else:
            steps = self.steps[self.stage - 1]
            self.got = [swap(x, name, bit) for x, (name, bit) in zip(sent, steps)]
        self.stage += 1

    def advance(self, got):
        last = self.high - 1
        dim = last + self.low
        if not self.split:
            self.got, self.sent = [], got if self.stage == 1 else []
            self.result = got[0].astype(jnp.float32)
            return
        if self.stage > len(self.steps):
            self.result = add(self.kept[0], got[0])
            self.got, self.sent = [], []
            return
        sums = [add_low(k, g) for k, g in zip(self.kept, got)]
        if self.stage == 1:
            sums = [x.reshape((2,) * dim + x.shape[1:]) for x in sums]
        steps = self.steps[self.stage - 1]
        if len(sums) > len(steps):
            sums = [jnp.concatenate(sums, axis=dim)]
        elif len(sums) < len(steps):
            size = sums[0].shape[dim]
            sums = [
                lax.slice_in_dim(sums[0], 0, size // 2, axis=dim),
                lax.slice_in_dim(sums[0], size // 2, size, axis=dim),
            ]
        halves = [
            halve(x, name, bit, (last if name == "batch" else dim - 1) - bit)
            for x, (name, bit) in zip(sums, steps)
        ]
        self.kept = [h[0] for h in halves]
        self.sent = [h[1] for h in halves]

    def finish(self):
        if not self.plain and not self.split:
            while self.got:
                self.advance(self.got)
                if self.sent:
                    self.launch(self.sent)
        if self.plain:
            results = []
            for grad in self.whole:
                grad = lax.psum_scatter(
                    grad.astype(jnp.bfloat16), ("batch", "seq"), scatter_dimension=0, tiled=True
                )
                results.append(grad.astype(jnp.float32))
            return results
        while self.got:
            self.advance(self.got)
            if self.sent:
                self.launch(self.sent)
        part = self.result.reshape(-1, 16, LANES)
        results, start = [None] * len(self.shapes), 0
        for indices in self.order:
            for i in indices:
                height, width = self.shapes[i]
                tiles = height // self.ranks // 8
                count = tiles * width // 256
                piece = part[start : start + count]
                start += count
                piece = piece.reshape(width // 256, tiles, 2, 8, LANES)
                piece = jnp.transpose(piece, (1, 3, 0, 2, 4))
                results[i] = piece.reshape(tiles * 8, width)
        return results


def tick(value, *flows, fresh=()):
    live = [flow for flow in flows if flow is not None and flow.got]
    gots = [flow.got for flow in live]
    sents = [list(flow.sent) for flow in fresh]
    value, gots, sents = lax.optimization_barrier((value, gots, sents))
    for flow, sent in zip(fresh, sents):
        flow.launch(sent)
    for flow, got in zip(live, gots):
        flow.advance(got)
    value, sents = lax.optimization_barrier((value, [list(flow.sent) for flow in live]))
    for flow, sent in zip(live, sents):
        if sent:
            flow.launch(sent)
    return value


def body(
    enc_in,
    dec_in,
    out_grad,
    enc_segs,
    dec_segs,
    enc_qkv,
    enc_proj,
    enc_wi,
    enc_wo,
    enc_rel,
    enc_gains,
    dec_qkv,
    dec_proj,
    dec_rel,
    cross_q,
    cross_kv,
    cross_proj,
    dec_wi,
    dec_wo,
    dec_gains,
):
    shares = lax.axis_size("seq")
    rows = enc_in.shape[0] // shares
    full_len = enc_segs.shape[1]
    target_len = dec_in.shape[1]
    width = enc_in.shape[2]
    low = jnp.bfloat16
    row_segs = lax.dynamic_slice_in_dim(enc_segs, lax.axis_index("seq") * rows, rows, 0)

    local_len = enc_in.shape[1]
    enc_row = turn_rows(enc_in.reshape(shares, rows, local_len, width))
    enc_values = jnp.swapaxes(enc_row, 0, 1).reshape(-1, width).astype(jnp.float32)
    dec_values = dec_in.reshape(-1, width).astype(jnp.float32)

    offsets = line_offsets(full_len, full_len)
    turned = turned_offsets(full_len, full_len)
    enc_select = enc_selector(offsets)
    enc_line = bias_line(enc_rel, enc_select)
    enc_turned = bias_line(enc_rel, enc_selector(turned))
    offsets = line_offsets(target_len, target_len)
    turned = turned_offsets(target_len, target_len)
    dec_select = dec_selector(offsets)
    dec_line = bias_line(dec_rel, dec_select)
    dec_line = jnp.where(jnp.asarray(offsets > 0), -BIG, dec_line)
    dec_turned = bias_line(dec_rel, dec_selector(turned))
    dec_turned = jnp.where(jnp.asarray(turned > 0), -BIG, dec_turned)
    enc_query_marks, enc_key_marks = marks(row_segs, row_segs)
    dec_query_marks, dec_key_marks = marks(dec_segs, dec_segs)

    dec_normed_one, dec_inverse_one = norm_fwd(dec_values, dec_gains[0])
    dec_normed_one = dec_normed_one.astype(low)
    dec_packed = row_dot(dec_normed_one, dec_qkv).astype(low)
    self_mixed, self_marks = attend_rows(
        rows, dec_packed, 0, dec_packed, 6, 12, dec_query_marks, dec_key_marks, dec_turned
    )
    dec_first = dec_values + row_dot(self_mixed, dec_proj)
    dec_normed_two, dec_inverse_two = norm_fwd(dec_first, dec_gains[1])
    dec_normed_two = dec_normed_two.astype(low)
    cross_query = row_dot(dec_normed_two, cross_q).astype(low)

    normed_one, inverse_one = norm_fwd(enc_values, enc_gains[0])
    normed_one = normed_one.astype(low)
    packed = row_dot(normed_one, enc_qkv).astype(low)
    enc_mixed, enc_marks = attend_rows(
        rows, packed, 0, packed, 6, 12, enc_query_marks, enc_key_marks, enc_turned
    )
    after_attn = enc_values + row_dot(enc_mixed, enc_proj)
    normed_two, inverse_two = norm_fwd(after_attn, enc_gains[1])
    normed_two = normed_two.astype(low)
    enc_hidden, enc_slope = gelu_pair(row_dot(normed_two, enc_wi))
    second = after_attn + row_dot(enc_hidden, enc_wo)
    encoded, inverse_three = norm_fwd(second, enc_gains[2])
    encoded = encoded.astype(low)
    cross_pack = row_dot(encoded, cross_kv).astype(low)

    cross_mixed, cross_marks = attend_rows(
        rows, cross_query, 0, cross_pack, 0, 6, dec_query_marks, enc_key_marks, None
    )
    dec_second = dec_first + row_dot(cross_mixed, cross_proj)
    dec_normed_three, dec_inverse_three = norm_fwd(dec_second, dec_gains[2])
    dec_normed_three = dec_normed_three.astype(low)
    dec_hidden, dec_slope = gelu_pair(row_dot(dec_normed_three, dec_wi))
    dec_result = (dec_second + row_dot(dec_hidden, dec_wo)).astype(low)

    upstream = out_grad.reshape(-1, width)
    grad_pre = (back_dot(upstream, dec_wo) * dec_slope.astype(jnp.float32)).astype(low)
    flow_one = Flow(((dec_hidden, upstream), (dec_normed_three, grad_pre)), False)
    grad_pre, dec_result = tick((grad_pre, dec_result), fresh=(flow_one,))
    grad_input, gain_dec_three = norm_back(
        dec_second, dec_inverse_three, dec_gains[2], back_dot(grad_pre, dec_wi)
    )
    grad_second = upstream.astype(jnp.float32) + grad_input
    grad_cross_branch = grad_second.astype(low)
    grad_mixed = back_dot(grad_cross_branch, cross_proj).astype(low)
    grad_cq, grad_ck, grad_cv, unused = attend_rows_back(
        rows, cross_query, 0, cross_pack, 0, 6, grad_mixed, cross_marks, enc_key_marks, None
    )
    grad_input, gain_dec_two = norm_back(
        dec_first, dec_inverse_two, dec_gains[1], back_dot(grad_cq, cross_q)
    )
    grad_first = grad_second + grad_input
    grad_self_branch = grad_first.astype(low)
    grad_mixed = back_dot(grad_self_branch, dec_proj).astype(low)
    grad_sq, grad_sk, grad_sv, dec_line_grad = attend_rows_back(
        rows, dec_packed, 0, dec_packed, 6, 12, grad_mixed, self_marks, dec_key_marks, dec_line
    )
    flow_two = Flow(
        (
            (dec_normed_one, grad_sq),
            (dec_normed_one, grad_sk),
            (dec_normed_one, grad_sv),
            (self_mixed, grad_self_branch),
            (dec_normed_two, grad_cq),
            (cross_mixed, grad_cross_branch),
            (encoded, grad_ck),
            (encoded, grad_cv),
        ),
        False,
    )
    (grad_sq, grad_ck, dec_line_grad, gain_dec_three, gain_dec_two) = tick(
        (grad_sq, grad_ck, dec_line_grad, gain_dec_three, gain_dec_two), fresh=(flow_two,)
    )
    rel_grad_dec = rel_grad(dec_line_grad, dec_select)

    grad_enc_second, gain_enc_three = norm_back(
        second,
        inverse_three,
        enc_gains[2],
        back_dot(grad_ck, cross_kv[:, :width]) + back_dot(grad_cv, cross_kv[:, width:]),
    )
    grad_branch = grad_enc_second.astype(low)
    grad_branch, rel_grad_dec, gain_enc_three = tick((grad_branch, rel_grad_dec, gain_enc_three))
    flow_three = Flow(((enc_hidden, grad_branch),), seq_first=True)
    grad_branch = tick(grad_branch, fresh=(flow_three,))
    grad_pre = slope_back(grad_branch, enc_wo, enc_slope)
    grad_pre = tick(grad_pre, flow_one, flow_three)
    grad_input, gain_enc_two = norm_back(
        after_attn, inverse_two, enc_gains[1], back_dot(grad_pre, enc_wi)
    )
    grad_enc_first = grad_enc_second + grad_input
    grad_branch = grad_enc_first.astype(low)
    flow_four = Flow(((normed_two, grad_pre), (enc_mixed, grad_branch)))
    grad_branch, gain_enc_two = tick((grad_branch, gain_enc_two), fresh=(flow_four,))
    grad_mixed = back_dot(grad_branch, enc_proj).astype(low)
    grad_mixed = tick(grad_mixed, flow_four)
    pieces, line_grads, through = [], [], None
    flows = {0: (flow_three, flow_four), 2: (flow_two, flow_four), 4: ()}
    for part in ((0, 2), (2, 2), (4, 2)):
        grad_eq, grad_ek, grad_ev, line_grad = attend_rows_back(
            rows,
            packed,
            0,
            packed,
            6,
            12,
            grad_mixed,
            enc_marks,
            enc_key_marks,
            enc_line,
            part,
        )
        grad_eq, grad_ek, grad_ev, line_grad, grad_mixed = tick(
            (grad_eq, grad_ek, grad_ev, line_grad, grad_mixed), *flows[part[0]]
        )
        line_grads.append(line_grad)
        pieces.append((grad_eq, grad_ek, grad_ev))
        if part[0] == 4:
            flow_five = Flow([(normed_one, piece[at]) for at in range(3) for piece in pieces])
            pieces = tick(pieces, fresh=(flow_five,))
            grad_eq, grad_ek, grad_ev = pieces[-1]
        for at, piece in enumerate((grad_eq, grad_ek, grad_ev)):
            start = at * width + part[0] * LANES
            term = back_dot(piece, enc_qkv[:, start : start + part[1] * LANES])
            through = term if through is None else through + term
        grad_mixed = after(grad_mixed, through)
    through = tick(through, flow_five)
    grad_input, gain_enc_one = norm_back(enc_values, inverse_one, enc_gains[0], through)
    enc_grad_row = (grad_enc_first + grad_input).astype(low)
    enc_grad_turned = enc_grad_row.reshape(rows, shares, local_len, width)
    enc_grad = turn_rows(jnp.swapaxes(enc_grad_turned, 0, 1)).reshape(enc_in.shape)

    grad_sq = after(grad_sq, enc_grad_row)
    grad_sq = tick(grad_sq, flow_one, flow_two, flow_three, flow_four, flow_five)
    grad_input, gain_dec_one = norm_back(
        dec_values,
        dec_inverse_one,
        dec_gains[0],
        back_dot(grad_sq, dec_qkv[:, :width])
        + back_dot(grad_sk, dec_qkv[:, width : 2 * width])
        + back_dot(grad_sv, dec_qkv[:, 2 * width :]),
    )
    dec_in_grad = grad_first + grad_input
    enc_line_grad = jnp.concatenate(line_grads, axis=0)
    rels = jnp.concatenate((rel_grad(enc_line_grad, enc_select), rel_grad_dec), axis=0)
    gains = (
        (gain_enc_one, gain_enc_two, gain_enc_three) + (gain_dec_one, gain_dec_two, gain_dec_three)
    )
    small = Small(jnp.concatenate((jnp.stack(gains), rels.reshape(1, -1)), axis=0))
    dec_in_grad, dec_result = tick((dec_in_grad, dec_result), flow_five, fresh=(small,))
    dec_result = tick(dec_result, flow_three, small)
    dec_result = tick(dec_result, flow_three, small)
    dec_result = tick(dec_result, small)
    dec_result, enc_grad = lax.optimization_barrier((dec_result, enc_grad))
    for unused in range(3):
        dec_result = tick(dec_result, flow_three, flow_four, flow_five, small)
    small = small.finish()
    gains_enc_total, gains_dec_total = small[:3], small[3:6]
    rels = small[6].reshape(2, NB, H)
    rel_enc_total, rel_dec_total = rels[0], rels[1]
    grad_dec_wo, grad_dec_wi = flow_one.finish()
    two = flow_two.finish()
    dec_q, dec_k, dec_v, grad_dec_proj, grad_cross_q, grad_cross_proj, cross_k, cross_v = two
    (grad_enc_wo,) = flow_three.finish()
    grad_enc_wi, grad_enc_proj = flow_four.finish()
    grad_enc_qkv = jnp.concatenate(flow_five.finish(), axis=1)
    return (
        dec_result.reshape(dec_in.shape),
        enc_grad.astype(jnp.float32),
        dec_in_grad.reshape(dec_in.shape),
        grad_enc_qkv,
        grad_enc_proj,
        grad_enc_wi,
        grad_enc_wo,
        rel_enc_total,
        gains_enc_total,
        jnp.concatenate((dec_q, dec_k, dec_v), axis=1),
        grad_dec_proj,
        rel_dec_total,
        grad_cross_q,
        jnp.concatenate((cross_k, cross_v), axis=1),
        grad_cross_proj,
        grad_dec_wi,
        grad_dec_wo,
        gains_dec_total,
    )


def solution(mesh):
    in_specs = (
        P("batch", "seq", None),
        P(("batch", "seq"), None, None),
        P(("batch", "seq"), None, None),
        P("batch", None),
        P(("batch", "seq"), None),
        P(),
        P(),
        P(),
        P(),
        P(),
        P(),
        P(),
        P(),
        P(),
        P(),
        P(),
        P(),
        P(),
        P(),
        P(),
    )
    out_specs = (
        P(("batch", "seq"), None, None),
        P("batch", "seq", None),
        P(("batch", "seq"), None, None),
        P(("batch", "seq"), None),
        P(("batch", "seq"), None),
        P(("batch", "seq"), None),
        P(("batch", "seq"), None),
        P(),
        P(),
        P(("batch", "seq"), None),
        P(("batch", "seq"), None),
        P(),
        P(("batch", "seq"), None),
        P(("batch", "seq"), None),
        P(("batch", "seq"), None),
        P(("batch", "seq"), None),
        P(("batch", "seq"), None),
        P(),
    )
    return jax.shard_map(body, mesh=mesh, in_specs=in_specs, out_specs=out_specs, check_vma=False)
```

```python
import functools
import math

import jax
import jax.numpy as jnp
import numpy as np
from jax import lax
from jax.experimental import pallas as pl
from jax.experimental.pallas import tpu as pltpu
from jax.sharding import PartitionSpec as P

H = 12
DK = 64
NB = 32
MAXD = 128
ENC_LEN = 1024
DEC_LEN = 256
LANES = 128
BQ = 256
BIG = 1e9
VLIM = 56 * 1024 * 1024
EPS = 1e-06

def bucket_steps(classes, distance, length):
    exact_part = classes // 2
    thresholds = []
    previous = 0
    for offset in range(1, length + 1):
        if offset < exact_part:
            bucket_level = offset
        else:
            bucket_level = min(
                classes - 1,
                exact_part
                + int(
                    math.log(offset / exact_part)
                    / math.log(distance / exact_part)
                    * (classes - exact_part)
                ),
            )
        if bucket_level > previous:
            thresholds.append((offset, bucket_level - previous))
            previous = bucket_level
    return thresholds


def step_buckets(distance, steps):
    buckets = np.zeros(distance.shape, np.int32)
    for edge, size in steps:
        buckets = buckets + size * (distance >= edge)
    return buckets


def line_offsets(queries, keys):
    place = np.arange(queries + keys)
    block = min(BQ, queries)
    wrapped = np.where(place >= queries + keys - block, place - queries - keys, place)
    return wrapped - (queries - block)


def turned_offsets(queries, keys):
    block = min(BQ, queries)
    place = np.arange(2 * block)
    wrapped = np.where(place >= block, place - 2 * block, place)
    starts = np.arange(0, keys + queries - block, block) - (queries - block)
    return (starts[:, None] - wrapped[None, :]).reshape(-1)


def enc_selector(offsets):
    half = NB // 2
    buckets = half * (offsets > 0) + step_buckets(np.abs(offsets), bucket_steps(half, MAXD, ENC_LEN))
    return jnp.asarray(buckets, jnp.int32)[:, None] == jnp.arange(NB, dtype=jnp.int32)[None, :]


def dec_selector(offsets):
    buckets = step_buckets(np.maximum(-offsets, 0), bucket_steps(NB, MAXD, DEC_LEN))
    return jnp.asarray(buckets, jnp.int32)[:, None] == jnp.arange(NB, dtype=jnp.int32)[None, :]


def bias_line(rel_table, selector):
    line = jnp.einsum(
        "nb,bh->hn", selector.astype(jnp.float32), rel_table, precision=lax.Precision.HIGHEST
    )
    return line.reshape(H // 2, 2, -1)


def rel_grad(line_grad, selector):
    return jnp.einsum(
        "hn,nb->bh",
        line_grad.reshape(H, -1),
        selector.astype(jnp.float32),
        precision=lax.Precision.HIGHEST,
    )


def gelu_pair(values):
    scale = math.sqrt(2.0 / math.pi)
    square = values * values
    curve = jnp.tanh(values * (scale + scale * 0.044715 * square))
    half = 0.5 * (1.0 + curve)
    inner = scale + 3.0 * scale * 0.044715 * square
    slope = half + 0.5 * values * (1.0 - curve * curve) * inner
    return (values * half).astype(jnp.bfloat16), slope.astype(jnp.bfloat16)


def row_dot(inputs, weight):
    return jnp.einsum("...i,ij->...j", inputs, weight, preferred_element_type=jnp.float32)


def back_dot(grad_vals, weight):
    return jnp.einsum("...j,ij->...i", grad_vals, weight, preferred_element_type=jnp.float32)


def weight_grad(inputs, grad_vals):
    return jnp.einsum(
        "ti,tj->ij",
        inputs.reshape(-1, inputs.shape[-1]),
        grad_vals.reshape(-1, grad_vals.shape[-1]),
        preferred_element_type=jnp.float32,
    )


def slope_kernel(grad_ref, weight_ref, slope_ref, out_ref):
    weight = weight_ref[...]
    for at in range(0, grad_ref.shape[0], 256):
        rows = slice(at, at + 256)
        grad = dot(grad_ref[rows, :], weight, NT)
        out_ref[rows, :] = (grad * slope_ref[rows, :].astype(jnp.float32)).astype(jnp.bfloat16)


def slope_back(grad, weight, slope):
    tokens, hidden = slope.shape
    step = 768
    return pl.pallas_call(
        slope_kernel,
        grid=(hidden // step,),
        in_specs=[
            pl.BlockSpec(grad.shape, lambda i: (0, 0)),
            pl.BlockSpec((step, weight.shape[1]), lambda i: (i, 0)),
            pl.BlockSpec((tokens, step), lambda i: (0, i)),
        ],
        out_specs=pl.BlockSpec((tokens, step), lambda i: (0, i)),
        out_shape=jax.ShapeDtypeStruct(slope.shape, jnp.bfloat16),
        compiler_params=pltpu.CompilerParams(vmem_limit_bytes=VLIM),
        cost_estimate=cost_of(),
        name="slope_back",
    )(grad, weight, slope)


def norm_fwd(values, gain_vec):
    inverse = lax.rsqrt(jnp.mean(values * values, axis=-1, keepdims=True) + EPS)
    return (values * inverse * gain_vec, inverse)


def norm_back(values, inverse, gain_vec, grad_vals):
    scaled = grad_vals * gain_vec
    grad_values = inverse * scaled - values * inverse**3 * jnp.mean(
        scaled * values, axis=-1, keepdims=True
    )
    grad_gain = jnp.sum((grad_vals * values * inverse).reshape(-1, values.shape[-1]), axis=0)
    return (grad_values, grad_gain)


NN=(((1,),(0,)),((),()))
NT=(((1,),(1,)),((),()))
TN=(((0,),(0,)),((),()))
def dot(a,b,dims=NN):
    return lax.dot_general(a,b,dims,preferred_element_type=jnp.float32)

def head_mask(rows):
    lane=lax.broadcasted_iota(jnp.int32,(rows,LANES),1)
    return lane<DK

def keep(x,first,head):
    zero=jnp.zeros_like(x)
    return jnp.where(first,x,zero) if head==0 else jnp.where(first,zero,x)

def skew_line(line_row,rows):
    width=line_row.shape[-1]
    wide=jnp.broadcast_to(line_row,(rows,width))
    return pltpu.roll(wide,0,1,stride=1,stride_axis=0)

def line_sums(band):
    rows,width=band.shape
    total=band[:8]
    for g in range(1,rows//8):
        total=total+pltpu.roll(band[8*g:8*g+8],width-8*g,1)
    row=lax.broadcasted_iota(jnp.int32,(8,width),0)
    for b in range(3):
        total=jnp.where((row>>b)&1==1,pltpu.roll(total,width-(1<<b),1),total)
    return jnp.sum(total,axis=0,keepdims=True)

def on_line(values,start,width):
    size=values.shape[1]
    blank=lambda n: [jnp.zeros((1,n),jnp.float32)] if n>0 else []
    if start>=0:
        return jnp.concatenate(blank(start)+[values]+blank(width-start-size),axis=1)
    late,early=values[:,-start:],values[:,:-start]
    late=jnp.concatenate([late]+blank(width-size-start),axis=1)
    return late+jnp.concatenate(blank(width+start)+[early],axis=1)

def fwd_kernel(bq,has_bias,*refs):
    if has_bias:
        q_ref,k_ref,v_ref,qx_ref,kx_ref,line_ref,o_ref,qb_ref,bias_ref=refs
    else:
        q_ref,k_ref,v_ref,qx_ref,kx_ref,o_ref,qb_ref=refs
    lq=q_ref.shape[0]; lk=k_ref.shape[0]
    if has_bias:
        for h in range(2):
            for b in range(bias_ref.shape[1]//bq):
                source=line_ref[0,h:h+1,2*b*bq:2*(b+1)*bq]
                least=b*bq-(lq-bq)-(bq-1)
                if least>=MAXD or least+2*bq-2<=-MAXD:
                    block=jnp.broadcast_to(source[:,:bq],(bq,bq))
                else:
                    block=skew_line(source,bq)[:,:bq]
                bias_ref[h,b*bq:(b+1)*bq,:]=block
    first=head_mask(bq)
    row=lax.broadcasted_iota(jnp.int32,(LANES,bq),0)
    keys=jnp.concatenate((k_ref[...],kx_ref[...]),axis=1)
    values=v_ref[...].T
    def score(n,h):
        rows=slice(n*bq,(n+1)*bq)
        return dot(keys,jnp.concatenate((keep(q_ref[rows,:],first,h),qx_ref[rows,:]),axis=1),NT)
    tiles=[(n,h) for n in range(lq//bq) for h in range(2)]
    ahead=score(*tiles[0])
    for at,(n,h) in enumerate(tiles):
        rows=slice(n*bq,(n+1)*bq)
        s=ahead
        if at+1<len(tiles):
            ahead=score(*tiles[at+1])
        if has_bias:
            off=lq-bq-n*bq
            bias=bias_ref[h,off:off+lk,:]
            top=jnp.max(s+bias,axis=0,keepdims=True)
            e=jnp.exp((s-top)+bias)
        else:
            top=jnp.max(s,axis=0,keepdims=True)
            e=jnp.exp(s-top)
        total=jnp.sum(e,axis=0,keepdims=True)
        p=(e*(1.0/total)).astype(jnp.bfloat16)
        out=dot(values,p)
        low=-(top+jnp.log(total))
        one=low.astype(jnp.bfloat16).astype(jnp.float32)
        two=(low-one).astype(jnp.bfloat16).astype(jnp.float32)
        three=low-one-two
        x=jnp.where(row==4,one,jnp.where(row==5,two,jnp.where(row==6,three,0.0)))
        qb_ref[h,rows,:]=(x.T+qx_ref[rows,:].astype(jnp.float32)).astype(jnp.bfloat16)
        if h==0:
            kept=out
        else:
            o_ref[rows,:]=jnp.where(row<DK,kept,out).T.astype(jnp.bfloat16)

def bwd_kernel(bq,has_bias,*refs):
    if has_bias:
        q_ref,k_ref,v_ref,g_ref,qb_ref,kx_ref,line_ref,dq_ref,dk_ref,dv_ref,dl_ref,bias_ref,acc_ref,far_ref,dka_ref,dva_ref=refs
    else:
        q_ref,k_ref,v_ref,g_ref,qb_ref,kx_ref,dq_ref,dk_ref,dv_ref,dka_ref,dva_ref=refs
    lq=q_ref.shape[0]; lk=k_ref.shape[0]
    wide=lk+lq-bq
    if has_bias:
        for h in range(2):
            bias_ref[h]=skew_line(line_ref[0,h:h+1,:],bq)[:,:wide]
        acc_ref[...]=jnp.zeros_like(acc_ref)
        far_ref[...]=jnp.zeros_like(far_ref)
    first=head_mask(bq)
    keyfirst=head_mask(lk)
    k=k_ref[...]
    keys=jnp.concatenate((k,kx_ref[...]),axis=1)
    values=v_ref[...]
    heads_k=[keep(k,keyfirst,h) for h in range(2)]
    def start(n,h):
        rows=slice(n*bq,(n+1)*bq)
        qh=keep(q_ref[rows,:],first,h); gh=keep(g_ref[rows,:],first,h)
        s=dot(jnp.concatenate((qh,qb_ref[h,rows,:]),axis=1),keys,NT)
        return qh,gh,s,dot(gh,values,NT)
    both_k=jnp.concatenate(heads_k,axis=0)
    count=lq//bq
    ahead=[start(0,h) for h in range(2)]
    for n in range(count):
        rows=slice(n*bq,(n+1)*bq)
        now,ahead=ahead,[]
        probs,grads=[],[]
        for h in range(2):
            qh,gh,s,dp=now[h]
            if n+1<count:
                ahead.append(start(n+1,h))
            if has_bias:
                off=lq-bq-n*bq
                s=s+bias_ref[h,:,off:off+lk]
            p=jnp.exp(s)
            inner=jnp.sum(p*dp,axis=1,keepdims=True)
            gs=(p*(dp-inner)).astype(jnp.bfloat16)
            if has_bias:
                lo,hi=max(0,n*bq-LANES),min(lk,n*bq+bq+LANES)
                spot=lo-n*bq+LANES
                acc_ref[h,:,spot:spot+hi-lo]+=gs[:,lo:hi].astype(jnp.float32)
                for side,(a,b) in enumerate(((0,lo),(hi,lk))):
                    if b>a:
                        total=gs[:,a:a+LANES].astype(jnp.float32)
                        for c in range(a+LANES,b,LANES):
                            total=total+gs[:,c:c+LANES].astype(jnp.float32)
                        far_ref[h,side]+=total
            probs.append(p.astype(jnp.bfloat16)); grads.append(gs)
        dv=dot(jnp.concatenate((now[0][1],now[1][1]),axis=0),jnp.concatenate(probs,axis=0),TN)
        dk=dot(jnp.concatenate((now[0][0],now[1][0]),axis=0),jnp.concatenate(grads,axis=0),TN)
        if n==0:
            dva_ref[...]=dv; dka_ref[...]=dk
        else:
            dva_ref[...]+=dv; dka_ref[...]+=dk
        dq_ref[rows,:]=dot(jnp.concatenate(grads,axis=1),both_k).astype(jnp.bfloat16)
    dk_ref[...]=dka_ref[...].T.astype(jnp.bfloat16)
    dv_ref[...]=dva_ref[...].T.astype(jnp.bfloat16)
    if has_bias:
        width=line_ref.shape[-1]
        lane=lax.broadcasted_iota(jnp.int32,(1,width),1)
        for h in range(2):
            band=jnp.concatenate((acc_ref[h],jnp.zeros((bq,bq),jnp.float32)),axis=1)
            sums=pltpu.roll(line_sums(band),bq,1)
            line=on_line(sums,lq-2*bq-LANES,width)
            for side,place in enumerate((0,wide-1)):
                far=jnp.sum(far_ref[h,side],axis=0,keepdims=True)
                far=jnp.sum(far,axis=1,keepdims=True)
                line=line+jnp.where(lane==place,far,0.0)
            dl_ref[0,h:h+1,:]=line

def cost_of():
    return pl.CostEstimate(flops=1,bytes_accessed=1,transcendentals=0)

def attend(q,qc,k,kc,v,vc,qx,kx,line,bq):
    lq=q.shape[0]; lk=k.shape[0]
    bq=min(bq,lq)
    has=line is not None
    blk=lambda rows,c: pl.BlockSpec((rows,LANES),lambda i,c=c:(0,c+i))
    fix=lambda rows: pl.BlockSpec((rows,LANES),lambda i:(0,0))
    ins=[blk(lq,qc),blk(lk,kc),blk(lk,vc),fix(lq),fix(lk)]
    args=[q,k,v,qx,kx]
    scratch=[]
    if has:
        ins.append(pl.BlockSpec((1,2,line.shape[-1]),lambda i:(i,0,0))); args.append(line)
        scratch=[pltpu.VMEM((2,lk+lq-bq,bq),jnp.float32)]
    return pl.pallas_call(functools.partial(fwd_kernel,bq,has),grid=(H//2,),in_specs=ins,
        out_specs=[blk(lq,0),pl.BlockSpec((2,lq,LANES),lambda i:(i,0,0))],
        out_shape=[jax.ShapeDtypeStruct((lq,H*DK),jnp.bfloat16),jax.ShapeDtypeStruct((H,lq,LANES),jnp.bfloat16)],
        scratch_shapes=scratch,compiler_params=pltpu.CompilerParams(vmem_limit_bytes=VLIM),cost_estimate=cost_of(),name="attend")(*args)

def attend_back(q,qc,k,kc,v,vc,g,qb,kx,line,bq,pairs=None):
    lq=q.shape[0]; lk=k.shape[0]
    bq=min(bq,lq)
    has=line is not None
    start,count=(0,H//2) if pairs is None else pairs
    blk=lambda rows,c: pl.BlockSpec((rows,LANES),lambda i,c=c:(0,c+start+i))
    fix=lambda rows: pl.BlockSpec((rows,LANES),lambda i:(0,0))
    ins=[blk(lq,qc),blk(lk,kc),blk(lk,vc),blk(lq,0),pl.BlockSpec((2,lq,LANES),lambda i:(start+i,0,0)),fix(lk)]
    args=[q,k,v,g,qb,kx]
    outs=[pl.BlockSpec((n,LANES),lambda i:(0,i)) for n in (lq,lk,lk)]
    shapes=[jax.ShapeDtypeStruct((n,count*LANES),jnp.bfloat16) for n in (lq,lk,lk)]
    scratch=[]
    if has:
        w=line.shape[-1]
        ins.append(pl.BlockSpec((1,2,w),lambda i:(start+i,0,0))); args.append(line)
        outs.append(pl.BlockSpec((1,2,w),lambda i:(i,0,0)))
        shapes.append(jax.ShapeDtypeStruct((count,2,w),jnp.float32))
        scratch=[pltpu.VMEM((2,bq,lk+lq-bq),jnp.float32),pltpu.VMEM((2,bq,bq+2*LANES),jnp.float32),pltpu.VMEM((2,2,bq,LANES),jnp.float32)]
    scratch=scratch+[pltpu.VMEM((LANES,lk),jnp.float32)]*2
    return pl.pallas_call(functools.partial(bwd_kernel,bq,has),grid=(count,),in_specs=ins,out_specs=outs,out_shape=shapes,
        scratch_shapes=scratch,compiler_params=pltpu.CompilerParams(vmem_limit_bytes=VLIM),cost_estimate=cost_of(),name="attend_back")(*args)

def seg_features(q_segs,k_segs):
    ids=jnp.arange(LANES,dtype=jnp.int32)[None,:]
    qx=jnp.where((ids<4)&(q_segs[:,None]!=ids),-BIG,0.0).astype(jnp.bfloat16)
    kx=jnp.where(((ids<4)&(k_segs[:,None]==ids))|((ids>=4)&(ids<7)),1.0,0.0).astype(jnp.bfloat16)
    return qx,kx


def marks(query_segs, key_segs):
    pairs = [seg_features(q, k) for q, k in zip(query_segs, key_segs)]
    return [p[0] for p in pairs], [p[1] for p in pairs]


def row_of(array, row, rows):
    length = array.shape[0] // rows
    return array[row * length : (row + 1) * length]


def join(parts):
    return parts[0] if len(parts) == 1 else jnp.concatenate(parts, axis=0)


def attend_rows(rows, queries, q_col, pairs, k_col, v_col, query_marks, key_marks, line):
    outs, kept = [], []
    for r in range(rows):
        q, kv = row_of(queries, r, rows), row_of(pairs, r, rows)
        out, mark = attend(
            q, q_col, kv, k_col, kv, v_col, query_marks[r], key_marks[r], line, BQ
        )
        outs.append(out)
        kept.append(mark)
    return join(outs), kept


def attend_rows_back(
    rows, queries, q_col, pairs, k_col, v_col, grads, kept, key_marks, line, part=None
):
    results = []
    for r in range(rows):
        q, kv = row_of(queries, r, rows), row_of(pairs, r, rows)
        grad = row_of(grads, r, rows)
        results.append(
            attend_back(
                q, q_col, kv, k_col, kv, v_col, grad, kept[r], key_marks[r], line, BQ, part
            )
        )
    gq, gk, gv = (join([res[i] for res in results]) for i in range(3))
    return gq, gk, gv, None if line is None else sum(res[3] for res in results)


def turn_rows(array):
    return lax.all_to_all(array, "seq", split_axis=0, concat_axis=0, tiled=True)


def bits_of(axis_name):
    return lax.axis_size(axis_name).bit_length() - 1


def swap(array, axis_name, bit):
    pairs = [(i, i ^ (1 << bit)) for i in range(lax.axis_size(axis_name))]
    return lax.ppermute(array, axis_name, pairs)


def halve(array, axis_name, bit, dim):
    mine = (lax.axis_index(axis_name) >> bit) & 1
    kept = lax.dynamic_slice_in_dim(array, mine, 1, dim)
    return kept, lax.dynamic_slice_in_dim(array, 1 - mine, 1, dim)


def add(kept, got):
    return kept.astype(jnp.float32) + got.astype(jnp.float32)


def add_low(kept, got):
    return add(kept, got).astype(jnp.bfloat16)


def grads_kernel(plan, stills, ranks, shares, core_ref, *refs):
    o_count = 1 + max(p[3] for p in plan)
    l_count = 1 + max(p[0] for p in plan)
    a_refs, g_refs = refs[:l_count], refs[l_count : l_count + len(plan)]
    o_refs = refs[l_count + len(plan) : l_count + len(plan) + 2 * o_count]
    t_refs = refs[l_count + len(plan) + 2 * o_count :]
    step = pl.program_id(0)
    core = core_ref[0]
    turned = set()
    for index, (at, first, steps, out, block) in enumerate(plan):
        if at in stills and at not in turned:
            turned.add(at)

            @pl.when(step == first)
            def turn(at=at):
                t_refs[stills.index(at)][...] = a_refs[at][...].T

        for mine in range(2):

            @pl.when((step >= first) & (step < first + steps) & (core == mine))
            def work(index=index, at=at, out=out, block=block, mine=mine):
                left, right = a_refs[at], g_refs[index]
                height, columns = left.shape[1], right.shape[1]
                tiles, group = block // 8, shares * block
                if at in stills:
                    turned_left = t_refs[stills.index(at)][...]
                else:
                    turned_left = left[...].T
                for col in range(0, columns, 256):
                    result = dot(turned_left, right[:, col : col + 256])
                    for place in range(height // group):
                        target = o_refs[2 * out + (0 if place % 2 == mine else 1)]
                        home = place // 2 * shares
                        piece = paired(result[place * group : (place + 1) * group], shares, tiles)
                        spot = col // 256 * tiles
                        target[home : home + shares, spot : spot + tiles] = piece


def whole_kernel(plan, stills, ranks, shares, *refs):
    l_count = 1 + max(p[0] for p in plan)
    a_refs, g_refs = refs[:l_count], refs[l_count : l_count + len(plan)]
    target = refs[l_count + len(plan)]
    t_refs = refs[l_count + len(plan) + 1 :]
    step = pl.program_id(0)
    turned = set()
    for index, (at, first, steps, start, block) in enumerate(plan):
        if at in stills and at not in turned:
            turned.add(at)

            @pl.when(step == first)
            def turn(at=at):
                t_refs[stills.index(at)][...] = a_refs[at][...].T

        @pl.when((step >= first) & (step < first + steps))
        def work(index=index, at=at, start=start, first=first, block=block):
            left, right = a_refs[at], g_refs[index]
            height, columns = left.shape[1], right.shape[1]
            tiles, group = block // 8, shares * block
            if at in stills:
                turned_left = t_refs[stills.index(at)][...]
                home, spot = 0, start + (step - first) * (columns // 256 * tiles)
            else:
                turned_left = left[...].T
                home, spot = (step - first) * (height // block), start
            for col in range(0, columns, 256):
                result = dot(turned_left, right[:, col : col + 256])
                for place in range(height // group):
                    piece = paired(result[place * group : (place + 1) * group], shares, tiles)
                    target[
                        pl.ds(home + place * shares, shares), pl.ds(spot + col // 256 * tiles, tiles)
                    ] = piece


def paired(piece, shares, tiles):
    halves = [
        piece[:, side * LANES : (side + 1) * LANES].reshape(shares, tiles, 8, LANES)
        for side in range(2)
    ]
    return jnp.concatenate(halves, axis=2).astype(jnp.bfloat16)


def tile_columns(shapes):
    columns = {}
    for height, width in shapes:
        columns[height] = math.gcd(columns.get(height, 768), width)
    return columns


def packed_grads(items, split=True):
    ranks = lax.axis_size("batch") * lax.axis_size("seq")
    shares = lax.axis_size("seq")
    shapes_in = [(left.shape[1], right.shape[1]) for left, right in items]
    widths = tile_columns(shapes_in)
    least = min([768] + [height for height, width in shapes_in])
    outs, plan, totals, firsts, stills = [], [], [], [], []
    lefts, left_specs, right_specs = [], [], []
    step = 0
    for left, right in items:
        height, width = left.shape[1], right.shape[1]
        if height not in outs:
            outs.append(height)
            totals.append(0)
            firsts.append(step)
        out = outs.index(height)
        tall = height > least
        steps = height // least if tall else width // widths[height]
        at = lambda i, c, first=step, last=steps - 1: (0, jnp.clip(i - first, 0, last))
        still = lambda i, c: (0, 0)
        same = [i for i in stills if lefts[i] is left]
        if same and not tall:
            where = same[0]
        else:
            where = len(lefts)
            lefts.append(left)
            left_specs.append(pl.BlockSpec((left.shape[0], least), at if tall else still))
            if not tall:
                stills.append(where)
        right_specs.append(pl.BlockSpec((right.shape[0], widths[height]), still if tall else at))
        plan.append((where, step, steps, out, height // ranks))
        totals[out] += steps
        step += steps
    shapes, specs = [], []
    for out, height in enumerate(outs):
        size = (height // ranks // 8) * (widths[height] // 256)
        tall = height > least
        count = 1 if tall else totals[out]
        parts = totals[out] if tall else 1
        for side in range(2):
            shapes.append(
                jax.ShapeDtypeStruct((ranks // 2, size * count, 16, LANES), jnp.bfloat16)
            )
            at = lambda i, c, first=firsts[out], last=totals[out] - 1, tall=tall: (
                (jnp.clip(i - first, 0, last), 0, 0, 0)
                if tall
                else (0, jnp.clip(i - first, 0, last), 0, 0)
            )
            specs.append(pl.BlockSpec((ranks // 2 // parts, size, 16, LANES), at))
    cost = cost_of()
    turned = [pltpu.VMEM((lefts[i].shape[1], lefts[i].shape[0]), jnp.bfloat16) for i in stills]
    if not split:
        whole_plan, tiles = [], 0
        for out in range(len(outs)):
            for where, first, steps, item_out, block in plan:
                if item_out == out:
                    whole_plan.append((where, first, steps, tiles, block))
                    height, width = shapes_in[len(whole_plan) - 1]
                    tiles += block // 8 * (width // 256)
        drop = lambda at: lambda i: at(i, None)
        return pl.pallas_call(
            functools.partial(whole_kernel, whole_plan, stills, ranks, shares),
            grid=(step,),
            in_specs=[
                pl.BlockSpec(x.block_shape, drop(x.index_map)) for x in left_specs + right_specs
            ],
            out_specs=pl.BlockSpec((ranks, tiles, 16, LANES), lambda i: (0, 0, 0, 0)),
            out_shape=jax.ShapeDtypeStruct((ranks, tiles, 16, LANES), jnp.bfloat16),
            scratch_shapes=turned,
            compiler_params=pltpu.CompilerParams(vmem_limit_bytes=VLIM),
            cost_estimate=cost,
            name="whole_grads",
        )(*lefts, *[right for left, right in items])
    core = (lax.axis_index("batch") & 1).astype(jnp.int32).reshape(1)
    results = pl.pallas_call(
        functools.partial(grads_kernel, plan, stills, ranks, shares),
        grid_spec=pltpu.PrefetchScalarGridSpec(
            num_scalar_prefetch=1,
            grid=(step,),
            in_specs=left_specs + right_specs,
            out_specs=specs,
            scratch_shapes=turned,
        ),
        out_shape=shapes,
        compiler_params=pltpu.CompilerParams(vmem_limit_bytes=VLIM),
        cost_estimate=cost,
        name="packed_grads",
    )(core, *lefts, *[right for left, right in items])
    return results[0::2], results[1::2]


def after(value, *others):
    return lax.optimization_barrier((value,) + others)[0]


class Small:
    def __init__(self, values):
        self.sent, self.got, self.kept = [values], [], values
        self.stages = [("batch", bit) for bit in range(bits_of("batch"))] + [("seq", -1)]

    def launch(self, sent):
        name, bit = self.stages.pop(0)
        if bit >= 0:
            self.got = [swap(sent[0], name, bit)]
            return
        size = lax.axis_size(name)
        self.got = [
            lax.ppermute(sent[0], name, [(i, i ^ step) for i in range(size)])
            for step in range(1, size)
        ]

    def advance(self, got):
        terms = [self.kept] + got
        while len(terms) > 1:
            terms = [terms[i] + terms[i + 1] for i in range(0, len(terms), 2)]
        self.kept = terms[0]
        self.got = []
        self.sent = [self.kept] if self.stages else []

    def finish(self):
        while self.got:
            self.advance(self.got)
            if self.sent:
                self.launch(self.sent)
        return self.kept


class Flow:
    def __init__(self, items, split=True, seq_first=False):
        self.split, self.seq_first = split, seq_first
        self.shapes = [(left.shape[1], right.shape[1]) for left, right in items]
        self.high, self.low = bits_of("batch"), bits_of("seq")
        self.ranks = 1 << (self.high + self.low)
        self.plain = min(shape[0] for shape in self.shapes) % (8 * self.ranks) != 0
        self.got, self.stage = [], 0
        if self.plain:
            self.sent = []
            self.whole = [weight_grad(left, right) for left, right in items]
            return
        heights = []
        for shape in self.shapes:
            if shape[0] not in heights:
                heights.append(shape[0])
        self.order = [
            [i for i, shape in enumerate(self.shapes) if shape[0] == height] for height in heights
        ]
        if split:
            self.kept, self.sent = packed_grads(items)
        else:
            self.sent = [packed_grads(items, False)]
        ups = [("batch", bit) for bit in range(1, self.high)]
        alongs = [("seq", bit) for bit in range(self.low)]
        if seq_first:
            self.steps = [[step] for step in alongs + ups]
        else:
            self.steps = [list(pair) for pair in zip(ups, ups[::-1])] + [None]

    def launch(self, sent):
        if self.plain:
            return
        if not self.split:
            axis_name = ("batch", "seq")[self.stage]
            self.got = [lax.psum_scatter(sent[0], axis_name, scatter_dimension=0, tiled=True)]
        elif self.stage == 0:
            self.got = [swap(x, "batch", 0) for x in sent]
        elif self.steps[self.stage - 1] is None:
            self.got = [
                lax.ppermute(x, "seq", [(i, i ^ step) for i in range(1 << self.low)])
                for step, x in enumerate(sent, 1)
            ]
        else:
            steps = self.steps[self.stage - 1]
            self.got = [swap(x, name, bit) for x, (name, bit) in zip(sent, steps)]
        self.stage += 1

    def advance(self, got):
        last = self.high - 1
        dim = last + self.low
        if not self.split:
            self.got, self.sent = [], got if self.stage == 1 else []
            self.result = got[0].astype(jnp.float32)
            return
        if self.stage > len(self.steps):
            self.result = add(self.kept[0], got[0])
            for more in got[1:]:
                self.result = self.result + more.astype(jnp.float32)
            self.got, self.sent = [], []
            return
        sums = [add_low(k, g) for k, g in zip(self.kept, got)]
        if self.stage == 1:
            sums = [x.reshape((2,) * dim + x.shape[1:]) for x in sums]
        steps = self.steps[self.stage - 1]
        if steps is None:
            whole = jnp.concatenate(sums, axis=dim)
            whole = whole.reshape((1 << self.low,) + whole.shape[dim:])
            place = lax.axis_index("seq")
            picks = [
                lax.dynamic_slice_in_dim(whole, place ^ step, 1, 0) for step in range(1 << self.low)
            ]
            self.kept, self.sent = picks[:1], picks[1:]
            return
        if len(sums) > len(steps):
            sums = [jnp.concatenate(sums, axis=dim)]
        elif len(sums) < len(steps):
            size = sums[0].shape[dim]
            sums = [
                lax.slice_in_dim(sums[0], 0, size // 2, axis=dim),
                lax.slice_in_dim(sums[0], size // 2, size, axis=dim),
            ]
        halves = [
            halve(x, name, bit, (last if name == "batch" else dim - 1) - bit)
            for x, (name, bit) in zip(sums, steps)
        ]
        self.kept = [h[0] for h in halves]
        self.sent = [h[1] for h in halves]

    def finish(self):
        if not self.plain and not self.split:
            while self.got:
                self.advance(self.got)
                if self.sent:
                    self.launch(self.sent)
        if self.plain:
            results = []
            for grad in self.whole:
                grad = lax.psum_scatter(
                    grad.astype(jnp.bfloat16), ("batch", "seq"), scatter_dimension=0, tiled=True
                )
                results.append(grad.astype(jnp.float32))
            return results
        while self.got:
            self.advance(self.got)
            if self.sent:
                self.launch(self.sent)
        part = self.result.reshape(-1, 16, LANES)
        results, start = [None] * len(self.shapes), 0
        for indices in self.order:
            for i in indices:
                height, width = self.shapes[i]
                tiles = height // self.ranks // 8
                count = tiles * width // 256
                piece = part[start : start + count]
                start += count
                piece = piece.reshape(width // 256, tiles, 2, 8, LANES)
                piece = jnp.transpose(piece, (1, 3, 0, 2, 4))
                results[i] = piece.reshape(tiles * 8, width)
        return results


def tick(value, *flows, fresh=()):
    live = [flow for flow in flows if flow is not None and flow.got]
    gots = [flow.got for flow in live]
    sents = [list(flow.sent) for flow in fresh]
    value, gots, sents = lax.optimization_barrier((value, gots, sents))
    for flow, sent in zip(fresh, sents):
        flow.launch(sent)
    for flow, got in zip(live, gots):
        flow.advance(got)
    value, sents = lax.optimization_barrier((value, [list(flow.sent) for flow in live]))
    for flow, sent in zip(live, sents):
        if sent:
            flow.launch(sent)
    return value


def body(
    enc_in,
    dec_in,
    out_grad,
    enc_segs,
    dec_segs,
    enc_qkv,
    enc_proj,
    enc_wi,
    enc_wo,
    enc_rel,
    enc_gains,
    dec_qkv,
    dec_proj,
    dec_rel,
    cross_q,
    cross_kv,
    cross_proj,
    dec_wi,
    dec_wo,
    dec_gains,
):
    shares = lax.axis_size("seq")
    rows = enc_in.shape[0] // shares
    full_len = enc_segs.shape[1]
    target_len = dec_in.shape[1]
    width = enc_in.shape[2]
    low = jnp.bfloat16
    row_segs = lax.dynamic_slice_in_dim(enc_segs, lax.axis_index("seq") * rows, rows, 0)

    local_len = enc_in.shape[1]
    enc_row = turn_rows(enc_in.reshape(shares, rows, local_len, width))
    enc_values = jnp.swapaxes(enc_row, 0, 1).reshape(-1, width).astype(jnp.float32)
    dec_values = dec_in.reshape(-1, width).astype(jnp.float32)

    offsets = line_offsets(full_len, full_len)
    turned = turned_offsets(full_len, full_len)
    enc_select = enc_selector(offsets)
    enc_line = bias_line(enc_rel, enc_select)
    enc_turned = bias_line(enc_rel, enc_selector(turned))
    offsets = line_offsets(target_len, target_len)
    turned = turned_offsets(target_len, target_len)
    dec_select = dec_selector(offsets)
    dec_line = bias_line(dec_rel, dec_select)
    dec_line = jnp.where(jnp.asarray(offsets > 0), -BIG, dec_line)
    dec_turned = bias_line(dec_rel, dec_selector(turned))
    dec_turned = jnp.where(jnp.asarray(turned > 0), -BIG, dec_turned)
    enc_query_marks, enc_key_marks = marks(row_segs, row_segs)
    dec_query_marks, dec_key_marks = marks(dec_segs, dec_segs)

    dec_normed_one, dec_inverse_one = norm_fwd(dec_values, dec_gains[0])
    dec_normed_one = dec_normed_one.astype(low)
    dec_packed = row_dot(dec_normed_one, dec_qkv).astype(low)
    self_mixed, self_marks = attend_rows(
        rows, dec_packed, 0, dec_packed, 6, 12, dec_query_marks, dec_key_marks, dec_turned
    )
    dec_first = dec_values + row_dot(self_mixed, dec_proj)
    dec_normed_two, dec_inverse_two = norm_fwd(dec_first, dec_gains[1])
    dec_normed_two = dec_normed_two.astype(low)
    cross_query = row_dot(dec_normed_two, cross_q).astype(low)

    normed_one, inverse_one = norm_fwd(enc_values, enc_gains[0])
    normed_one = normed_one.astype(low)
    packed = row_dot(normed_one, enc_qkv).astype(low)
    enc_mixed, enc_marks = attend_rows(
        rows, packed, 0, packed, 6, 12, enc_query_marks, enc_key_marks, enc_turned
    )
    after_attn = enc_values + row_dot(enc_mixed, enc_proj)
    normed_two, inverse_two = norm_fwd(after_attn, enc_gains[1])
    normed_two = normed_two.astype(low)
    enc_hidden, enc_slope = gelu_pair(row_dot(normed_two, enc_wi))
    second = after_attn + row_dot(enc_hidden, enc_wo)
    encoded, inverse_three = norm_fwd(second, enc_gains[2])
    encoded = encoded.astype(low)
    cross_pack = row_dot(encoded, cross_kv).astype(low)

    cross_mixed, cross_marks = attend_rows(
        rows, cross_query, 0, cross_pack, 0, 6, dec_query_marks, enc_key_marks, None
    )
    dec_second = dec_first + row_dot(cross_mixed, cross_proj)
    dec_normed_three, dec_inverse_three = norm_fwd(dec_second, dec_gains[2])
    dec_normed_three = dec_normed_three.astype(low)
    dec_hidden, dec_slope = gelu_pair(row_dot(dec_normed_three, dec_wi))
    dec_result = (dec_second + row_dot(dec_hidden, dec_wo)).astype(low)

    upstream = out_grad.reshape(-1, width)
    grad_pre = (back_dot(upstream, dec_wo) * dec_slope.astype(jnp.float32)).astype(low)
    flow_one = Flow(((dec_hidden, upstream), (dec_normed_three, grad_pre)), False)
    grad_pre, dec_result = tick((grad_pre, dec_result), fresh=(flow_one,))
    grad_input, gain_dec_three = norm_back(
        dec_second, dec_inverse_three, dec_gains[2], back_dot(grad_pre, dec_wi)
    )
    grad_second = upstream.astype(jnp.float32) + grad_input
    grad_cross_branch = grad_second.astype(low)
    grad_mixed = back_dot(grad_cross_branch, cross_proj).astype(low)
    grad_cq, grad_ck, grad_cv, unused = attend_rows_back(
        rows, cross_query, 0, cross_pack, 0, 6, grad_mixed, cross_marks, enc_key_marks, None
    )
    grad_input, gain_dec_two = norm_back(
        dec_first, dec_inverse_two, dec_gains[1], back_dot(grad_cq, cross_q)
    )
    grad_first = grad_second + grad_input
    grad_self_branch = grad_first.astype(low)
    grad_mixed = back_dot(grad_self_branch, dec_proj).astype(low)
    grad_sq, grad_sk, grad_sv, dec_line_grad = attend_rows_back(
        rows, dec_packed, 0, dec_packed, 6, 12, grad_mixed, self_marks, dec_key_marks, dec_line
    )
    flow_two = Flow(
        (
            (dec_normed_one, grad_sq),
            (dec_normed_one, grad_sk),
            (dec_normed_one, grad_sv),
            (self_mixed, grad_self_branch),
            (dec_normed_two, grad_cq),
            (cross_mixed, grad_cross_branch),
            (encoded, grad_ck),
            (encoded, grad_cv),
        ),
        False,
    )
    (grad_sq, grad_ck, dec_line_grad, gain_dec_three, gain_dec_two) = tick(
        (grad_sq, grad_ck, dec_line_grad, gain_dec_three, gain_dec_two), fresh=(flow_two,)
    )
    rel_grad_dec = rel_grad(dec_line_grad, dec_select)

    grad_enc_second, gain_enc_three = norm_back(
        second,
        inverse_three,
        enc_gains[2],
        back_dot(grad_ck, cross_kv[:, :width]) + back_dot(grad_cv, cross_kv[:, width:]),
    )
    grad_branch = grad_enc_second.astype(low)
    grad_branch, rel_grad_dec, gain_enc_three = tick((grad_branch, rel_grad_dec, gain_enc_three))
    flow_three = Flow(((enc_hidden, grad_branch),), seq_first=True)
    grad_branch = tick(grad_branch, fresh=(flow_three,))
    grad_pre = slope_back(grad_branch, enc_wo, enc_slope)
    grad_pre = tick(grad_pre, flow_one, flow_three)
    grad_input, gain_enc_two = norm_back(
        after_attn, inverse_two, enc_gains[1], back_dot(grad_pre, enc_wi)
    )
    grad_enc_first = grad_enc_second + grad_input
    grad_branch = grad_enc_first.astype(low)
    flow_four = Flow(((normed_two, grad_pre), (enc_mixed, grad_branch)))
    grad_branch, gain_enc_two = tick((grad_branch, gain_enc_two), fresh=(flow_four,))
    grad_mixed = back_dot(grad_branch, enc_proj).astype(low)
    grad_mixed = tick(grad_mixed, flow_four)
    pieces, line_grads, through = [], [], None
    flows = {0: (flow_three, flow_four), 2: (flow_two, flow_four), 4: ()}
    for part in ((0, 2), (2, 2), (4, 2)):
        grad_eq, grad_ek, grad_ev, line_grad = attend_rows_back(
            rows,
            packed,
            0,
            packed,
            6,
            12,
            grad_mixed,
            enc_marks,
            enc_key_marks,
            enc_line,
            part,
        )
        grad_eq, grad_ek, grad_ev, line_grad, grad_mixed = tick(
            (grad_eq, grad_ek, grad_ev, line_grad, grad_mixed), *flows[part[0]]
        )
        line_grads.append(line_grad)
        pieces.append((grad_eq, grad_ek, grad_ev))
        if part[0] == 4:
            flow_five = Flow([(normed_one, piece[at]) for at in range(3) for piece in pieces])
            pieces = tick(pieces, fresh=(flow_five,))
            grad_eq, grad_ek, grad_ev = pieces[-1]
        for at, piece in enumerate((grad_eq, grad_ek, grad_ev)):
            start = at * width + part[0] * LANES
            term = back_dot(piece, enc_qkv[:, start : start + part[1] * LANES])
            through = term if through is None else through + term
        grad_mixed = after(grad_mixed, through)
    through = tick(through, flow_five)
    grad_input, gain_enc_one = norm_back(enc_values, inverse_one, enc_gains[0], through)
    enc_grad_row = (grad_enc_first + grad_input).astype(low)
    enc_grad_turned = enc_grad_row.reshape(rows, shares, local_len, width)
    enc_grad = turn_rows(jnp.swapaxes(enc_grad_turned, 0, 1)).reshape(enc_in.shape)

    grad_sq = after(grad_sq, enc_grad_row)
    grad_sq = tick(grad_sq, flow_one, flow_two, flow_three, flow_four, flow_five)
    grad_input, gain_dec_one = norm_back(
        dec_values,
        dec_inverse_one,
        dec_gains[0],
        back_dot(grad_sq, dec_qkv[:, :width])
        + back_dot(grad_sk, dec_qkv[:, width : 2 * width])
        + back_dot(grad_sv, dec_qkv[:, 2 * width :]),
    )
    dec_in_grad = grad_first + grad_input
    enc_line_grad = jnp.concatenate(line_grads, axis=0)
    rels = jnp.concatenate((rel_grad(enc_line_grad, enc_select), rel_grad_dec), axis=0)
    gains = (
        (gain_enc_one, gain_enc_two, gain_enc_three) + (gain_dec_one, gain_dec_two, gain_dec_three)
    )
    small = Small(jnp.concatenate((jnp.stack(gains), rels.reshape(1, -1)), axis=0))
    dec_in_grad, dec_result = tick((dec_in_grad, dec_result), flow_five, fresh=(small,))
    dec_result = tick(dec_result, flow_three, small)
    dec_result = tick(dec_result, flow_three, small)
    dec_result = tick(dec_result, small)
    dec_result, enc_grad = lax.optimization_barrier((dec_result, enc_grad))
    for unused in range(3):
        dec_result = tick(dec_result, flow_three, flow_four, flow_five, small)
    small = small.finish()
    gains_enc_total, gains_dec_total = small[:3], small[3:6]
    rels = small[6].reshape(2, NB, H)
    rel_enc_total, rel_dec_total = rels[0], rels[1]
    grad_dec_wo, grad_dec_wi = flow_one.finish()
    two = flow_two.finish()
    dec_q, dec_k, dec_v, grad_dec_proj, grad_cross_q, grad_cross_proj, cross_k, cross_v = two
    (grad_enc_wo,) = flow_three.finish()
    grad_enc_wi, grad_enc_proj = flow_four.finish()
    grad_enc_qkv = jnp.concatenate(flow_five.finish(), axis=1)
    return (
        dec_result.reshape(dec_in.shape),
        enc_grad.astype(jnp.float32),
        dec_in_grad.reshape(dec_in.shape),
        grad_enc_qkv,
        grad_enc_proj,
        grad_enc_wi,
        grad_enc_wo,
        rel_enc_total,
        gains_enc_total,
        jnp.concatenate((dec_q, dec_k, dec_v), axis=1),
        grad_dec_proj,
        rel_dec_total,
        grad_cross_q,
        jnp.concatenate((cross_k, cross_v), axis=1),
        grad_cross_proj,
        grad_dec_wi,
        grad_dec_wo,
        gains_dec_total,
    )


def solution(mesh):
    in_specs = (
        P("batch", "seq", None),
        P(("batch", "seq"), None, None),
        P(("batch", "seq"), None, None),
        P("batch", None),
        P(("batch", "seq"), None),
        P(),
        P(),
        P(),
        P(),
        P(),
        P(),
        P(),
        P(),
        P(),
        P(),
        P(),
        P(),
        P(),
        P(),
        P(),
    )
    out_specs = (
        P(("batch", "seq"), None, None),
        P("batch", "seq", None),
        P(("batch", "seq"), None, None),
        P(("batch", "seq"), None),
        P(("batch", "seq"), None),
        P(("batch", "seq"), None),
        P(("batch", "seq"), None),
        P(),
        P(),
        P(("batch", "seq"), None),
        P(("batch", "seq"), None),
        P(),
        P(("batch", "seq"), None),
        P(("batch", "seq"), None),
        P(("batch", "seq"), None),
        P(("batch", "seq"), None),
        P(("batch", "seq"), None),
        P(),
    )
    return jax.shard_map(body, mesh=mesh, in_specs=in_specs, out_specs=out_specs, check_vma=False)
```

```python
import functools
import math

import jax
import jax.numpy as jnp
import numpy as np
from jax import lax
from jax.experimental import pallas as pl
from jax.experimental.pallas import tpu as pltpu
from jax.sharding import PartitionSpec as P

H = 12
DK = 64
NB = 32
MAXD = 128
ENC_LEN = 1024
DEC_LEN = 256
LANES = 128
BQ = 256
BIG = 1e9
VLIM = 56 * 1024 * 1024
EPS = 1e-06

def bucket_steps(classes, distance, length):
    exact_part = classes // 2
    thresholds = []
    previous = 0
    for offset in range(1, length + 1):
        if offset < exact_part:
            bucket_level = offset
        else:
            bucket_level = min(
                classes - 1,
                exact_part
                + int(
                    math.log(offset / exact_part)
                    / math.log(distance / exact_part)
                    * (classes - exact_part)
                ),
            )
        if bucket_level > previous:
            thresholds.append((offset, bucket_level - previous))
            previous = bucket_level
    return thresholds


def step_buckets(distance, steps):
    buckets = np.zeros(distance.shape, np.int32)
    for edge, size in steps:
        buckets = buckets + size * (distance >= edge)
    return buckets


def line_offsets(queries, keys):
    place = np.arange(queries + keys)
    block = min(BQ, queries)
    wrapped = np.where(place >= queries + keys - block, place - queries - keys, place)
    return wrapped - (queries - block)


def turned_offsets(queries, keys):
    block = min(BQ, queries)
    place = np.arange(2 * block)
    wrapped = np.where(place >= block, place - 2 * block, place)
    starts = np.arange(0, keys + queries - block, block) - (queries - block)
    return (starts[:, None] - wrapped[None, :]).reshape(-1)


def enc_selector(offsets):
    half = NB // 2
    buckets = half * (offsets > 0) + step_buckets(np.abs(offsets), bucket_steps(half, MAXD, ENC_LEN))
    return jnp.asarray(buckets, jnp.int32)[:, None] == jnp.arange(NB, dtype=jnp.int32)[None, :]


def dec_selector(offsets):
    buckets = step_buckets(np.maximum(-offsets, 0), bucket_steps(NB, MAXD, DEC_LEN))
    return jnp.asarray(buckets, jnp.int32)[:, None] == jnp.arange(NB, dtype=jnp.int32)[None, :]


def bias_line(rel_table, selector):
    line = jnp.einsum(
        "nb,bh->hn", selector.astype(jnp.float32), rel_table, precision=lax.Precision.HIGHEST
    )
    return line.reshape(H // 2, 2, -1)


def rel_grad(line_grad, selector):
    return jnp.einsum(
        "hn,nb->bh",
        line_grad.reshape(H, -1),
        selector.astype(jnp.float32),
        precision=lax.Precision.HIGHEST,
    )


def gelu_pair(values):
    scale = math.sqrt(2.0 / math.pi)
    square = values * values
    curve = jnp.tanh(values * (scale + scale * 0.044715 * square))
    half = 0.5 * (1.0 + curve)
    inner = scale + 3.0 * scale * 0.044715 * square
    slope = half + 0.5 * values * (1.0 - curve * curve) * inner
    return (values * half).astype(jnp.bfloat16), slope.astype(jnp.bfloat16)


def row_dot(inputs, weight):
    return jnp.einsum("...i,ij->...j", inputs, weight, preferred_element_type=jnp.float32)


def back_dot(grad_vals, weight):
    return jnp.einsum("...j,ij->...i", grad_vals, weight, preferred_element_type=jnp.float32)


def weight_grad(inputs, grad_vals):
    return jnp.einsum(
        "ti,tj->ij",
        inputs.reshape(-1, inputs.shape[-1]),
        grad_vals.reshape(-1, grad_vals.shape[-1]),
        preferred_element_type=jnp.float32,
    )


def slope_kernel(grad_ref, weight_ref, slope_ref, out_ref):
    weight = weight_ref[...]
    for at in range(0, grad_ref.shape[0], 256):
        rows = slice(at, at + 256)
        grad = dot(grad_ref[rows, :], weight, NT)
        out_ref[rows, :] = (grad * slope_ref[rows, :].astype(jnp.float32)).astype(jnp.bfloat16)


def slope_back(grad, weight, slope):
    tokens, hidden = slope.shape
    step = 768
    return pl.pallas_call(
        slope_kernel,
        grid=(hidden // step,),
        in_specs=[
            pl.BlockSpec(grad.shape, lambda i: (0, 0)),
            pl.BlockSpec((step, weight.shape[1]), lambda i: (i, 0)),
            pl.BlockSpec((tokens, step), lambda i: (0, i)),
        ],
        out_specs=pl.BlockSpec((tokens, step), lambda i: (0, i)),
        out_shape=jax.ShapeDtypeStruct(slope.shape, jnp.bfloat16),
        compiler_params=pltpu.CompilerParams(vmem_limit_bytes=VLIM),
        cost_estimate=cost_of(),
        name="slope_back",
    )(grad, weight, slope)


def norm_fwd(values, gain_vec):
    inverse = lax.rsqrt(jnp.mean(values * values, axis=-1, keepdims=True) + EPS)
    return (values * inverse * gain_vec, inverse)


def norm_back(values, inverse, gain_vec, grad_vals):
    scaled = grad_vals * gain_vec
    grad_values = inverse * scaled - values * inverse**3 * jnp.mean(
        scaled * values, axis=-1, keepdims=True
    )
    grad_gain = jnp.sum((grad_vals * values * inverse).reshape(-1, values.shape[-1]), axis=0)
    return (grad_values, grad_gain)


NN=(((1,),(0,)),((),()))
NT=(((1,),(1,)),((),()))
TN=(((0,),(0,)),((),()))
def dot(a,b,dims=NN):
    return lax.dot_general(a,b,dims,preferred_element_type=jnp.float32)

def head_mask(rows):
    lane=lax.broadcasted_iota(jnp.int32,(rows,LANES),1)
    return lane<DK

def keep(x,first,head):
    zero=jnp.zeros_like(x)
    return jnp.where(first,x,zero) if head==0 else jnp.where(first,zero,x)

def skew_line(line_row,rows):
    width=line_row.shape[-1]
    wide=jnp.broadcast_to(line_row,(rows,width))
    return pltpu.roll(wide,0,1,stride=1,stride_axis=0)

def line_sums(band):
    rows,width=band.shape
    total=band[:8]
    for g in range(1,rows//8):
        total=total+pltpu.roll(band[8*g:8*g+8],width-8*g,1)
    row=lax.broadcasted_iota(jnp.int32,(8,width),0)
    for b in range(3):
        total=jnp.where((row>>b)&1==1,pltpu.roll(total,width-(1<<b),1),total)
    return jnp.sum(total,axis=0,keepdims=True)

def on_line(values,start,width):
    size=values.shape[1]
    blank=lambda n: [jnp.zeros((1,n),jnp.float32)] if n>0 else []
    if start>=0:
        return jnp.concatenate(blank(start)+[values]+blank(width-start-size),axis=1)
    late,early=values[:,-start:],values[:,:-start]
    late=jnp.concatenate([late]+blank(width-size-start),axis=1)
    return late+jnp.concatenate(blank(width+start)+[early],axis=1)

def fwd_kernel(bq,has_bias,*refs):
    if has_bias:
        q_ref,k_ref,v_ref,qx_ref,kx_ref,line_ref,o_ref,qb_ref,bias_ref=refs
    else:
        q_ref,k_ref,v_ref,qx_ref,kx_ref,o_ref,qb_ref=refs
    lq=q_ref.shape[0]; lk=k_ref.shape[0]
    if has_bias:
        for h in range(2):
            for b in range(bias_ref.shape[1]//bq):
                source=line_ref[0,h:h+1,2*b*bq:2*(b+1)*bq]
                least=b*bq-(lq-bq)-(bq-1)
                if least>=MAXD or least+2*bq-2<=-MAXD:
                    block=jnp.broadcast_to(source[:,:bq],(bq,bq))
                else:
                    block=skew_line(source,bq)[:,:bq]
                bias_ref[h,b*bq:(b+1)*bq,:]=block
    first=head_mask(bq)
    row=lax.broadcasted_iota(jnp.int32,(LANES,bq),0)
    keys=jnp.concatenate((k_ref[...],kx_ref[...]),axis=1)
    values=v_ref[...].T
    def score(n,h):
        rows=slice(n*bq,(n+1)*bq)
        return dot(keys,jnp.concatenate((keep(q_ref[rows,:],first,h),qx_ref[rows,:]),axis=1),NT)
    tiles=[(n,h) for n in range(lq//bq) for h in range(2)]
    ahead=score(*tiles[0])
    for at,(n,h) in enumerate(tiles):
        rows=slice(n*bq,(n+1)*bq)
        s=ahead
        if at+1<len(tiles):
            ahead=score(*tiles[at+1])
        if has_bias:
            off=lq-bq-n*bq
            bias=bias_ref[h,off:off+lk,:]
            top=jnp.max(s+bias,axis=0,keepdims=True)
            e=jnp.exp((s-top)+bias)
        else:
            top=jnp.max(s,axis=0,keepdims=True)
            e=jnp.exp(s-top)
        total=jnp.sum(e,axis=0,keepdims=True)
        p=(e*(1.0/total)).astype(jnp.bfloat16)
        out=dot(values,p)
        low=-(top+jnp.log(total))
        one=low.astype(jnp.bfloat16).astype(jnp.float32)
        two=(low-one).astype(jnp.bfloat16).astype(jnp.float32)
        three=low-one-two
        x=jnp.where(row==4,one,jnp.where(row==5,two,jnp.where(row==6,three,0.0)))
        qb_ref[h,rows,:]=(x.T+qx_ref[rows,:].astype(jnp.float32)).astype(jnp.bfloat16)
        if h==0:
            kept=out
        else:
            o_ref[rows,:]=jnp.where(row<DK,kept,out).T.astype(jnp.bfloat16)

def bwd_kernel(bq,has_bias,*refs):
    if has_bias:
        q_ref,k_ref,v_ref,g_ref,qb_ref,kx_ref,line_ref,dq_ref,dk_ref,dv_ref,dl_ref,bias_ref,acc_ref,far_ref,dka_ref,dva_ref=refs
    else:
        q_ref,k_ref,v_ref,g_ref,qb_ref,kx_ref,dq_ref,dk_ref,dv_ref,dka_ref,dva_ref=refs
    lq=q_ref.shape[0]; lk=k_ref.shape[0]
    wide=lk+lq-bq
    if has_bias:
        for h in range(2):
            bias_ref[h]=skew_line(line_ref[0,h:h+1,:],bq)[:,:wide]
        acc_ref[...]=jnp.zeros_like(acc_ref)
        far_ref[...]=jnp.zeros_like(far_ref)
    first=head_mask(bq)
    keyfirst=head_mask(lk)
    k=k_ref[...]
    keys=jnp.concatenate((k,kx_ref[...]),axis=1)
    values=v_ref[...]
    heads_k=[keep(k,keyfirst,h) for h in range(2)]
    def start(n,h):
        rows=slice(n*bq,(n+1)*bq)
        qh=keep(q_ref[rows,:],first,h); gh=keep(g_ref[rows,:],first,h)
        s=dot(jnp.concatenate((qh,qb_ref[h,rows,:]),axis=1),keys,NT)
        return qh,gh,s,dot(gh,values,NT)
    both_k=jnp.concatenate(heads_k,axis=0)
    count=lq//bq
    ahead=[start(0,h) for h in range(2)]
    for n in range(count):
        rows=slice(n*bq,(n+1)*bq)
        now,ahead=ahead,[]
        probs,grads=[],[]
        for h in range(2):
            qh,gh,s,dp=now[h]
            if n+1<count:
                ahead.append(start(n+1,h))
            if has_bias:
                off=lq-bq-n*bq
                s=s+bias_ref[h,:,off:off+lk]
            p=jnp.exp(s)
            inner=jnp.sum(p*dp,axis=1,keepdims=True)
            gs=(p*(dp-inner)).astype(jnp.bfloat16)
            if has_bias:
                lo,hi=max(0,n*bq-LANES),min(lk,n*bq+bq+LANES)
                spot=lo-n*bq+LANES
                acc_ref[h,:,spot:spot+hi-lo]+=gs[:,lo:hi].astype(jnp.float32)
                for side,(a,b) in enumerate(((0,lo),(hi,lk))):
                    if b>a:
                        total=gs[:,a:a+LANES].astype(jnp.float32)
                        for c in range(a+LANES,b,LANES):
                            total=total+gs[:,c:c+LANES].astype(jnp.float32)
                        far_ref[h,side]+=total
            probs.append(p.astype(jnp.bfloat16)); grads.append(gs)
        dv=dot(jnp.concatenate((now[0][1],now[1][1]),axis=0),jnp.concatenate(probs,axis=0),TN)
        dk=dot(jnp.concatenate((now[0][0],now[1][0]),axis=0),jnp.concatenate(grads,axis=0),TN)
        if n==0:
            dva_ref[...]=dv; dka_ref[...]=dk
        else:
            dva_ref[...]+=dv; dka_ref[...]+=dk
        dq_ref[rows,:]=dot(jnp.concatenate(grads,axis=1),both_k).astype(jnp.bfloat16)
    dk_ref[...]=dka_ref[...].T.astype(jnp.bfloat16)
    dv_ref[...]=dva_ref[...].T.astype(jnp.bfloat16)
    if has_bias:
        width=line_ref.shape[-1]
        lane=lax.broadcasted_iota(jnp.int32,(1,width),1)
        for h in range(2):
            band=jnp.concatenate((acc_ref[h],jnp.zeros((bq,bq),jnp.float32)),axis=1)
            sums=pltpu.roll(line_sums(band),bq,1)
            line=on_line(sums,lq-2*bq-LANES,width)
            for side,place in enumerate((0,wide-1)):
                far=jnp.sum(far_ref[h,side],axis=0,keepdims=True)
                far=jnp.sum(far,axis=1,keepdims=True)
                line=line+jnp.where(lane==place,far,0.0)
            dl_ref[0,h:h+1,:]=line

def cost_of():
    return pl.CostEstimate(flops=1,bytes_accessed=1,transcendentals=0)

def attend(q,qc,k,kc,v,vc,qx,kx,line,bq):
    lq=q.shape[0]; lk=k.shape[0]
    bq=min(bq,lq)
    has=line is not None
    blk=lambda rows,c: pl.BlockSpec((rows,LANES),lambda i,c=c:(0,c+i))
    fix=lambda rows: pl.BlockSpec((rows,LANES),lambda i:(0,0))
    ins=[blk(lq,qc),blk(lk,kc),blk(lk,vc),fix(lq),fix(lk)]
    args=[q,k,v,qx,kx]
    scratch=[]
    if has:
        ins.append(pl.BlockSpec((1,2,line.shape[-1]),lambda i:(i,0,0))); args.append(line)
        scratch=[pltpu.VMEM((2,lk+lq-bq,bq),jnp.float32)]
    return pl.pallas_call(functools.partial(fwd_kernel,bq,has),grid=(H//2,),in_specs=ins,
        out_specs=[blk(lq,0),pl.BlockSpec((2,lq,LANES),lambda i:(i,0,0))],
        out_shape=[jax.ShapeDtypeStruct((lq,H*DK),jnp.bfloat16),jax.ShapeDtypeStruct((H,lq,LANES),jnp.bfloat16)],
        scratch_shapes=scratch,compiler_params=pltpu.CompilerParams(vmem_limit_bytes=VLIM),cost_estimate=cost_of(),name="attend")(*args)

def attend_back(q,qc,k,kc,v,vc,g,qb,kx,line,bq,pairs=None):
    lq=q.shape[0]; lk=k.shape[0]
    bq=min(bq,lq)
    has=line is not None
    start,count=(0,H//2) if pairs is None else pairs
    blk=lambda rows,c: pl.BlockSpec((rows,LANES),lambda i,c=c:(0,c+start+i))
    fix=lambda rows: pl.BlockSpec((rows,LANES),lambda i:(0,0))
    ins=[blk(lq,qc),blk(lk,kc),blk(lk,vc),blk(lq,0),pl.BlockSpec((2,lq,LANES),lambda i:(start+i,0,0)),fix(lk)]
    args=[q,k,v,g,qb,kx]
    outs=[pl.BlockSpec((n,LANES),lambda i:(0,i)) for n in (lq,lk,lk)]
    shapes=[jax.ShapeDtypeStruct((n,count*LANES),jnp.bfloat16) for n in (lq,lk,lk)]
    scratch=[]
    if has:
        w=line.shape[-1]
        ins.append(pl.BlockSpec((1,2,w),lambda i:(start+i,0,0))); args.append(line)
        outs.append(pl.BlockSpec((1,2,w),lambda i:(i,0,0)))
        shapes.append(jax.ShapeDtypeStruct((count,2,w),jnp.float32))
        scratch=[pltpu.VMEM((2,bq,lk+lq-bq),jnp.float32),pltpu.VMEM((2,bq,bq+2*LANES),jnp.float32),pltpu.VMEM((2,2,bq,LANES),jnp.float32)]
    scratch=scratch+[pltpu.VMEM((LANES,lk),jnp.float32)]*2
    return pl.pallas_call(functools.partial(bwd_kernel,bq,has),grid=(count,),in_specs=ins,out_specs=outs,out_shape=shapes,
        scratch_shapes=scratch,compiler_params=pltpu.CompilerParams(vmem_limit_bytes=VLIM),cost_estimate=cost_of(),name="attend_back")(*args)

def seg_features(q_segs,k_segs):
    ids=jnp.arange(LANES,dtype=jnp.int32)[None,:]
    qx=jnp.where((ids<4)&(q_segs[:,None]!=ids),-BIG,0.0).astype(jnp.bfloat16)
    kx=jnp.where(((ids<4)&(k_segs[:,None]==ids))|((ids>=4)&(ids<7)),1.0,0.0).astype(jnp.bfloat16)
    return qx,kx


def marks(query_segs, key_segs):
    pairs = [seg_features(q, k) for q, k in zip(query_segs, key_segs)]
    return [p[0] for p in pairs], [p[1] for p in pairs]


def row_of(array, row, rows):
    length = array.shape[0] // rows
    return array[row * length : (row + 1) * length]


def join(parts):
    return parts[0] if len(parts) == 1 else jnp.concatenate(parts, axis=0)


def attend_rows(rows, queries, q_col, pairs, k_col, v_col, query_marks, key_marks, line):
    outs, kept = [], []
    for r in range(rows):
        q, kv = row_of(queries, r, rows), row_of(pairs, r, rows)
        out, mark = attend(
            q, q_col, kv, k_col, kv, v_col, query_marks[r], key_marks[r], line, BQ
        )
        outs.append(out)
        kept.append(mark)
    return join(outs), kept


def attend_rows_back(
    rows, queries, q_col, pairs, k_col, v_col, grads, kept, key_marks, line, part=None
):
    results = []
    for r in range(rows):
        q, kv = row_of(queries, r, rows), row_of(pairs, r, rows)
        grad = row_of(grads, r, rows)
        results.append(
            attend_back(
                q, q_col, kv, k_col, kv, v_col, grad, kept[r], key_marks[r], line, BQ, part
            )
        )
    gq, gk, gv = (join([res[i] for res in results]) for i in range(3))
    return gq, gk, gv, None if line is None else sum(res[3] for res in results)


def turn_rows(array):
    return lax.all_to_all(array, "seq", split_axis=0, concat_axis=0, tiled=True)


def bits_of(axis_name):
    return lax.axis_size(axis_name).bit_length() - 1


def swap(array, axis_name, bit):
    pairs = [(i, i ^ (1 << bit)) for i in range(lax.axis_size(axis_name))]
    return lax.ppermute(array, axis_name, pairs)


def halve(array, axis_name, bit, dim):
    mine = (lax.axis_index(axis_name) >> bit) & 1
    kept = lax.dynamic_slice_in_dim(array, mine, 1, dim)
    return kept, lax.dynamic_slice_in_dim(array, 1 - mine, 1, dim)


def add(kept, got):
    return kept.astype(jnp.float32) + got.astype(jnp.float32)


def add_low(kept, got):
    return add(kept, got).astype(jnp.bfloat16)


def grads_kernel(plan, stills, ranks, shares, core_ref, *refs):
    o_count = 1 + max(p[3] for p in plan)
    l_count = 1 + max(p[0] for p in plan)
    a_refs, g_refs = refs[:l_count], refs[l_count : l_count + len(plan)]
    o_refs = refs[l_count + len(plan) : l_count + len(plan) + 2 * o_count]
    t_refs = refs[l_count + len(plan) + 2 * o_count :]
    step = pl.program_id(0)
    core = core_ref[0]
    turned = set()
    for index, (at, first, steps, out, block) in enumerate(plan):
        if at in stills and at not in turned:
            turned.add(at)

            @pl.when(step == first)
            def turn(at=at):
                t_refs[stills.index(at)][...] = a_refs[at][...].T

        for mine in range(2):

            @pl.when((step >= first) & (step < first + steps) & (core == mine))
            def work(index=index, at=at, out=out, block=block, mine=mine):
                left, right = a_refs[at], g_refs[index]
                height, columns = left.shape[1], right.shape[1]
                tiles, group = block // 8, shares * block
                if at in stills:
                    turned_left = t_refs[stills.index(at)][...]
                else:
                    turned_left = left[...].T
                for col in range(0, columns, 256):
                    result = dot(turned_left, right[:, col : col + 256])
                    for place in range(height // group):
                        target = o_refs[2 * out + (0 if place % 2 == mine else 1)]
                        home = place // 2 * shares
                        piece = paired(result[place * group : (place + 1) * group], shares, tiles)
                        spot = col // 256 * tiles
                        target[home : home + shares, spot : spot + tiles] = piece


def whole_kernel(plan, stills, ranks, shares, *refs):
    l_count = 1 + max(p[0] for p in plan)
    a_refs, g_refs = refs[:l_count], refs[l_count : l_count + len(plan)]
    target = refs[l_count + len(plan)]
    t_refs = refs[l_count + len(plan) + 1 :]
    step = pl.program_id(0)
    turned = set()
    for index, (at, first, steps, start, block) in enumerate(plan):
        if at in stills and at not in turned:
            turned.add(at)

            @pl.when(step == first)
            def turn(at=at):
                t_refs[stills.index(at)][...] = a_refs[at][...].T

        @pl.when((step >= first) & (step < first + steps))
        def work(index=index, at=at, start=start, first=first, block=block):
            left, right = a_refs[at], g_refs[index]
            height, columns = left.shape[1], right.shape[1]
            tiles, group = block // 8, shares * block
            if at in stills:
                turned_left = t_refs[stills.index(at)][...]
                home, spot = 0, start + (step - first) * (columns // 256 * tiles)
            else:
                turned_left = left[...].T
                home, spot = (step - first) * (height // block), start
            for col in range(0, columns, 256):
                result = dot(turned_left, right[:, col : col + 256])
                for place in range(height // group):
                    piece = paired(result[place * group : (place + 1) * group], shares, tiles)
                    target[
                        pl.ds(home + place * shares, shares), pl.ds(spot + col // 256 * tiles, tiles)
                    ] = piece


def paired(piece, shares, tiles):
    halves = [
        piece[:, side * LANES : (side + 1) * LANES].reshape(shares, tiles, 8, LANES)
        for side in range(2)
    ]
    return jnp.concatenate(halves, axis=2).astype(jnp.bfloat16)


def tile_columns(shapes):
    columns = {}
    for height, width in shapes:
        columns[height] = math.gcd(columns.get(height, 768), width)
    return columns


def packed_grads(items, split=True):
    ranks = lax.axis_size("batch") * lax.axis_size("seq")
    shares = lax.axis_size("seq")
    shapes_in = [(left.shape[1], right.shape[1]) for left, right in items]
    widths = tile_columns(shapes_in)
    least = min([768] + [height for height, width in shapes_in])
    outs, plan, totals, firsts, stills = [], [], [], [], []
    lefts, left_specs, right_specs = [], [], []
    step = 0
    for left, right in items:
        height, width = left.shape[1], right.shape[1]
        if height not in outs:
            outs.append(height)
            totals.append(0)
            firsts.append(step)
        out = outs.index(height)
        tall = height > least
        steps = height // least if tall else width // widths[height]
        at = lambda i, c, first=step, last=steps - 1: (0, jnp.clip(i - first, 0, last))
        still = lambda i, c: (0, 0)
        same = [i for i in stills if lefts[i] is left]
        if same and not tall:
            where = same[0]
        else:
            where = len(lefts)
            lefts.append(left)
            left_specs.append(pl.BlockSpec((left.shape[0], least), at if tall else still))
            if not tall:
                stills.append(where)
        right_specs.append(pl.BlockSpec((right.shape[0], widths[height]), still if tall else at))
        plan.append((where, step, steps, out, height // ranks))
        totals[out] += steps
        step += steps
    shapes, specs = [], []
    for out, height in enumerate(outs):
        size = (height // ranks // 8) * (widths[height] // 256)
        tall = height > least
        count = 1 if tall else totals[out]
        parts = totals[out] if tall else 1
        for side in range(2):
            shapes.append(
                jax.ShapeDtypeStruct((ranks // 2, size * count, 16, LANES), jnp.bfloat16)
            )
            at = lambda i, c, first=firsts[out], last=totals[out] - 1, tall=tall: (
                (jnp.clip(i - first, 0, last), 0, 0, 0)
                if tall
                else (0, jnp.clip(i - first, 0, last), 0, 0)
            )
            specs.append(pl.BlockSpec((ranks // 2 // parts, size, 16, LANES), at))
    cost = cost_of()
    turned = [pltpu.VMEM((lefts[i].shape[1], lefts[i].shape[0]), jnp.bfloat16) for i in stills]
    if not split:
        whole_plan, tiles = [], 0
        for out in range(len(outs)):
            for where, first, steps, item_out, block in plan:
                if item_out == out:
                    whole_plan.append((where, first, steps, tiles, block))
                    height, width = shapes_in[len(whole_plan) - 1]
                    tiles += block // 8 * (width // 256)
        drop = lambda at: lambda i: at(i, None)
        return pl.pallas_call(
            functools.partial(whole_kernel, whole_plan, stills, ranks, shares),
            grid=(step,),
            in_specs=[
                pl.BlockSpec(x.block_shape, drop(x.index_map)) for x in left_specs + right_specs
            ],
            out_specs=pl.BlockSpec((ranks, tiles, 16, LANES), lambda i: (0, 0, 0, 0)),
            out_shape=jax.ShapeDtypeStruct((ranks, tiles, 16, LANES), jnp.bfloat16),
            scratch_shapes=turned,
            compiler_params=pltpu.CompilerParams(vmem_limit_bytes=VLIM),
            cost_estimate=cost,
            name="whole_grads",
        )(*lefts, *[right for left, right in items])
    core = (lax.axis_index("batch") & 1).astype(jnp.int32).reshape(1)
    results = pl.pallas_call(
        functools.partial(grads_kernel, plan, stills, ranks, shares),
        grid_spec=pltpu.PrefetchScalarGridSpec(
            num_scalar_prefetch=1,
            grid=(step,),
            in_specs=left_specs + right_specs,
            out_specs=specs,
            scratch_shapes=turned,
        ),
        out_shape=shapes,
        compiler_params=pltpu.CompilerParams(vmem_limit_bytes=VLIM),
        cost_estimate=cost,
        name="packed_grads",
    )(core, *lefts, *[right for left, right in items])
    return results[0::2], results[1::2]


def after(value, *others):
    return lax.optimization_barrier((value,) + others)[0]


class Small:
    def __init__(self, values):
        self.sent, self.got, self.kept = [values], [], values
        self.stages = [("batch", bit) for bit in range(bits_of("batch"))] + [("seq", -1)]

    def launch(self, sent):
        name, bit = self.stages.pop(0)
        if bit >= 0:
            self.got = [swap(sent[0], name, bit)]
            return
        size = lax.axis_size(name)
        self.got = [
            lax.ppermute(sent[0], name, [(i, i ^ step) for i in range(size)])
            for step in range(1, size)
        ]

    def advance(self, got):
        terms = [self.kept] + got
        while len(terms) > 1:
            terms = [terms[i] + terms[i + 1] for i in range(0, len(terms), 2)]
        self.kept = terms[0]
        self.got = []
        self.sent = [self.kept] if self.stages else []

    def finish(self):
        while self.got:
            self.advance(self.got)
            if self.sent:
                self.launch(self.sent)
        return self.kept


class Flow:
    def __init__(self, items, split=True, seq_first=False):
        self.split, self.seq_first = split, seq_first
        self.shapes = [(left.shape[1], right.shape[1]) for left, right in items]
        self.high, self.low = bits_of("batch"), bits_of("seq")
        self.ranks = 1 << (self.high + self.low)
        self.plain = min(shape[0] for shape in self.shapes) % (8 * self.ranks) != 0
        self.got, self.stage = [], 0
        if self.plain:
            self.sent = []
            self.whole = [weight_grad(left, right) for left, right in items]
            return
        heights = []
        for shape in self.shapes:
            if shape[0] not in heights:
                heights.append(shape[0])
        self.order = [
            [i for i, shape in enumerate(self.shapes) if shape[0] == height] for height in heights
        ]
        if split:
            self.kept, self.sent = packed_grads(items)
        else:
            self.sent = [packed_grads(items, False)]
        ups = [("batch", bit) for bit in range(1, self.high)]
        alongs = [("seq", bit) for bit in range(self.low)]
        if seq_first:
            self.steps = [[step] for step in alongs + ups]
        else:
            self.steps = [list(pair) for pair in zip(ups, ups[::-1])] + [None]

    def launch(self, sent):
        if self.plain:
            return
        if not self.split:
            axis_name = ("batch", "seq")[self.stage]
            self.got = [lax.psum_scatter(sent[0], axis_name, scatter_dimension=0, tiled=True)]
        elif self.stage == 0:
            self.got = [swap(x, "batch", 0) for x in sent]
        elif self.steps[self.stage - 1] is None:
            self.got = [
                lax.ppermute(x, "seq", [(i, i ^ step) for i in range(1 << self.low)])
                for step, x in enumerate(sent, 1)
            ]
        else:
            steps = self.steps[self.stage - 1]
            self.got = [swap(x, name, bit) for x, (name, bit) in zip(sent, steps)]
        self.stage += 1

    def advance(self, got):
        last = self.high - 1
        dim = last + self.low
        if not self.split:
            self.got, self.sent = [], got if self.stage == 1 else []
            self.result = got[0].astype(jnp.float32)
            return
        if self.stage > len(self.steps):
            self.result = add(self.kept[0], got[0])
            for more in got[1:]:
                self.result = self.result + more.astype(jnp.float32)
            self.got, self.sent = [], []
            return
        sums = [add_low(k, g) for k, g in zip(self.kept, got)]
        if self.stage == 1:
            sums = [x.reshape((2,) * dim + x.shape[1:]) for x in sums]
        steps = self.steps[self.stage - 1]
        if steps is None:
            whole = jnp.concatenate(sums, axis=dim)
            whole = whole.reshape((1 << self.low,) + whole.shape[dim:])
            place = lax.axis_index("seq")
            picks = [
                lax.dynamic_slice_in_dim(whole, place ^ step, 1, 0) for step in range(1 << self.low)
            ]
            self.kept, self.sent = picks[:1], picks[1:]
            return
        if len(sums) > len(steps):
            sums = [jnp.concatenate(sums, axis=dim)]
        elif len(sums) < len(steps):
            size = sums[0].shape[dim]
            sums = [
                lax.slice_in_dim(sums[0], 0, size // 2, axis=dim),
                lax.slice_in_dim(sums[0], size // 2, size, axis=dim),
            ]
        halves = [
            halve(x, name, bit, (last if name == "batch" else dim - 1) - bit)
            for x, (name, bit) in zip(sums, steps)
        ]
        self.kept = [h[0] for h in halves]
        self.sent = [h[1] for h in halves]

    def finish(self):
        if not self.plain and not self.split:
            while self.got:
                self.advance(self.got)
                if self.sent:
                    self.launch(self.sent)
        if self.plain:
            results = []
            for grad in self.whole:
                grad = lax.psum_scatter(
                    grad.astype(jnp.bfloat16), ("batch", "seq"), scatter_dimension=0, tiled=True
                )
                results.append(grad.astype(jnp.float32))
            return results
        while self.got:
            self.advance(self.got)
            if self.sent:
                self.launch(self.sent)
        part = self.result.reshape(-1, 16, LANES)
        results, start = [None] * len(self.shapes), 0
        for indices in self.order:
            for i in indices:
                height, width = self.shapes[i]
                tiles = height // self.ranks // 8
                count = tiles * width // 256
                piece = part[start : start + count]
                start += count
                piece = piece.reshape(width // 256, tiles, 2, 8, LANES)
                piece = jnp.transpose(piece, (1, 3, 0, 2, 4))
                results[i] = piece.reshape(tiles * 8, width)
        return results


def tick(value, *flows, fresh=()):
    live = [flow for flow in flows if flow is not None and flow.got]
    gots = [flow.got for flow in live]
    sents = [list(flow.sent) for flow in fresh]
    value, gots, sents = lax.optimization_barrier((value, gots, sents))
    for flow, sent in zip(fresh, sents):
        flow.launch(sent)
    for flow, got in zip(live, gots):
        flow.advance(got)
    value, sents = lax.optimization_barrier((value, [list(flow.sent) for flow in live]))
    for flow, sent in zip(live, sents):
        if sent:
            flow.launch(sent)
    return value


def body(
    enc_in,
    dec_in,
    out_grad,
    enc_segs,
    dec_segs,
    enc_qkv,
    enc_proj,
    enc_wi,
    enc_wo,
    enc_rel,
    enc_gains,
    dec_qkv,
    dec_proj,
    dec_rel,
    cross_q,
    cross_kv,
    cross_proj,
    dec_wi,
    dec_wo,
    dec_gains,
):
    shares = lax.axis_size("seq")
    rows = enc_in.shape[0] // shares
    full_len = enc_segs.shape[1]
    target_len = dec_in.shape[1]
    width = enc_in.shape[2]
    low = jnp.bfloat16
    row_segs = lax.dynamic_slice_in_dim(enc_segs, lax.axis_index("seq") * rows, rows, 0)

    local_len = enc_in.shape[1]
    enc_row = turn_rows(enc_in.reshape(shares, rows, local_len, width))
    enc_values = jnp.swapaxes(enc_row, 0, 1).reshape(-1, width).astype(jnp.float32)
    dec_values = dec_in.reshape(-1, width).astype(jnp.float32)

    offsets = line_offsets(full_len, full_len)
    turned = turned_offsets(full_len, full_len)
    enc_select = enc_selector(offsets)
    enc_line = bias_line(enc_rel, enc_select)
    enc_turned = bias_line(enc_rel, enc_selector(turned))
    offsets = line_offsets(target_len, target_len)
    turned = turned_offsets(target_len, target_len)
    dec_select = dec_selector(offsets)
    dec_line = bias_line(dec_rel, dec_select)
    dec_line = jnp.where(jnp.asarray(offsets > 0), -BIG, dec_line)
    dec_turned = bias_line(dec_rel, dec_selector(turned))
    dec_turned = jnp.where(jnp.asarray(turned > 0), -BIG, dec_turned)
    enc_query_marks, enc_key_marks = marks(row_segs, row_segs)
    dec_query_marks, dec_key_marks = marks(dec_segs, dec_segs)

    dec_normed_one, dec_inverse_one = norm_fwd(dec_values, dec_gains[0])
    dec_normed_one = dec_normed_one.astype(low)
    dec_packed = row_dot(dec_normed_one, dec_qkv).astype(low)
    self_mixed, self_marks = attend_rows(
        rows, dec_packed, 0, dec_packed, 6, 12, dec_query_marks, dec_key_marks, dec_turned
    )
    dec_first = dec_values + row_dot(self_mixed, dec_proj)
    dec_normed_two, dec_inverse_two = norm_fwd(dec_first, dec_gains[1])
    dec_normed_two = dec_normed_two.astype(low)
    cross_query = row_dot(dec_normed_two, cross_q).astype(low)

    normed_one, inverse_one = norm_fwd(enc_values, enc_gains[0])
    normed_one = normed_one.astype(low)
    packed = row_dot(normed_one, enc_qkv).astype(low)
    enc_mixed, enc_marks = attend_rows(
        rows, packed, 0, packed, 6, 12, enc_query_marks, enc_key_marks, enc_turned
    )
    after_attn = enc_values + row_dot(enc_mixed, enc_proj)
    normed_two, inverse_two = norm_fwd(after_attn, enc_gains[1])
    normed_two = normed_two.astype(low)
    enc_hidden, enc_slope = gelu_pair(row_dot(normed_two, enc_wi))
    second = after_attn + row_dot(enc_hidden, enc_wo)
    encoded, inverse_three = norm_fwd(second, enc_gains[2])
    encoded = encoded.astype(low)
    cross_pack = row_dot(encoded, cross_kv).astype(low)

    cross_mixed, cross_marks = attend_rows(
        rows, cross_query, 0, cross_pack, 0, 6, dec_query_marks, enc_key_marks, None
    )
    dec_second = dec_first + row_dot(cross_mixed, cross_proj)
    dec_normed_three, dec_inverse_three = norm_fwd(dec_second, dec_gains[2])
    dec_normed_three = dec_normed_three.astype(low)
    dec_hidden, dec_slope = gelu_pair(row_dot(dec_normed_three, dec_wi))
    dec_result = (dec_second + row_dot(dec_hidden, dec_wo)).astype(low)

    upstream = out_grad.reshape(-1, width)
    grad_pre = (back_dot(upstream, dec_wo) * dec_slope.astype(jnp.float32)).astype(low)
    flow_one = Flow(((dec_hidden, upstream), (dec_normed_three, grad_pre)), False)
    grad_pre, dec_result = tick((grad_pre, dec_result), fresh=(flow_one,))
    grad_input, gain_dec_three = norm_back(
        dec_second, dec_inverse_three, dec_gains[2], back_dot(grad_pre, dec_wi)
    )
    grad_second = upstream.astype(jnp.float32) + grad_input
    grad_cross_branch = grad_second.astype(low)
    grad_mixed = back_dot(grad_cross_branch, cross_proj).astype(low)
    grad_cq, grad_ck, grad_cv, unused = attend_rows_back(
        rows, cross_query, 0, cross_pack, 0, 6, grad_mixed, cross_marks, enc_key_marks, None
    )
    grad_input, gain_dec_two = norm_back(
        dec_first, dec_inverse_two, dec_gains[1], back_dot(grad_cq, cross_q)
    )
    grad_first = grad_second + grad_input
    grad_self_branch = grad_first.astype(low)
    grad_mixed = back_dot(grad_self_branch, dec_proj).astype(low)
    grad_sq, grad_sk, grad_sv, dec_line_grad = attend_rows_back(
        rows, dec_packed, 0, dec_packed, 6, 12, grad_mixed, self_marks, dec_key_marks, dec_line
    )
    flow_two = Flow(
        (
            (dec_normed_one, grad_sq),
            (dec_normed_one, grad_sk),
            (dec_normed_one, grad_sv),
            (self_mixed, grad_self_branch),
            (dec_normed_two, grad_cq),
            (cross_mixed, grad_cross_branch),
            (encoded, grad_ck),
            (encoded, grad_cv),
        ),
        False,
    )
    (grad_sq, grad_ck, dec_line_grad, gain_dec_three, gain_dec_two) = tick(
        (grad_sq, grad_ck, dec_line_grad, gain_dec_three, gain_dec_two), fresh=(flow_two,)
    )
    rel_grad_dec = rel_grad(dec_line_grad, dec_select)

    grad_enc_second, gain_enc_three = norm_back(
        second,
        inverse_three,
        enc_gains[2],
        back_dot(grad_ck, cross_kv[:, :width]) + back_dot(grad_cv, cross_kv[:, width:]),
    )
    grad_branch = grad_enc_second.astype(low)
    grad_branch, rel_grad_dec, gain_enc_three = tick((grad_branch, rel_grad_dec, gain_enc_three))
    flow_three = Flow(((enc_hidden, grad_branch),), seq_first=True)
    grad_branch = tick(grad_branch, fresh=(flow_three,))
    grad_pre = slope_back(grad_branch, enc_wo, enc_slope)
    grad_pre = tick(grad_pre, flow_one, flow_three)
    grad_input, gain_enc_two = norm_back(
        after_attn, inverse_two, enc_gains[1], back_dot(grad_pre, enc_wi)
    )
    grad_enc_first = grad_enc_second + grad_input
    grad_branch = grad_enc_first.astype(low)
    flow_four = Flow(((normed_two, grad_pre), (enc_mixed, grad_branch)))
    grad_branch, gain_enc_two = tick((grad_branch, gain_enc_two), fresh=(flow_four,))
    grad_mixed = back_dot(grad_branch, enc_proj).astype(low)
    grad_mixed = tick(grad_mixed, flow_four)
    pieces, line_grads, through = [], [], None
    flows = {0: (flow_three, flow_four), 2: (flow_two, flow_four), 4: ()}
    for part in ((0, 2), (2, 2), (4, 2)):
        grad_eq, grad_ek, grad_ev, line_grad = attend_rows_back(
            rows,
            packed,
            0,
            packed,
            6,
            12,
            grad_mixed,
            enc_marks,
            enc_key_marks,
            enc_line,
            part,
        )
        grad_eq, grad_ek, grad_ev, line_grad, grad_mixed = tick(
            (grad_eq, grad_ek, grad_ev, line_grad, grad_mixed), *flows[part[0]]
        )
        line_grads.append(line_grad)
        pieces.append((grad_eq, grad_ek, grad_ev))
        if part[0] == 4:
            flow_five = Flow([(normed_one, piece[at]) for at in range(3) for piece in pieces])
            pieces = tick(pieces, fresh=(flow_five,))
            grad_eq, grad_ek, grad_ev = pieces[-1]
        for at, piece in enumerate((grad_eq, grad_ek, grad_ev)):
            start = at * width + part[0] * LANES
            term = back_dot(piece, enc_qkv[:, start : start + part[1] * LANES])
            through = term if through is None else through + term
        grad_mixed = after(grad_mixed, through)
    through = tick(through, flow_five)
    grad_input, gain_enc_one = norm_back(enc_values, inverse_one, enc_gains[0], through)
    enc_grad_row = (grad_enc_first + grad_input).astype(low)
    enc_grad_turned = enc_grad_row.reshape(rows, shares, local_len, width)
    enc_grad = turn_rows(jnp.swapaxes(enc_grad_turned, 0, 1)).reshape(enc_in.shape)

    grad_sq = after(grad_sq, enc_grad_row)
    grad_sq = tick(grad_sq, flow_three, flow_four, flow_five)
    grad_input, gain_dec_one = norm_back(
        dec_values,
        dec_inverse_one,
        dec_gains[0],
        back_dot(grad_sq, dec_qkv[:, :width])
        + back_dot(grad_sk, dec_qkv[:, width : 2 * width])
        + back_dot(grad_sv, dec_qkv[:, 2 * width :]),
    )
    dec_in_grad = grad_first + grad_input
    enc_line_grad = jnp.concatenate(line_grads, axis=0)
    rels = jnp.concatenate((rel_grad(enc_line_grad, enc_select), rel_grad_dec), axis=0)
    gains = (
        (gain_enc_one, gain_enc_two, gain_enc_three) + (gain_dec_one, gain_dec_two, gain_dec_three)
    )
    small = Small(jnp.concatenate((jnp.stack(gains), rels.reshape(1, -1)), axis=0))
    dec_in_grad, dec_result = tick((dec_in_grad, dec_result), flow_five, fresh=(small,))
    dec_result = tick(dec_result, flow_three, small)
    dec_result = tick(dec_result, flow_three, small)
    dec_result = tick(dec_result, flow_one, flow_two, small)
    dec_result, enc_grad = lax.optimization_barrier((dec_result, enc_grad))
    for unused in range(3):
        dec_result = tick(dec_result, flow_three, flow_four, flow_five, small)
    small = small.finish()
    gains_enc_total, gains_dec_total = small[:3], small[3:6]
    rels = small[6].reshape(2, NB, H)
    rel_enc_total, rel_dec_total = rels[0], rels[1]
    grad_dec_wo, grad_dec_wi = flow_one.finish()
    two = flow_two.finish()
    dec_q, dec_k, dec_v, grad_dec_proj, grad_cross_q, grad_cross_proj, cross_k, cross_v = two
    (grad_enc_wo,) = flow_three.finish()
    grad_enc_wi, grad_enc_proj = flow_four.finish()
    grad_enc_qkv = jnp.concatenate(flow_five.finish(), axis=1)
    return (
        dec_result.reshape(dec_in.shape),
        enc_grad.astype(jnp.float32),
        dec_in_grad.reshape(dec_in.shape),
        grad_enc_qkv,
        grad_enc_proj,
        grad_enc_wi,
        grad_enc_wo,
        rel_enc_total,
        gains_enc_total,
        jnp.concatenate((dec_q, dec_k, dec_v), axis=1),
        grad_dec_proj,
        rel_dec_total,
        grad_cross_q,
        jnp.concatenate((cross_k, cross_v), axis=1),
        grad_cross_proj,
        grad_dec_wi,
        grad_dec_wo,
        gains_dec_total,
    )


def solution(mesh):
    in_specs = (
        P("batch", "seq", None),
        P(("batch", "seq"), None, None),
        P(("batch", "seq"), None, None),
        P("batch", None),
        P(("batch", "seq"), None),
        P(),
        P(),
        P(),
        P(),
        P(),
        P(),
        P(),
        P(),
        P(),
        P(),
        P(),
        P(),
        P(),
        P(),
        P(),
    )
    out_specs = (
        P(("batch", "seq"), None, None),
        P("batch", "seq", None),
        P(("batch", "seq"), None, None),
        P(("batch", "seq"), None),
        P(("batch", "seq"), None),
        P(("batch", "seq"), None),
        P(("batch", "seq"), None),
        P(),
        P(),
        P(("batch", "seq"), None),
        P(("batch", "seq"), None),
        P(),
        P(("batch", "seq"), None),
        P(("batch", "seq"), None),
        P(("batch", "seq"), None),
        P(("batch", "seq"), None),
        P(("batch", "seq"), None),
        P(),
    )
    return jax.shard_map(body, mesh=mesh, in_specs=in_specs, out_specs=out_specs, check_vma=False)
```
